32 devices in a mesh: rows: 8 (over z, y), img: 4 (over x, core).
Axes of the slice: x: 2, y: 2, z: 4, core: 2. Of those that a mesh axis runs over, the one named last changes fastest.
Arguments:
- images_in: bfloat16 [16, 32, 44, 2048], P('img', 'rows'), may hold values from -6 to 6
- out_grad: bfloat16 [16, 32, 44, 2048], P('img', 'rows'), may hold values from -6 to 6
- box_rows: int32 [16, 100, 2], P('img'), may hold values from 0 to 31
- box_cols: int32 [16, 100, 2], P('img'), may hold values from 0 to 43
- box_count: int32 [16], P('img'), may hold values from 1 to 100, as said below
- valid_mask: int32 [16, 32, 44], P('img', 'rows'), may hold values 0 or 1
- reduce_one: bfloat16 [2048, 512], P(('rows', 'img')), may hold values from -0.125 to 0.125
- offset_one: bfloat16 [18432, 18], P(('rows', 'img')), may hold values from -0.107910156 to 0.107910156
- deform_one: bfloat16 [4608, 512], P(('rows', 'img')), may hold values from -0.09375 to 0.09375
- expand_one: bfloat16 [512, 2048], P(('rows', 'img')), may hold values from -0.25 to 0.25
- mid_gain_one: bfloat16 [2, 512], P(None, ('rows', 'img')), may hold values from 0.5 to 1.5
- mid_bias_one: bfloat16 [2, 512], P(None, ('rows', 'img')), may hold values from -3 to 3
- wide_gain_one: bfloat16 [2048], P(('rows', 'img')), may hold values from 0.5 to 1.5
- wide_bias_one: bfloat16 [2048], P(('rows', 'img')), may hold values from -3 to 3
- reduce_two: bfloat16 [2048, 512], P(('rows', 'img')), may hold values from -0.125 to 0.125
- spatial_two: bfloat16 [4608, 512], P(('rows', 'img')), may hold values from -0.09375 to 0.09375
- expand_two: bfloat16 [512, 2048], P(('rows', 'img')), may hold values from -0.25 to 0.25
- mid_gain_two: bfloat16 [2, 512], P(None, ('rows', 'img')), may hold values from 0.5 to 1.5
- mid_bias_two: bfloat16 [2, 512], P(None, ('rows', 'img')), may hold values from -3 to 3
- wide_gain_two: bfloat16 [2048], P(('rows', 'img')), may hold values from 0.5 to 1.5
- wide_bias_two: bfloat16 [2048], P(('rows', 'img')), may hold values from -3 to 3
Outputs:
- block_out: bfloat16 [16, 32, 44, 2048], P('img', 'rows')
- grad_images: float32 [16, 32, 44, 2048], P('img', 'rows')
- grad_reduce_one: float32 [2048, 512], P(('rows', 'img'))
- grad_offset_one: float32 [18432, 18], P(('rows', 'img'))
- grad_deform_one: float32 [4608, 512], P(('rows', 'img'))
- grad_expand_one: float32 [512, 2048], P(('rows', 'img'))
- grad_mid_gain_one: float32 [2, 512], P(None, ('rows', 'img'))
- grad_mid_bias_one: float32 [2, 512], P(None, ('rows', 'img'))
- grad_wide_gain_one: float32 [2048], P(('rows', 'img'))
- grad_wide_bias_one: float32 [2048], P(('rows', 'img'))
- grad_reduce_two: float32 [2048, 512], P(('rows', 'img'))
- grad_spatial_two: float32 [4608, 512], P(('rows', 'img'))
- grad_expand_two: float32 [512, 2048], P(('rows', 'img'))
- grad_mid_gain_two: float32 [2, 512], P(None, ('rows', 'img'))
- grad_mid_bias_two: float32 [2, 512], P(None, ('rows', 'img'))
- grad_wide_gain_two: float32 [2048], P(('rows', 'img'))
- grad_wide_bias_two: float32 [2048], P(('rows', 'img'))
The draws below stay inside these ranges and needn't reach their ends.
Inputs may be any that keep to these rules, and one draw needn't show every extreme that they name: Image i uses its first box_count[i] box slots, and some image uses all 100.
All inputs are finite; a program needn't handle non-finite values. No bound on the sum of `valid_mask` on one device may be relied on, other than what follows from the above.
Results may differ from the reference program's by a relative error of at most 0.025.
Values may be sent and summed in bfloat16 or wider, within the bound.
No kernel may reach another device: no remote copies, remote signals or barrier semaphores. Data moves between devices by JAX's collectives and lax.ppermute only.
A program may use at most 320 MiB of HBM per device.

```python
import jax
import jax.numpy as jnp
from jax import lax

C = 2048
M = 512
CLIP = 8
HALO = 10
W = 44
NBOX = 100
MB = 2
IMG_MB = 2
H = 32
IMAGES = 16
N_IMG = 4


def draw_box_count(key, part):
    first_key = jax.random.fold_in(key, 11)
    second_key = jax.random.fold_in(key, 23)
    counts = jax.random.randint(first_key, (IMAGES,), 1, NBOX + 1)
    chosen = jax.random.randint(second_key, (), 0, IMAGES)
    return jnp.where(jnp.arange(IMAGES) == chosen, NBOX, counts).astype(jnp.int32)


def plant(array, key, low, top_value):
    place = [jax.random.randint(jax.random.fold_in(key, axis), (), 0, length) for axis, length in enumerate(array.shape)]
    main_axis = array.shape.index(max(array.shape))
    next_to = place[:main_axis] + [(place[main_axis] + 1) % array.shape[main_axis]] + place[main_axis + 1:]
    return array.at[tuple(place)].set(low).at[tuple(next_to)].set(top_value)


def raised(result, own_key, source, target, shards_of, factor):
    owner, partner = [(jnp.arange(result.shape[position]) // (result.shape[position] // shards_of)).reshape([-1 if axis == position else 1 for axis in range(result.ndim)]) for position in (source, target)]
    chosen = jax.random.permutation(own_key, shards_of)[partner]
    strong = (owner == chosen) | (owner == (partner + shards_of // 2) % shards_of)
    return jnp.where(strong, factor * result, result)


def shard_levels(stream_key, extent, cuts, smallest, high):
    gain = 1.0
    for position, parts in cuts:
        steps = jax.random.uniform(jax.random.fold_in(jax.random.fold_in(stream_key, 6), position), (parts,), jnp.float32, smallest / len(cuts), high / len(cuts))
        gain = gain * jnp.repeat(jnp.exp(steps), extent[position] // parts).reshape((-1,) + (1,) * (len(extent) - 1 - position))
    return gain


def noise(own_key, dims, scale, most, shards=(), held_as=jnp.bfloat16):
    values = jax.random.normal(own_key, dims, jnp.float32) * scale
    if len(shards) > 0:
        values = shard_levels(own_key, dims, shards, -0.22, 0.18) * values
    return jnp.clip(values, min=-most, max=most).astype(held_as)


def heavy_noise(key, dims, deviation, most, pieces, heavy, dtype=jnp.bfloat16):
    result = deviation * jax.random.normal(key, dims, jnp.float32)
    if pieces:
        result = result * shard_levels(key, dims, pieces, -0.22, 0.18)
    return jnp.clip(raised(result, jax.random.fold_in(key, 3), *heavy), -most, most).astype(dtype)


def setup_inputs(seed: int = 0) -> dict:
    arg_keys = jax.random.split(jax.random.key(seed), 22)
    images_in = heavy_noise(arg_keys[0], (IMAGES, H, W, C), 1.0, 6.0, ((0, 4), (1, 8)), (1, 3, 8, 2.0))
    out_grad = noise(arg_keys[1], (IMAGES, H, W, C), 1.0, 6.0, ((0, 4), (1, 8)))
    box_rows = plant(jax.random.randint(arg_keys[2], (IMAGES, NBOX, 2), 0, H), jax.random.fold_in(arg_keys[2], 1), 0, H - 1).astype(jnp.int32)
    box_cols = plant(jax.random.randint(arg_keys[3], (IMAGES, NBOX, 2), 0, W), jax.random.fold_in(arg_keys[3], 1), 0, W - 1).astype(jnp.int32)
    box_count = draw_box_count(jax.random.fold_in(arg_keys[21], 71), 0)
    valid_mask = plant((jax.random.randint(arg_keys[5], (IMAGES, H, W), 0, 8) < 7).astype(jnp.int32), jax.random.fold_in(arg_keys[5], 1), 0, 1)
    reduce_one = noise(arg_keys[6], (C, M), C ** -0.5, 0.125, ((0, 32),))
    offset_one = noise(arg_keys[7], (9 * C, 18), 0.018, 0.107910156, ((0, 32),))
    deform_one = noise(arg_keys[8], (9 * M, M), (9 * M) ** -0.5, 0.09375, ((0, 32),))
    expand_one = noise(arg_keys[9], (M, C), M ** -0.5, 0.25, ((0, 32),))
    mid_gain_one = jnp.clip(1.0 + 0.1 * jax.random.normal(arg_keys[10], (2, M), jnp.float32), 0.5, 1.5).astype(jnp.bfloat16)
    mid_bias_one = noise(arg_keys[11], (2, M), 0.5, 3.0, ((1, 32),))
    wide_gain_one = jnp.clip(1.0 + 0.1 * jax.random.normal(arg_keys[12], (C,), jnp.float32), 0.5, 1.5).astype(jnp.bfloat16)
    wide_bias_one = noise(arg_keys[13], (C,), 0.5, 3.0, ((0, 32),))
    reduce_two = noise(arg_keys[14], (C, M), C ** -0.5, 0.125, ((0, 32),))
    spatial_two = noise(arg_keys[15], (9 * M, M), (9 * M) ** -0.5, 0.09375, ((0, 32),))
    expand_two = noise(arg_keys[16], (M, C), M ** -0.5, 0.25, ((0, 32),))
    mid_gain_two = jnp.clip(1.0 + 0.1 * jax.random.normal(arg_keys[17], (2, M), jnp.float32), 0.5, 1.5).astype(jnp.bfloat16)
    mid_bias_two = noise(arg_keys[18], (2, M), 0.5, 3.0, ((1, 32),))
    wide_gain_two = jnp.clip(1.0 + 0.1 * jax.random.normal(arg_keys[19], (C,), jnp.float32), 0.5, 1.5).astype(jnp.bfloat16)
    wide_bias_two = noise(arg_keys[20], (C,), 0.5, 3.0, ((0, 32),))
    return dict(images_in=images_in, out_grad=out_grad, box_rows=box_rows, box_cols=box_cols, box_count=box_count, valid_mask=valid_mask, reduce_one=reduce_one, offset_one=offset_one, deform_one=deform_one, expand_one=expand_one, mid_gain_one=mid_gain_one, mid_bias_one=mid_bias_one, wide_gain_one=wide_gain_one, wide_bias_one=wide_bias_one, reduce_two=reduce_two, spatial_two=spatial_two, expand_two=expand_two, mid_gain_two=mid_gain_two, mid_bias_two=mid_bias_two, wide_gain_two=wide_gain_two, wide_bias_two=wide_bias_two)


epsilon = 1e-05
exact = lax.Precision.HIGHEST

@jax.custom_vjp
def low(v):
    return lax.optimization_barrier(v.astype(jnp.bfloat16)).astype(jnp.float32)

@jax.custom_vjp
def low_back(v):
    return v

def low_keep(v):
    return (low(v), None)

def low_pass(kept, grad):
    return (grad,)

def back_keep(v):
    return (v, None)

def back_low(kept, grad):
    return (low(grad),)
low.defvjp(low_keep, low_pass)
low_back.defvjp(back_keep, back_low)

def product(left_side, right_side):
    return jnp.dot(left_side, right_side, precision=exact, preferred_element_type=jnp.float32)

def batch_norm(values, gain_term, bias_term):
    center = lax.optimization_barrier(jnp.mean(values, axis=0))
    spread = lax.rsqrt(lax.optimization_barrier(jnp.mean(values * values, axis=0)) - center * center + epsilon)
    return (values - center) * spread * gain_term + bias_term

def spatial_conv(source, weight, spacing):
    images, heights, columns, channels = source.shape
    padded = jnp.pad(source, ((0, 0), (spacing, spacing), (spacing, spacing), (0, 0)))
    running = jnp.zeros((images * heights * columns, weight.shape[1]), jnp.float32)
    for tap_index in range(9):
        row_start = tap_index // 3 * spacing
        col_start = tap_index % 3 * spacing
        portion = padded[:, row_start:row_start + heights, col_start:col_start + columns, :].reshape(-1, channels)
        running = running + product(portion, weight[tap_index * channels:(tap_index + 1) * channels])
    return running

def spline(values):
    magnitude = jnp.abs(values)
    outer = 1.5 - magnitude
    return jnp.where(magnitude < 0.5, 0.75 - values * values, jnp.where(magnitude < 1.5, 0.5 * outer * outer, 0.0))

def tent_weights(clipped, rel_rows):
    tap_ids = jnp.arange(9)
    base_rows = (tap_ids // 3 - 1).astype(jnp.float32)
    base_cols = (tap_ids % 3 - 1).astype(jnp.float32)
    shift_rows = clipped[..., :9] + base_rows
    shift_cols = clipped[..., 9:] + base_cols
    span_cols = clipped.shape[-2]
    rel_cols = (jnp.arange(span_cols)[None, :] - jnp.arange(span_cols)[:, None]).astype(jnp.float32)
    weight_rows = spline(shift_rows[..., None] - rel_rows[:, None, None, :])
    weight_cols = spline(shift_cols[..., None] - rel_cols[:, None, :])
    return weight_rows[..., :, None] * weight_cols[..., None, :]

def sample_image(operands):
    source, clipped = operands
    heights = source.shape[0]
    padded = jnp.pad(source, ((HALO, HALO), (0, 0), (0, 0)))
    stacked = jnp.stack([padded[row_offset:row_offset + heights] for row_offset in range(2 * HALO + 1)], axis=1)
    rel_line = (jnp.arange(2 * HALO + 1) - HALO).astype(jnp.float32)
    rel_rows = jnp.broadcast_to(rel_line[None, :], (heights, 2 * HALO + 1))
    sampler = low(tent_weights(clipped, rel_rows))
    return low(jnp.einsum('hwkjq,hjqm->hwkm', sampler, stacked, precision=exact))

def block_one(inputs, parameters):
    reduce_weight, offset_weight, deform_weight, expand_weight, mid_gain, mid_bias, wide_gain, wide_bias = parameters
    images, heights, columns, channels = inputs.shape
    flat_inputs = inputs.reshape(-1, channels)
    first_conv = low_back(product(flat_inputs, reduce_weight))
    hidden = low(jax.nn.silu(batch_norm(first_conv, mid_gain[0], mid_bias[0])))
    hidden_maps = hidden.reshape(images, heights, columns, -1)
    offsets = low_back(spatial_conv(inputs, offset_weight, 2))
    clipped = (CLIP * jnp.tanh(offsets / CLIP)).reshape(images, heights, columns, 18)
    sampled = low_back(lax.map(jax.checkpoint(sample_image), (hidden_maps, clipped)))
    second_conv = low_back(product(sampled.reshape(images * heights * columns, -1), deform_weight))
    hidden_two = low(jax.nn.silu(batch_norm(second_conv, mid_gain[1], mid_bias[1])))
    third_conv = low_back(product(hidden_two, expand_weight))
    joined = jax.nn.silu(batch_norm(third_conv, wide_gain, wide_bias) + flat_inputs)
    return low(joined).reshape(inputs.shape)

def block_two(inputs, parameters):
    reduce_weight, spatial_weight, expand_weight, mid_gain, mid_bias, wide_gain, wide_bias = parameters
    images, heights, columns, channels = inputs.shape
    flat_inputs = inputs.reshape(-1, channels)
    first_conv = low_back(product(flat_inputs, reduce_weight))
    inner_one = low(jax.nn.silu(batch_norm(first_conv, mid_gain[0], mid_bias[0])))
    second_conv = low_back(spatial_conv(inner_one.reshape(images, heights, columns, -1), spatial_weight, 1))
    inner_two = low(jax.nn.silu(batch_norm(second_conv, mid_gain[1], mid_bias[1])))
    third_conv = low_back(product(inner_two, expand_weight))
    return jax.nn.silu(batch_norm(third_conv, wide_gain, wide_bias) + flat_inputs).reshape(inputs.shape)

def forward(images_float, params_one, params_two):
    grouped = images_float.reshape(N_IMG, MB, IMG_MB, H, W, C)
    results = []
    for section_index in range(MB):
        section_maps = grouped[:, section_index].reshape(N_IMG * IMG_MB, H, W, C)
        middle = block_one(section_maps, params_one)
        results.append(block_two(middle, params_two).reshape(N_IMG, IMG_MB, H, W, C))
    return jnp.stack(results, axis=1).reshape(IMAGES, H, W, C)

def box_weights(box_rows, box_cols, box_count, valid_mask):
    row_ids = jnp.arange(H).astype(jnp.int32)
    col_ids = jnp.arange(W).astype(jnp.int32)
    row_low = jnp.minimum(box_rows[..., 0], box_rows[..., 1])
    row_high = jnp.maximum(box_rows[..., 0], box_rows[..., 1])
    col_low = jnp.minimum(box_cols[..., 0], box_cols[..., 1])
    col_high = jnp.maximum(box_cols[..., 0], box_cols[..., 1])
    inside_rows = ((row_ids >= row_low[..., None]) & (row_ids <= row_high[..., None])).astype(jnp.float32)
    inside_cols = ((col_ids >= col_low[..., None]) & (col_ids <= col_high[..., None])).astype(jnp.float32)
    live_boxes = (jnp.arange(box_rows.shape[1]).astype(jnp.int32)[None, :] < box_count[:, None]).astype(jnp.float32)
    covered = jnp.einsum('ib,ibh,ibw->ihw', live_boxes, inside_rows, inside_cols, precision=exact)
    return valid_mask.astype(jnp.float32) * (0.5 + covered / box_count.astype(jnp.float32)[:, None, None])

def reference(images_in, out_grad, box_rows, box_cols, box_count, valid_mask, reduce_one, offset_one, deform_one, expand_one, mid_gain_one, mid_bias_one, wide_gain_one, wide_bias_one, reduce_two, spatial_two, expand_two, mid_gain_two, mid_bias_two, wide_gain_two, wide_bias_two):
    params_one = tuple((entry.astype(jnp.float32) for entry in (reduce_one, offset_one, deform_one, expand_one, mid_gain_one, mid_bias_one, wide_gain_one, wide_bias_one)))
    params_two = tuple((entry.astype(jnp.float32) for entry in (reduce_two, spatial_two, expand_two, mid_gain_two, mid_bias_two, wide_gain_two, wide_bias_two)))
    primal, pullback = jax.vjp(forward, images_in.astype(jnp.float32), params_one, params_two)
    grad_weight = box_weights(box_rows, box_cols, box_count, valid_mask)
    cotangent = out_grad.astype(jnp.float32) * grad_weight[..., None]
    grad_images, grads_one, grads_two = pullback(cotangent)
    return (primal.astype(jnp.bfloat16), grad_images, grads_one[0], grads_one[1], grads_one[2], grads_one[3], grads_one[4], grads_one[5], grads_one[6], grads_one[7], grads_two[0], grads_two[1], grads_two[2], grads_two[3], grads_two[4], grads_two[5], grads_two[6])
```

```python
from functools import partial

import jax
import jax.numpy as jnp
from jax import lax
from jax.experimental import pallas as pl
from jax.experimental.pallas import tpu as pltpu
from jax.sharding import PartitionSpec as P

CLIP = 8
HALO = 10
MB = 2
BOTH = ("rows", "img")
MIB = 2**20

epsilon = 1e-05
exact = lax.Precision.HIGHEST
f32 = jnp.float32
bf16 = jnp.bfloat16

STRIP_ROWS = 4
COLS = 44
STRIP = STRIP_ROWS * COLS
QUERIES = 9 * STRIP
LANES = 1664
CELLS = (STRIP_ROWS + 2 * HALO) * COLS
ROW_ORDER = (10, 11, 12, 13, 14, 15, 16, 17, 6, 7, 8, 9, 18, 19, 20, 21, 2, 3, 4, 5, 22, 23, 0, 1)


def dot(left, right):
    return jnp.dot(left, right, preferred_element_type=f32)


def dot_nt(left, right):
    return lax.dot_general(left, right, (((1,), (1,)), ((), ())), preferred_element_type=f32)


def dot_tn(left, right):
    return lax.dot_general(left, right, (((0,), (0,)), ((), ())), preferred_element_type=f32)


def device_count():
    return lax.axis_size(BOTH)


def exchange(value, mask):
    return lax.ppermute(value, BOTH, [(i, i ^ mask) for i in range(device_count())])


def all_sum(value):
    count = device_count()
    bit = 1
    while bit < count:
        masks = [bit, 2 * bit, 3 * bit] if 2 * bit < count else [bit]
        parts = [exchange(value, mask) for mask in masks]
        for part in parts:
            value = value + part
        bit *= 4
    return value


def scatter_sum(chunks, order):
    count = device_count()
    me = lax.axis_index(BOTH)
    bits = [1 << k for k in range(count.bit_length() - 1)][::-1]
    value = chunks.reshape((2,) * len(bits) + chunks.shape[1:])
    order = [b for b in order if b in bits] + [b for b in bits[::-1] if b not in order]
    left = list(bits)
    for position, bit in enumerate(order):
        axis = left.index(bit)
        mine = (me // bit) % 2
        keep = lax.dynamic_index_in_dim(value, mine, axis, keepdims=False)
        send = lax.dynamic_index_in_dim(value, 1 - mine, axis, keepdims=False)
        value = keep.astype(f32) + exchange(send, bit).astype(f32)
        if position < len(order) - 1:
            value = value.astype(bf16)
        left.pop(axis)
    return value


def from_behind(value, steps):
    count = lax.axis_size("rows")
    first, last = (max(0, -steps), min(count, count - steps))
    return lax.ppermute(value, "rows", [(source, source + steps) for source in range(first, last)])


def spline(values):
    magnitude = jnp.abs(values)
    outer = 1.5 - magnitude
    return jnp.where(
        magnitude < 0.5,
        0.75 - values * values,
        jnp.where(magnitude < 1.5, 0.5 * outer * outer, 0.0),
    )


def spline_slope(values):
    magnitude = jnp.abs(values)
    outer = 1.5 - magnitude
    return jnp.where(
        magnitude < 0.5,
        -2.0 * values,
        jnp.where(magnitude < 1.5, jnp.where(values > 0, -outer, outer), 0.0),
    )


def fill_factors(pos_ref, row_ref, col_weight, row_weight, col_slope=None, row_slope=None):
    cell_cols = lax.broadcasted_iota(jnp.int32, (2 * COLS, LANES), 0)
    cell_cols = jnp.where(cell_cols >= COLS, cell_cols - COLS, cell_cols).astype(f32)
    col_gap = pos_ref[0, 1:2, :] - cell_cols
    row_gap = pos_ref[0, 0:1, :] - row_ref[...]
    col_weight[...] = spline(col_gap)
    row_weight[...] = spline(row_gap)
    if col_slope is not None:
        col_slope[...] = spline_slope(col_gap)
        row_slope[...] = spline_slope(row_gap)


def fill_sampler(col_weight, row_weight, sampler):
    low = lax.broadcasted_iota(jnp.int32, (8, 128), 0) < 4

    def body(tile, carry):
        lanes = pl.ds(pl.multiple_of(tile * 128, 128), 128)
        for block in range(6):
            for chunk in range(11):
                halves = []
                for group in (2 * chunk, 2 * chunk + 1):
                    first, last = (8 * group) // COLS, (8 * group + 7) // COLS
                    weight = row_weight[4 * block + first : 4 * block + first + 1, lanes]
                    if first != last:
                        weight = jnp.where(
                            low, weight, row_weight[4 * block + last : 4 * block + last + 1, lanes]
                        )
                    local = group % 11
                    halves.append(col_weight[8 * local : 8 * local + 8, lanes] * weight)
                start = block * STRIP + 16 * chunk
                sampler[start : start + 16, lanes] = jnp.concatenate(halves, axis=0).astype(bf16)
        return carry

    lax.fori_loop(0, LANES // 128, body, 0)


def fill_window(pieces, window):
    for index, piece in enumerate(pieces[:5]):
        window[index * STRIP : (index + 1) * STRIP, :] = piece[0]
    window[5 * STRIP : 6 * STRIP, :] = jnp.concatenate([pieces[5][0], pieces[6][0]], axis=0)


def sample_kernel(pos_ref, row_ref, *refs):
    pieces, out_ref = refs[:7], refs[7]
    col_weight, row_weight, sampler, window = refs[8:]
    fill_factors(pos_ref, row_ref, col_weight, row_weight)
    fill_sampler(col_weight, row_weight, sampler)
    fill_window(pieces, window)
    result = dot_tn(window[...], sampler[...]).T.astype(bf16)
    width = window.shape[1]
    for tap in range(9):
        out_ref[0, :, tap * width : (tap + 1) * width] = result[tap * STRIP : (tap + 1) * STRIP]


def sample_back_kernel(pos_ref, row_ref, *refs):
    pieces, upstream_ref = refs[:7], refs[7]
    grads, pos_grad = refs[8:15], refs[15]
    (
        col_weight,
        row_weight,
        col_slope,
        row_slope,
        sampler,
        window,
        upstream,
        sampler_grad,
    ) = refs[16:]
    fill_factors(pos_ref, row_ref, col_weight, row_weight, col_slope, row_slope)
    fill_sampler(col_weight, row_weight, sampler)
    fill_window(pieces, window)
    width = window.shape[1]
    for tap in range(9):
        upstream[tap * STRIP : (tap + 1) * STRIP, :] = upstream_ref[
            0, :, tap * width : (tap + 1) * width
        ]
    upstream[QUERIES:LANES, :] = jnp.zeros((LANES - QUERIES, width), bf16)
    sampler_grad[...] = dot_nt(window[...], upstream[...])
    for index, grad in enumerate(grads[:5]):
        grad[0] = dot(sampler[index * STRIP : (index + 1) * STRIP, :], upstream[...]).astype(
            grad.dtype
        )
    last = dot(sampler[5 * STRIP :, :], upstream[...])
    grads[5][0] = last[: STRIP // 2].astype(bf16)
    grads[6][0] = last[STRIP // 2 :].astype(bf16)
    low = lax.broadcasted_iota(jnp.int32, (8, 128), 0) < 4

    def body(tile, carry):
        lanes = pl.ds(pl.multiple_of(tile * 128, 128), 128)
        zero = jnp.zeros((8, 128), f32)
        weights = [col_weight[8 * group : 8 * group + 8, lanes] for group in range(11)]
        middle_low = jnp.where(low, weights[5], 0.0)
        middle_high = jnp.where(low, 0.0, weights[5])
        row_total = zero
        col_totals = [zero] * 11
        for pair in range(12):
            first = row_weight[2 * pair : 2 * pair + 1, lanes]
            second = row_weight[2 * pair + 1 : 2 * pair + 2, lanes]
            mixed = jnp.where(low, first, second)
            first_sum = zero
            second_sum = zero
            for group in range(11):
                start = 88 * pair + 8 * group
                value = sampler_grad[start : start + 8, lanes]
                if group < 5:
                    first_sum = first_sum + value * weights[group]
                    col_totals[group] = col_totals[group] + value * first
                elif group > 5:
                    second_sum = second_sum + value * weights[group]
                    col_totals[group] = col_totals[group] + value * second
                else:
                    first_sum = first_sum + value * middle_low
                    second_sum = second_sum + value * middle_high
                    col_totals[group] = col_totals[group] + value * mixed
            row_total = (
                row_total
                + first_sum * row_slope[2 * pair : 2 * pair + 1, lanes]
                + second_sum * row_slope[2 * pair + 1 : 2 * pair + 2, lanes]
            )
        col_total = zero
        for group in range(11):
            col_total = col_total + col_totals[group] * col_slope[8 * group : 8 * group + 8, lanes]
        pos_grad[0, 0:1, lanes] = jnp.sum(row_total, axis=0, keepdims=True)
        pos_grad[0, 1:2, lanes] = jnp.sum(col_total, axis=0, keepdims=True)
        return carry

    lax.fori_loop(0, LANES // 128, body, 0)


def piece_specs(width):
    full = pl.BlockSpec((1, STRIP, width), lambda i: (i, 0, 0))
    half = pl.BlockSpec((1, STRIP // 2, width), lambda i: (i, 0, 0))
    return [full] * 5 + [half] * 2


def sampler_specs(width):
    return [
        pl.BlockSpec((1, 2, LANES), lambda i: (i, 0, 0)),
        pl.BlockSpec((len(ROW_ORDER), 1), lambda i: (0, 0)),
    ] + piece_specs(width)


def row_ids():
    return jnp.array(ROW_ORDER, f32)[:, None]


def sample(positions, pieces):
    images, _, width = pieces[0].shape
    return pl.pallas_call(
        sample_kernel,
        grid=(images,),
        in_specs=sampler_specs(width),
        out_specs=pl.BlockSpec((1, STRIP, 9 * width), lambda i: (i, 0, 0)),
        out_shape=jax.ShapeDtypeStruct((images, STRIP, 9 * width), bf16),
        scratch_shapes=[
            pltpu.VMEM((2 * COLS, LANES), f32),
            pltpu.VMEM((len(ROW_ORDER), LANES), f32),
            pltpu.VMEM((CELLS, LANES), bf16),
            pltpu.VMEM((CELLS, width), bf16),
        ],
        compiler_params=pltpu.CompilerParams(vmem_limit_bytes=40 * MIB),
        cost_estimate=pl.CostEstimate(
            flops=2 * images * CELLS * LANES * width,
            bytes_accessed=2 * images * (CELLS + QUERIES) * width,
            transcendentals=0,
        ),
        name="sample",
    )(positions, row_ids(), *pieces)


def sample_back(positions, pieces, upstream):
    images, _, width = pieces[0].shape
    full = (images, STRIP, width)
    half = (images, STRIP // 2, width)
    return pl.pallas_call(
        sample_back_kernel,
        grid=(images,),
        in_specs=sampler_specs(width)
        + [pl.BlockSpec((1, STRIP, 9 * width), lambda i: (i, 0, 0))],
        out_specs=piece_specs(width) + [pl.BlockSpec((1, 2, LANES), lambda i: (i, 0, 0))],
        out_shape=[jax.ShapeDtypeStruct(full, f32)]
        + [jax.ShapeDtypeStruct(full, bf16)] * 4
        + [jax.ShapeDtypeStruct(half, bf16)] * 2
        + [jax.ShapeDtypeStruct((images, 2, LANES), f32)],
        scratch_shapes=[
            pltpu.VMEM((2 * COLS, LANES), f32),
            pltpu.VMEM((len(ROW_ORDER), LANES), f32),
            pltpu.VMEM((2 * COLS, LANES), f32),
            pltpu.VMEM((len(ROW_ORDER), LANES), f32),
            pltpu.VMEM((CELLS, LANES), bf16),
            pltpu.VMEM((CELLS, width), bf16),
            pltpu.VMEM((LANES, width), bf16),
            pltpu.VMEM((CELLS, LANES), f32),
        ],
        compiler_params=pltpu.CompilerParams(vmem_limit_bytes=48 * MIB),
        cost_estimate=pl.CostEstimate(
            flops=4 * images * CELLS * LANES * width,
            bytes_accessed=4 * images * (CELLS + QUERIES) * width,
            transcendentals=0,
        ),
        name="sample_back",
    )(positions, row_ids(), *pieces, upstream)


def tap_slabs(above, own, below, padded, image):
    padded[8 : 8 + COLS, :] = above[image].astype(f32)
    padded[8 + COLS : 8 + COLS + STRIP, :] = own[image].astype(f32)
    padded[8 + COLS + STRIP : 8 + 2 * COLS + STRIP, :] = below[image].astype(f32)
    cols = lax.broadcasted_iota(jnp.int32, (STRIP, 1), 0) % COLS
    for tap in range(9):
        start = 8 + COLS * (tap // 3) + tap % 3 - 1
        slab = padded[start : start + STRIP, :]
        if tap % 3 == 0:
            slab = jnp.where(cols > 0, slab, 0.0)
        elif tap % 3 == 2:
            slab = jnp.where(cols < COLS - 1, slab, 0.0)
        yield tap, slab.astype(bf16)


def conv_kernel(above, own, below, weight, out_ref, slabs_ref, padded):
    width = own.shape[2]
    images = own.shape[0]
    for image in range(images):
        for tap, slab in tap_slabs(above, own, below, padded, image):
            slabs_ref[image, :, tap * width : (tap + 1) * width] = slab
    total = None
    for tap in range(9):
        lanes = slice(tap * width, (tap + 1) * width)
        part = dot(slabs_ref[:, :, lanes].reshape(images * STRIP, width), weight[lanes, :])
        total = part if total is None else total + part
    out_ref[...] = total.reshape(out_ref.shape)


def conv_back_kernel(above, own, below, weight, out_ref, padded, slabs):
    width = own.shape[2]
    images = own.shape[0]
    for image in range(images):
        for tap, slab in tap_slabs(above, own, below, padded, image):
            slabs[8 - tap, image * STRIP : (image + 1) * STRIP, :] = slab
    total = None
    for tap in range(9):
        part = dot_nt(slabs[tap], weight[tap * width : (tap + 1) * width, :])
        total = part if total is None else total + part
    out_ref[...] = total.reshape(out_ref.shape)


def conv_specs(images, width):
    rim = pl.BlockSpec((images, COLS, width), lambda i: (i, 0, 0))
    own = pl.BlockSpec((images, STRIP, width), lambda i: (i, 0, 0))
    return [rim, own, rim, pl.BlockSpec((9 * width, width), lambda i: (0, 0))]


def conv(above, own, below, weight):
    images, _, width = own.shape
    step = images // MB
    return pl.pallas_call(
        conv_kernel,
        grid=(MB,),
        in_specs=conv_specs(step, width),
        out_specs=[
            pl.BlockSpec((step, STRIP, width), lambda i: (i, 0, 0)),
            pl.BlockSpec((step, STRIP, 9 * width), lambda i: (i, 0, 0)),
        ],
        out_shape=[
            jax.ShapeDtypeStruct((images, STRIP, width), f32),
            jax.ShapeDtypeStruct((images, STRIP, 9 * width), bf16),
        ],
        scratch_shapes=[pltpu.VMEM((16 + 2 * COLS + STRIP, width), f32)],
        compiler_params=pltpu.CompilerParams(vmem_limit_bytes=40 * MIB),
        cost_estimate=pl.CostEstimate(
            flops=18 * images * STRIP * width * width,
            bytes_accessed=18 * width * width,
            transcendentals=0,
        ),
        name="conv",
    )(above, own, below, weight)


def conv_back(above, own, below, weight):
    images, _, width = own.shape
    step = images // MB
    return pl.pallas_call(
        conv_back_kernel,
        grid=(MB,),
        in_specs=conv_specs(step, width),
        out_specs=pl.BlockSpec((step, STRIP, width), lambda i: (i, 0, 0)),
        out_shape=jax.ShapeDtypeStruct((images, STRIP, width), f32),
        scratch_shapes=[
            pltpu.VMEM((16 + 2 * COLS + STRIP, width), f32),
            pltpu.VMEM((9, step * STRIP, width), bf16),
        ],
        compiler_params=pltpu.CompilerParams(vmem_limit_bytes=40 * MIB),
        cost_estimate=pl.CostEstimate(
            flops=18 * images * STRIP * width * width,
            bytes_accessed=18 * width * width,
            transcendentals=0,
        ),
        name="conv_back",
    )(above, own, below, weight)


def silu_slope(values):
    logistic = jax.nn.sigmoid(values)
    return logistic * (1.0 + values * (1.0 - logistic))


def box_weights(box_rows, box_cols, box_count, valid_mask, strip_rows, span_cols):
    row_ids_ = lax.axis_index("rows") * strip_rows + jnp.arange(strip_rows)
    col_ids = jnp.arange(span_cols)
    row_low = jnp.minimum(box_rows[..., 0], box_rows[..., 1])
    row_high = jnp.maximum(box_rows[..., 0], box_rows[..., 1])
    col_low = jnp.minimum(box_cols[..., 0], box_cols[..., 1])
    col_high = jnp.maximum(box_cols[..., 0], box_cols[..., 1])
    inside_rows = ((row_ids_ >= row_low[..., None]) & (row_ids_ <= row_high[..., None])).astype(f32)
    inside_cols = ((col_ids >= col_low[..., None]) & (col_ids <= col_high[..., None])).astype(f32)
    live_boxes = (jnp.arange(box_rows.shape[1])[None, :] < box_count[:, None]).astype(f32)
    covered = jnp.einsum("ib,ibh,ibw->ihw", live_boxes, inside_rows, inside_cols, precision=exact)
    return valid_mask.astype(f32) * (0.5 + covered / box_count.astype(f32)[:, None, None])


def per_batch(values):
    return values.reshape(MB, values.shape[0] // MB, values.shape[1])


def batch_totals(first, second):
    totals = all_sum(jnp.concatenate([jnp.sum(first, axis=1), jnp.sum(second, axis=1)], axis=0))
    return totals[:MB], totals[MB:]


class Norm:
    def __init__(self, values, gain, bias):
        values = per_batch(values)
        self.count = values.shape[1] * device_count()
        sums, squares = batch_totals(values, values * values)
        self.values = values
        self.center = (sums / self.count)[:, None, :]
        self.spread = lax.rsqrt(squares[:, None, :] / self.count - self.center * self.center + epsilon)
        self.gain = gain.astype(f32)
        self.bias = bias.astype(f32)

    def normed(self):
        return (self.values - self.center) * self.spread

    def forward(self):
        return self.normed() * self.gain + self.bias

    def backward(self, upstream):
        normed = self.normed()
        bias_sums, gain_sums = batch_totals(upstream, upstream * normed)
        self.gain_grad = jnp.sum(gain_sums, axis=0)
        self.bias_grad = jnp.sum(bias_sums, axis=0)
        result = (self.spread * self.gain) * (
            upstream
            - (bias_sums / self.count)[:, None, :]
            - normed * (gain_sums / self.count)[:, None, :]
        )
        return result.astype(bf16).reshape(-1, result.shape[-1])


def stacked_columns(weight, width):
    return jnp.concatenate(jnp.split(weight, weight.shape[1] // width, axis=1), axis=0)


def unstacked_columns(blocks, columns):
    count, stacked, width = blocks.shape
    parts = columns // width
    blocks = blocks.reshape(count, parts, stacked // parts, width).transpose(0, 2, 1, 3)
    return blocks.reshape(-1, columns)


def gather(pieces):
    whole = lax.all_gather(jnp.concatenate(pieces, axis=0), BOTH, axis=0)
    results = []
    start = 0
    for piece in pieces:
        results.append(whole[:, start : start + piece.shape[0]])
        start += piece.shape[0]
    return results


def to_width(flat, width):
    rows = -(-flat.shape[-1] // width)
    pad = rows * width - flat.shape[-1]
    return jnp.pad(flat, [(0, 0)] * (flat.ndim - 1) + [(0, pad)]).reshape(
        flat.shape[:-1] + (rows, width)
    )


def shifted(values, steps, columns):
    if steps == 0:
        return values
    cells = values.shape[-1]
    column = jnp.arange(cells) % columns
    pad = [(0, 0)] * (values.ndim - 1)
    if steps > 0:
        moved = jnp.pad(values[..., steps:], pad + [(0, steps)])
    else:
        moved = jnp.pad(values[..., :steps], pad + [(-steps, 0)])
    return jnp.where((column + steps >= 0) & (column + steps < columns), moved, 0)


def on_device(
    images_in,
    out_grad,
    box_rows,
    box_cols,
    box_count,
    valid_mask,
    reduce_one,
    offset_one,
    deform_one,
    expand_one,
    mid_gain_one,
    mid_bias_one,
    wide_gain_one,
    wide_bias_one,
    reduce_two,
    spatial_two,
    expand_two,
    mid_gain_two,
    mid_bias_two,
    wide_gain_two,
    wide_bias_two,
):
    images, strip_rows, span_cols, wide = images_in.shape
    mid = reduce_one.shape[1]
    assert strip_rows == STRIP_ROWS and span_cols == COLS
    count = device_count()
    pixels = images * STRIP

    vectors = jnp.concatenate(
        [mid_gain_one, mid_bias_one, mid_gain_two, mid_bias_two], axis=0
    ).reshape(-1)
    vectors = jnp.concatenate(
        [vectors, wide_gain_one, wide_bias_one, wide_gain_two, wide_bias_two]
    )
    vector_count = vectors.shape[0]
    offset_rows = offset_one.shape[0]
    offset_piece = to_width(offset_one.T, mid).transpose(1, 0, 2).reshape(-1, mid)
    reduce_all, offset_all, vector_all = gather(
        [reduce_one, offset_piece, to_width(vectors, mid)]
    )
    deform_all, expand_all = gather([deform_one, stacked_columns(expand_one, mid)])
    reduce_two_all, spatial_all, expand_two_all = gather(
        [reduce_two, spatial_two, stacked_columns(expand_two, mid)]
    )
    weight_reduce_one = reduce_all.reshape(wide, mid)
    weight_deform_one = deform_all.reshape(9 * mid, mid)
    weight_expand_one = unstacked_columns(expand_all, wide)
    weight_reduce_two = reduce_two_all.reshape(wide, mid)
    weight_spatial_two = spatial_all.reshape(9 * mid, mid)
    weight_expand_two = unstacked_columns(expand_two_all, wide)
    tap_weights = (
        offset_all.reshape(count, -1, 18, mid)
        .transpose(2, 0, 1, 3)
        .reshape(18, count, -1)[:, :, :offset_rows]
        .reshape(18, 9, wide)
        .transpose(1, 0, 2)
        .reshape(162, wide)
    )
    vector_all = vector_all.reshape(count, -1)[:, :vector_count]
    mid_part = mid // count
    wide_part = wide // count
    mid_vectors = (
        vector_all[:, : 8 * mid_part].reshape(count, 8, mid_part).transpose(1, 0, 2).reshape(8, mid)
    )
    wide_vectors = (
        vector_all[:, 8 * mid_part :].reshape(count, 4, wide_part).transpose(1, 0, 2).reshape(4, wide)
    )
    gain_mid_one, bias_mid_one = mid_vectors[0:2], mid_vectors[2:4]
    gain_mid_two, bias_mid_two = mid_vectors[4:6], mid_vectors[6:8]

    def maps(values):
        return values.reshape(images, STRIP, values.shape[-1])

    grad_weight = box_weights(box_rows, box_cols, box_count, valid_mask, strip_rows, span_cols)
    flat_inputs = images_in.reshape(pixels, wide)

    norm_a1 = Norm(dot(flat_inputs, weight_reduce_one), gain_mid_one[0], bias_mid_one[0])
    hidden = jax.nn.silu(norm_a1.forward()).astype(bf16).reshape(images, STRIP, mid)
    half = STRIP // 2
    pieces = [
        hidden,
        from_behind(hidden, -1),
        from_behind(hidden, 1),
        from_behind(hidden, -2),
        from_behind(hidden, 2),
        from_behind(hidden[:, :half], -3),
        from_behind(hidden[:, half:], 3),
    ]

    partial_offsets = dot_nt(tap_weights, flat_inputs).reshape(3, 54, images, STRIP)
    from_above = from_behind(partial_offsets[0, :, :, half:], 1)
    from_below = from_behind(partial_offsets[2, :, :, :half], -1)
    by_row = [
        jnp.concatenate([from_above, partial_offsets[0, :, :, :half]], axis=-1),
        partial_offsets[1],
        jnp.concatenate([partial_offsets[2, :, :, half:], from_below], axis=-1),
    ]
    offsets = 0.0
    for row in by_row:
        for col_tap in range(3):
            offsets = offsets + shifted(
                row[18 * col_tap : 18 * col_tap + 18], 2 * (col_tap - 1), COLS
            )
    squashed = jnp.tanh(offsets / CLIP)
    taps = jnp.arange(9)
    cells = jnp.arange(STRIP)
    row_base = ((taps // 3 - 1)[:, None] + (cells // COLS + HALO)[None, :]).astype(f32)
    col_base = ((taps % 3 - 1)[:, None] + (cells % COLS)[None, :]).astype(f32)
    base = jnp.stack([row_base, col_base])[:, :, None, :]
    positions = (CLIP * squashed).reshape(2, 9, images, STRIP) + base
    positions = positions.transpose(2, 0, 1, 3).reshape(images, 2, QUERIES)
    positions = jnp.pad(
        positions, ((0, 0), (0, 0), (0, LANES - QUERIES)), constant_values=-1000.0
    )
    sampled = sample(positions, pieces).reshape(pixels, 9 * mid)
    norm_a2 = Norm(dot(sampled, weight_deform_one), gain_mid_one[1], bias_mid_one[1])
    hidden_two = jax.nn.silu(norm_a2.forward()).astype(bf16).reshape(pixels, mid)
    norm_a3 = Norm(dot(hidden_two, weight_expand_one), wide_vectors[0], wide_vectors[1])
    joined_one = norm_a3.forward() + per_batch(flat_inputs).astype(f32)
    middle = jax.nn.silu(joined_one).astype(bf16).reshape(pixels, wide)

    norm_b1 = Norm(dot(middle, weight_reduce_two), gain_mid_two[0], bias_mid_two[0])
    inner_one = maps(jax.nn.silu(norm_b1.forward()).astype(bf16))
    fifth_conv, inner_slabs = conv(
        from_behind(inner_one[:, STRIP - COLS :], 1),
        inner_one,
        from_behind(inner_one[:, :COLS], -1),
        weight_spatial_two,
    )
    norm_b2 = Norm(fifth_conv.reshape(pixels, mid), gain_mid_two[1], bias_mid_two[1])
    inner_two = jax.nn.silu(norm_b2.forward()).astype(bf16).reshape(pixels, mid)
    norm_b3 = Norm(dot(inner_two, weight_expand_two), wide_vectors[2], wide_vectors[3])
    joined_two = norm_b3.forward() + per_batch(middle).astype(f32)
    block_out = jax.nn.silu(joined_two).astype(bf16).reshape(images_in.shape)

    upstream = per_batch(
        out_grad.reshape(pixels, wide)
    ).astype(f32) * grad_weight.reshape(MB, pixels // MB, 1)
    masked_six = upstream * silu_slope(joined_two)
    back_sixth = norm_b3.backward(masked_six)
    grad_expand_two = dot_tn(inner_two, back_sixth).astype(bf16)
    back_fifth = norm_b2.backward(
        per_batch(dot_nt(back_sixth, weight_expand_two)) * silu_slope(norm_b2.forward())
    )
    grad_spatial_two = dot_tn(inner_slabs.reshape(pixels, 9 * mid), back_fifth).astype(bf16)
    back_maps = maps(back_fifth)
    back_inner = conv_back(
        from_behind(back_maps[:, STRIP - COLS :], 1),
        back_maps,
        from_behind(back_maps[:, :COLS], -1),
        weight_spatial_two,
    ).reshape(pixels, mid)
    back_fourth = norm_b1.backward(per_batch(back_inner) * silu_slope(norm_b1.forward()))
    grad_reduce_two = dot_tn(middle, back_fourth).astype(bf16)

    def chunked(grad):
        return grad.reshape(count, -1, mid)

    def chunked_columns(grad):
        parts = grad.shape[1] // mid
        return (
            grad.reshape(count, -1, parts, mid).transpose(0, 2, 1, 3).reshape(count, -1, mid)
        )

    def unchunked_columns(shard):
        parts = wide // mid
        return shard.reshape(parts, -1, mid).transpose(1, 0, 2).reshape(-1, wide)

    def split_rows(shard, sizes):
        results = []
        start = 0
        for size in sizes:
            results.append(shard[start : start + size])
            start += size
        return results

    two_sizes = [reduce_two.shape[0], spatial_two.shape[0], expand_two.shape[0] * wide // mid]
    two_chunks = jnp.concatenate(
        [chunked(grad_reduce_two), chunked(grad_spatial_two), chunked_columns(grad_expand_two)],
        axis=1,
    )
    two_shards = split_rows(
        lax.psum_scatter(
            two_chunks.reshape(-1, mid), BOTH, scatter_dimension=0, tiled=True
        ).astype(f32),
        two_sizes,
    )

    back_middle = masked_six + per_batch(dot_nt(back_fourth, weight_reduce_two))
    masked_three = back_middle * silu_slope(joined_one)
    back_third = norm_a3.backward(masked_three)
    grad_expand_one = dot_tn(hidden_two, back_third).astype(bf16)
    back_second = norm_a2.backward(
        per_batch(dot_nt(back_third, weight_expand_one)) * silu_slope(norm_a2.forward())
    )
    grad_deform_one = dot_tn(sampled, back_second).astype(bf16)
    one_sizes = [deform_one.shape[0], expand_one.shape[0] * wide // mid]
    one_shards = split_rows(
        scatter_sum(
            jnp.concatenate([chunked(grad_deform_one), chunked_columns(grad_expand_one)], axis=1),
            (1, 4, 2, 8, 16),
        ),
        one_sizes,
    )
    back_sampled = dot_nt(back_second, weight_deform_one).astype(bf16).reshape(images, STRIP, -1)
    own, *others, position_grad = sample_back(positions, pieces, back_sampled)
    own = (
        own
        + from_behind(others[0], 1).astype(f32)
        + from_behind(others[1], -1).astype(f32)
        + from_behind(others[2], 2).astype(f32)
        + from_behind(others[3], -2).astype(f32)
        + jnp.concatenate(
            [from_behind(others[4], 3).astype(f32), from_behind(others[5], -3).astype(f32)], axis=1
        )
    )
    back_clipped = (
        position_grad[:, :, :QUERIES]
        .reshape(images, 2, 9, STRIP)
        .transpose(1, 2, 0, 3)
        .reshape(18, images, STRIP)
    )
    back_offsets = (back_clipped * (1.0 - squashed * squashed)).astype(bf16)
    rim_above = from_behind(back_offsets[:, :, half:], 1)
    rim_below = from_behind(back_offsets[:, :, :half], -1)
    by_row = [
        jnp.concatenate([back_offsets[:, :, half:], rim_below], axis=-1),
        back_offsets,
        jnp.concatenate([rim_above, back_offsets[:, :, :half]], axis=-1),
    ]
    stacked = jnp.concatenate(
        [shifted(row, -2 * (col_tap - 1), COLS) for row in by_row for col_tap in range(3)], axis=0
    ).reshape(162, pixels)
    grad_offset_one = dot(stacked, flat_inputs).astype(bf16)
    grad_offset_one = (
        grad_offset_one.reshape(9, 18, wide)
        .transpose(1, 0, 2)
        .reshape(18, count, offset_rows)
        .transpose(1, 0, 2)
    )
    offset_chunks = to_width(grad_offset_one, mid).transpose(0, 2, 1, 3).reshape(count, -1, mid)
    offset_to_images = dot_tn(stacked, tap_weights)

    back_first = norm_a1.backward(
        per_batch(own.reshape(pixels, mid)) * silu_slope(norm_a1.forward())
    )
    grad_reduce_one = dot_tn(flat_inputs, back_first).astype(bf16)
    grad_images = (
        masked_three.reshape(pixels, wide)
        + dot_nt(back_first, weight_reduce_one)
        + offset_to_images
    ).reshape(images_in.shape)
    last_shards = split_rows(
        scatter_sum(
            jnp.concatenate([chunked(grad_reduce_one), offset_chunks], axis=1), (1, 2, 4, 8, 16)
        ),
        [reduce_one.shape[0], offset_chunks.shape[1]],
    )
    offset_shard = (
        last_shards[1].reshape(-1, 18, mid).transpose(1, 0, 2).reshape(18, -1)[:, :offset_rows].T
    )

    me = lax.axis_index(BOTH)
    mid_grads = jnp.stack(
        [
            norm_a1.gain_grad,
            norm_a2.gain_grad,
            norm_a1.bias_grad,
            norm_a2.bias_grad,
            norm_b1.gain_grad,
            norm_b2.gain_grad,
            norm_b1.bias_grad,
            norm_b2.bias_grad,
        ]
    )
    mid_grads = lax.dynamic_slice_in_dim(mid_grads, me * mid_part, mid_part, 1)
    wide_grads = jnp.stack(
        [norm_a3.gain_grad, norm_a3.bias_grad, norm_b3.gain_grad, norm_b3.bias_grad]
    )
    wide_grads = lax.dynamic_slice_in_dim(wide_grads, me * wide_part, wide_part, 1)
    return (
        block_out,
        grad_images,
        last_shards[0],
        offset_shard,
        one_shards[0],
        unchunked_columns(one_shards[1]),
        mid_grads[0:2],
        mid_grads[2:4],
        wide_grads[0],
        wide_grads[1],
        two_shards[0],
        two_shards[1],
        unchunked_columns(two_shards[2]),
        mid_grads[4:6],
        mid_grads[6:8],
        wide_grads[2],
        wide_grads[3],
    )


def solution(mesh):
    whole = P(BOTH, None)
    part = P(None, BOTH)
    line = P(BOTH)
    maps = P("img", "rows", None, None)
    return jax.shard_map(
        on_device,
        mesh=mesh,
        in_specs=(
            maps,
            maps,
            P("img", None, None),
            P("img", None, None),
            P("img"),
            P("img", "rows", None),
            whole,
            whole,
            whole,
            whole,
            part,
            part,
            line,
            line,
            whole,
            whole,
            whole,
            part,
            part,
            line,
            line,
        ),
        out_specs=(
            maps,
            maps,
            whole,
            whole,
            whole,
            whole,
            part,
            part,
            line,
            line,
            whole,
            whole,
            whole,
            part,
            part,
            line,
            line,
        ),
        check_vma=False,
    )
```

```python
from functools import partial

import jax
import jax.numpy as jnp
from jax import lax
from jax.experimental import pallas as pl
from jax.experimental.pallas import tpu as pltpu
from jax.sharding import PartitionSpec as P

CLIP = 8
HALO = 10
MB = 2
BOTH = ("rows", "img")
MIB = 2**20

epsilon = 1e-05
exact = lax.Precision.HIGHEST
f32 = jnp.float32
bf16 = jnp.bfloat16

STRIP_ROWS = 4
COLS = 44
STRIP = STRIP_ROWS * COLS
QUERIES = 9 * STRIP
LANES = 1664
CELLS = (STRIP_ROWS + 2 * HALO) * COLS
ROW_ORDER = (10, 11, 12, 13, 14, 15, 16, 17, 6, 7, 8, 9, 18, 19, 20, 21, 2, 3, 4, 5, 22, 23, 0, 1)


SMALL = pl.CostEstimate(flops=1, bytes_accessed=1, transcendentals=0)


def dot(left, right):
    return jnp.dot(left, right, preferred_element_type=f32)


def dot_nt(left, right):
    return lax.dot_general(left, right, (((1,), (1,)), ((), ())), preferred_element_type=f32)


def dot_tn(left, right):
    return lax.dot_general(left, right, (((0,), (0,)), ((), ())), preferred_element_type=f32)


def device_count():
    return lax.axis_size(BOTH)


def exchange(value, mask):
    return lax.ppermute(value, BOTH, [(i, i ^ mask) for i in range(device_count())])


def all_sum(value):
    count = device_count()
    bit = 1
    while bit < count:
        masks = [bit, 2 * bit, 3 * bit] if 2 * bit < count else [bit]
        parts = [exchange(value, mask) for mask in masks]
        for part in parts:
            value = value + part
        bit *= 4
    return value


def bits_of(order):
    bits = [1 << k for k in range(device_count().bit_length() - 1)]
    return [b for b in order if b in bits] + [b for b in bits if b not in order]


def tie(value, *others):
    return lax.optimization_barrier((value,) + others)[0]


def meet(*values):
    return lax.optimization_barrier(values)


class Scatter:
    def __init__(self, pieces, order):
        self.order = bits_of(order)
        bits = sorted(self.order, reverse=True)
        count = len(bits)
        axes = [bits.index(b) for b in self.order] + [count, count + 1]
        self.value = jnp.concatenate(
            [piece.reshape((2,) * count + piece.shape[1:]).transpose(axes) for piece in pieces],
            axis=-2,
        )

    def step(self):
        bit = self.order.pop(0)
        mine = (lax.axis_index(BOTH) // bit) % 2
        keep = lax.dynamic_index_in_dim(self.value, mine, 0, keepdims=False)
        send = lax.dynamic_index_in_dim(self.value, 1 - mine, 0, keepdims=False)
        total = keep.astype(f32) + exchange(send, bit).astype(f32)
        self.value = total.astype(bf16) if self.order else total
        return self.value

    def finish(self):
        while self.order:
            self.step()
        return self.value


class Gather:
    def __init__(self, piece, groups):
        bits = bits_of(())
        self.groups = [tuple(b for b in group if b in bits) for group in groups]
        self.groups += [(b,) for b in bits if not any(b in group for group in self.groups)]
        self.done = []
        self.piece = piece
        self.value = piece

    def step(self):
        group = self.groups.pop(0)
        by_mask = {0: self.value}
        for bit in group:
            for mask in sub_masks(group, bit):
                by_mask[bit + mask] = exchange(self.value, bit + mask)
        for bit in group:
            mine = (lax.axis_index(BOTH) // bit) % 2 == 1
            self.done = sorted(self.done + [bit], reverse=True)
            axis = self.done.index(bit)
            merged = {}
            for mask, part in by_mask.items():
                if not mask & bit:
                    other = by_mask[mask + bit]
                    merged[mask] = jnp.stack(
                        [jnp.where(mine, other, part), jnp.where(mine, part, other)], axis=axis
                    )
            by_mask = merged
        (self.value,) = by_mask.values()

    def result(self):
        return self.value.reshape((-1,) + self.piece.shape)


def sub_masks(group, bit):
    masks = [0]
    for other in group[: group.index(bit)]:
        masks = masks + [mask + other for mask in masks]
    return masks


def from_behind(value, steps):
    count = lax.axis_size("rows")
    first, last = (max(0, -steps), min(count, count - steps))
    return lax.ppermute(value, "rows", [(source, source + steps) for source in range(first, last)])


def spline(values):
    magnitude = jnp.abs(values)
    outer = 1.5 - magnitude
    return jnp.where(
        magnitude < 0.5,
        0.75 - values * values,
        jnp.where(magnitude < 1.5, 0.5 * outer * outer, 0.0),
    )


def spline_slope(values):
    magnitude = jnp.abs(values)
    outer = 1.5 - magnitude
    return jnp.where(
        magnitude < 0.5,
        -2.0 * values,
        jnp.where(magnitude < 1.5, jnp.where(values > 0, -outer, outer), 0.0),
    )


def fill_factors(pos_ref, row_ref, col_weight, row_weight, col_slope=None, row_slope=None):
    cell_cols = lax.broadcasted_iota(jnp.int32, (2 * COLS, LANES), 0)
    cell_cols = jnp.where(cell_cols >= COLS, cell_cols - COLS, cell_cols).astype(f32)
    col_gap = pos_ref[0, 1:2, :] - cell_cols
    row_gap = pos_ref[0, 0:1, :] - row_ref[...]
    col_weight[...] = spline(col_gap)
    row_weight[...] = spline(row_gap)
    if col_slope is not None:
        col_slope[...] = spline_slope(col_gap)
        row_slope[...] = spline_slope(row_gap)


def fill_sampler(col_weight, row_weight, sampler):
    low = lax.broadcasted_iota(jnp.int32, (8, 128), 0) < 4

    def body(tile, carry):
        lanes = pl.ds(pl.multiple_of(tile * 128, 128), 128)
        for block in range(6):
            for chunk in range(11):
                halves = []
                for group in (2 * chunk, 2 * chunk + 1):
                    first, last = (8 * group) // COLS, (8 * group + 7) // COLS
                    weight = row_weight[4 * block + first : 4 * block + first + 1, lanes]
                    if first != last:
                        weight = jnp.where(
                            low, weight, row_weight[4 * block + last : 4 * block + last + 1, lanes]
                        )
                    local = group % 11
                    halves.append(col_weight[8 * local : 8 * local + 8, lanes] * weight)
                start = block * STRIP + 16 * chunk
                sampler[start : start + 16, lanes] = jnp.concatenate(halves, axis=0).astype(bf16)
        return carry

    lax.fori_loop(0, LANES // 128, body, 0)


def fill_window(pieces, window):
    for index, piece in enumerate(pieces[:5]):
        window[index * STRIP : (index + 1) * STRIP, :] = piece[0]
    window[5 * STRIP : 6 * STRIP, :] = jnp.concatenate([pieces[5][0], pieces[6][0]], axis=0)


def sample_kernel(pos_ref, row_ref, *refs):
    pieces, out_ref = refs[:7], refs[7]
    col_weight, row_weight, sampler, window = refs[8:]
    fill_factors(pos_ref, row_ref, col_weight, row_weight)
    fill_sampler(col_weight, row_weight, sampler)
    fill_window(pieces, window)
    result = dot_tn(window[...], sampler[...]).T.astype(bf16)
    width = window.shape[1]
    for tap in range(9):
        out_ref[0, :, tap * width : (tap + 1) * width] = result[tap * STRIP : (tap + 1) * STRIP]


def sample_back_kernel(pos_ref, row_ref, *refs):
    pieces, upstream_ref = refs[:7], refs[7]
    grads, pos_grad = refs[8:15], refs[15]
    (
        col_weight,
        row_weight,
        col_slope,
        row_slope,
        sampler,
        window,
        upstream,
        sampler_grad,
    ) = refs[16:]
    fill_factors(pos_ref, row_ref, col_weight, row_weight, col_slope, row_slope)
    fill_sampler(col_weight, row_weight, sampler)
    fill_window(pieces, window)
    width = window.shape[1]
    for tap in range(9):
        upstream[tap * STRIP : (tap + 1) * STRIP, :] = upstream_ref[
            0, :, tap * width : (tap + 1) * width
        ]
    upstream[QUERIES:LANES, :] = jnp.zeros((LANES - QUERIES, width), bf16)
    sampler_grad[...] = dot_nt(window[...], upstream[...])
    for index, grad in enumerate(grads[:5]):
        grad[0] = dot(sampler[index * STRIP : (index + 1) * STRIP, :], upstream[...]).astype(
            grad.dtype
        )
    last = dot(sampler[5 * STRIP :, :], upstream[...])
    grads[5][0] = last[: STRIP // 2].astype(bf16)
    grads[6][0] = last[STRIP // 2 :].astype(bf16)
    low = lax.broadcasted_iota(jnp.int32, (8, 128), 0) < 4

    def body(tile, carry):
        lanes = pl.ds(pl.multiple_of(tile * 128, 128), 128)
        zero = jnp.zeros((8, 128), f32)
        weights = [col_weight[8 * group : 8 * group + 8, lanes] for group in range(11)]
        middle_low = jnp.where(low, weights[5], 0.0)
        middle_high = jnp.where(low, 0.0, weights[5])
        row_total = zero
        col_totals = [zero] * 11
        for pair in range(12):
            first = row_weight[2 * pair : 2 * pair + 1, lanes]
            second = row_weight[2 * pair + 1 : 2 * pair + 2, lanes]
            mixed = jnp.where(low, first, second)
            first_sum = zero
            second_sum = zero
            for group in range(11):
                start = 88 * pair + 8 * group
                value = sampler_grad[start : start + 8, lanes]
                if group < 5:
                    first_sum = first_sum + value * weights[group]
                    col_totals[group] = col_totals[group] + value * first
                elif group > 5:
                    second_sum = second_sum + value * weights[group]
                    col_totals[group] = col_totals[group] + value * second
                else:
                    first_sum = first_sum + value * middle_low
                    second_sum = second_sum + value * middle_high
                    col_totals[group] = col_totals[group] + value * mixed
            row_total = (
                row_total
                + first_sum * row_slope[2 * pair : 2 * pair + 1, lanes]
                + second_sum * row_slope[2 * pair + 1 : 2 * pair + 2, lanes]
            )
        col_total = zero
        for group in range(11):
            col_total = col_total + col_totals[group] * col_slope[8 * group : 8 * group + 8, lanes]
        pos_grad[0, 0:1, lanes] = jnp.sum(row_total, axis=0, keepdims=True)
        pos_grad[0, 1:2, lanes] = jnp.sum(col_total, axis=0, keepdims=True)
        return carry

    lax.fori_loop(0, LANES // 128, body, 0)


def piece_specs(width, first=0):
    full = pl.BlockSpec((1, STRIP, width), lambda i: (i + first, 0, 0))
    half = pl.BlockSpec((1, STRIP // 2, width), lambda i: (i + first, 0, 0))
    return [full] * 5 + [half] * 2


def sampler_specs(width, first=0):
    return [
        pl.BlockSpec((1, 2, LANES), lambda i: (i + first, 0, 0)),
        pl.BlockSpec((len(ROW_ORDER), 1), lambda i: (0, 0)),
    ] + piece_specs(width, first)


def row_ids():
    return jnp.array(ROW_ORDER, f32)[:, None]


def sample(positions, pieces):
    images, _, width = pieces[0].shape
    return pl.pallas_call(
        sample_kernel,
        grid=(images,),
        in_specs=sampler_specs(width),
        out_specs=pl.BlockSpec((1, STRIP, 9 * width), lambda i: (i, 0, 0)),
        out_shape=jax.ShapeDtypeStruct((images, STRIP, 9 * width), bf16),
        scratch_shapes=[
            pltpu.VMEM((2 * COLS, LANES), f32),
            pltpu.VMEM((len(ROW_ORDER), LANES), f32),
            pltpu.VMEM((CELLS, LANES), bf16),
            pltpu.VMEM((CELLS, width), bf16),
        ],
        compiler_params=pltpu.CompilerParams(vmem_limit_bytes=60 * MIB),
        cost_estimate=SMALL,
        name="sample",
    )(positions, row_ids(), *pieces)


def sample_back(positions, pieces, upstream, first, images):
    width = pieces[0].shape[2]
    full = (images, STRIP, width)
    half = (images, STRIP // 2, width)
    return pl.pallas_call(
        sample_back_kernel,
        grid=(images,),
        in_specs=sampler_specs(width, first)
        + [pl.BlockSpec((1, STRIP, 9 * width), lambda i: (i + first, 0, 0))],
        out_specs=piece_specs(width) + [pl.BlockSpec((1, 2, LANES), lambda i: (i, 0, 0))],
        out_shape=[jax.ShapeDtypeStruct(full, f32)]
        + [jax.ShapeDtypeStruct(full, bf16)] * 4
        + [jax.ShapeDtypeStruct(half, bf16)] * 2
        + [jax.ShapeDtypeStruct((images, 2, LANES), f32)],
        scratch_shapes=[
            pltpu.VMEM((2 * COLS, LANES), f32),
            pltpu.VMEM((len(ROW_ORDER), LANES), f32),
            pltpu.VMEM((2 * COLS, LANES), f32),
            pltpu.VMEM((len(ROW_ORDER), LANES), f32),
            pltpu.VMEM((CELLS, LANES), bf16),
            pltpu.VMEM((CELLS, width), bf16),
            pltpu.VMEM((LANES, width), bf16),
            pltpu.VMEM((CELLS, LANES), f32),
        ],
        compiler_params=pltpu.CompilerParams(vmem_limit_bytes=34 * MIB),
        cost_estimate=SMALL,
        name="sample_back",
    )(positions, row_ids(), *pieces, upstream)


def tap_slabs(above, own, below, padded, image):
    padded[8 : 8 + COLS, :] = above[image].astype(f32)
    padded[8 + COLS : 8 + COLS + STRIP, :] = own[image].astype(f32)
    padded[8 + COLS + STRIP : 8 + 2 * COLS + STRIP, :] = below[image].astype(f32)
    cols = lax.broadcasted_iota(jnp.int32, (STRIP, 1), 0) % COLS
    for tap in range(9):
        start = 8 + COLS * (tap // 3) + tap % 3 - 1
        slab = padded[start : start + STRIP, :]
        if tap % 3 == 0:
            slab = jnp.where(cols > 0, slab, 0.0)
        elif tap % 3 == 2:
            slab = jnp.where(cols < COLS - 1, slab, 0.0)
        yield tap, slab.astype(bf16)


def conv_kernel(above, own, below, weight, out_ref, slabs_ref, padded):
    width = own.shape[2]
    images = own.shape[0]
    for image in range(images):
        for tap, slab in tap_slabs(above, own, below, padded, image):
            slabs_ref[image, :, tap * width : (tap + 1) * width] = slab
    total = None
    for tap in range(9):
        lanes = slice(tap * width, (tap + 1) * width)
        part = dot(slabs_ref[:, :, lanes].reshape(images * STRIP, width), weight[lanes, :])
        total = part if total is None else total + part
    out_ref[...] = total.reshape(out_ref.shape)


def conv_back_kernel(above, own, below, weight, out_ref, padded, slabs):
    width = own.shape[2]
    images = own.shape[0]
    for image in range(images):
        for tap, slab in tap_slabs(above, own, below, padded, image):
            slabs[8 - tap, image * STRIP : (image + 1) * STRIP, :] = slab
    total = None
    for tap in range(9):
        part = dot_nt(slabs[tap], weight[tap * width : (tap + 1) * width, :])
        total = part if total is None else total + part
    out_ref[...] = total.reshape(out_ref.shape)


def conv_specs(images, width):
    rim = pl.BlockSpec((images, COLS, width), lambda i: (i, 0, 0))
    own = pl.BlockSpec((images, STRIP, width), lambda i: (i, 0, 0))
    return [rim, own, rim, pl.BlockSpec((9 * width, width), lambda i: (0, 0))]


def conv(above, own, below, weight):
    images, _, width = own.shape
    step = images // MB
    return pl.pallas_call(
        conv_kernel,
        grid=(MB,),
        in_specs=conv_specs(step, width),
        out_specs=[
            pl.BlockSpec((step, STRIP, width), lambda i: (i, 0, 0)),
            pl.BlockSpec((step, STRIP, 9 * width), lambda i: (i, 0, 0)),
        ],
        out_shape=[
            jax.ShapeDtypeStruct((images, STRIP, width), f32),
            jax.ShapeDtypeStruct((images, STRIP, 9 * width), bf16),
        ],
        scratch_shapes=[pltpu.VMEM((16 + 2 * COLS + STRIP, width), f32)],
        compiler_params=pltpu.CompilerParams(vmem_limit_bytes=24 * MIB),
        cost_estimate=SMALL,
        name="conv",
    )(above, own, below, weight)


def conv_back(above, own, below, weight):
    images, _, width = own.shape
    step = images // MB
    return pl.pallas_call(
        conv_back_kernel,
        grid=(MB,),
        in_specs=conv_specs(step, width),
        out_specs=pl.BlockSpec((step, STRIP, width), lambda i: (i, 0, 0)),
        out_shape=jax.ShapeDtypeStruct((images, STRIP, width), f32),
        scratch_shapes=[
            pltpu.VMEM((16 + 2 * COLS + STRIP, width), f32),
            pltpu.VMEM((9, step * STRIP, width), bf16),
        ],
        compiler_params=pltpu.CompilerParams(vmem_limit_bytes=24 * MIB),
        cost_estimate=SMALL,
        name="conv_back",
    )(above, own, below, weight)


TAP = 32


def offset_spans(device, rows, wide):
    spans = []
    start = device * rows
    while start < (device + 1) * rows:
        tap, column = divmod(start, wide)
        size = min((device + 1) * rows - start, wide - column)
        spans.append((tap, column, start - device * rows, size))
        start += size
    return spans


def offset_stack(strip, extra, width):
    rows = strip.shape[-1]
    lead = [(0, 0)] * (strip.ndim - 2)
    strip = jnp.pad(strip, lead + [(0, TAP - 18), (0, 0)])
    full = rows // width * width
    blocks = [strip[..., start : start + width] for start in range(0, full, width)]
    rest = strip[..., full:]
    rest = jnp.concatenate([rest[..., :16, :], rest[..., 16:, :]], axis=-1)
    pad = width - rest.shape[-1] - extra.shape[-1]
    assert pad >= 0
    blocks.append(jnp.pad(jnp.concatenate([rest, extra], axis=-1), lead + [(0, 0), (0, pad)]))
    return jnp.concatenate(blocks, axis=-2)


def spread_rows(values, images, take):
    parts = []
    for image in range(images):
        parts += take(image)
    return jnp.concatenate(parts, axis=1)


def own_lanes(values, image, start):
    first = image * STRIP + start
    return values[:, first : first + STRIP // 2]


def rim_lanes(values, image):
    return values[:, image * STRIP // 2 : (image + 1) * STRIP // 2]


def down_two(own, above, images):
    return spread_rows(own, images, lambda i: [rim_lanes(above, i), own_lanes(own, i, 0)])


def up_two(own, below, images):
    return spread_rows(own, images, lambda i: [own_lanes(own, i, STRIP // 2), rim_lanes(below, i)])


def beside(values, steps):
    if steps == 0:
        return values
    rows, cells = values.shape
    column = lax.broadcasted_iota(jnp.int32, (1, cells), 1) % COLS
    empty = jnp.zeros((rows, abs(steps)), values.dtype)
    if steps > 0:
        moved = jnp.concatenate([values[:, steps:], empty], axis=1)
    else:
        moved = jnp.concatenate([empty, values[:, :steps]], axis=1)
    return jnp.where((column + steps >= 0) & (column + steps < COLS), moved, 0.0)


def offset_conv_kernel(rows, small_ref, input_ref, taps_ref, partial_ref, last_ref, first_ref):
    count, _, width = small_ref.shape
    wide = input_ref.shape[1]
    images = input_ref.shape[0] // STRIP
    full = rows // width
    rest = rows - full * width
    for device in range(count):
        blocks = [small_ref[device, TAP * i : TAP * (i + 1), :] for i in range(full)]
        if rest:
            block = small_ref[device, TAP * full : TAP * full + 16, :]
            blocks.append(
                jnp.concatenate([block[:, :rest], block[:, rest : 2 * rest]], axis=0)
            )
        strip = jnp.concatenate(blocks, axis=1)
        for tap, column, local, size in offset_spans(device, rows, wide):
            taps_ref[TAP * tap : TAP * (tap + 1), column : column + size] = strip[
                :, local : local + size
            ]
    partial = dot_nt(taps_ref[...], input_ref[...])
    partial_ref[...] = partial
    half = STRIP // 2
    for image in range(images):
        lanes = slice(image * half, (image + 1) * half)
        last_ref[:, lanes] = own_lanes(partial[: 3 * TAP], image, half)
        first_ref[:, lanes] = own_lanes(partial[6 * TAP :], image, 0)


def offset_conv(small_all, rows, inputs):
    pixels, wide = inputs.shape
    rim = (3 * TAP, pixels // 2)
    return pl.pallas_call(
        partial(offset_conv_kernel, rows),
        out_shape=[
            jax.ShapeDtypeStruct((9 * TAP, wide), bf16),
            jax.ShapeDtypeStruct((9 * TAP, pixels), f32),
            jax.ShapeDtypeStruct(rim, f32),
            jax.ShapeDtypeStruct(rim, f32),
        ],
        compiler_params=pltpu.CompilerParams(vmem_limit_bytes=24 * MIB),
        name="offset_conv",
    )(small_all, inputs)


def positions_kernel(partial_ref, above_ref, below_ref, squashed_ref, positions_ref):
    images = positions_ref.shape[0]
    rows = [
        down_two(partial_ref[: 3 * TAP, :], above_ref[...], images),
        partial_ref[3 * TAP : 6 * TAP, :],
        up_two(partial_ref[6 * TAP :, :], below_ref[...], images),
    ]
    offsets = None
    for row in rows:
        for col_tap in range(3):
            part = beside(row[TAP * col_tap : TAP * (col_tap + 1)], 2 * (col_tap - 1))
            offsets = part if offsets is None else offsets + part
    squashed = jnp.tanh(offsets / CLIP)
    squashed_ref[...] = squashed
    clipped = CLIP * squashed
    cells = images * STRIP
    lane = lax.broadcasted_iota(jnp.int32, (9, cells), 1) % STRIP
    tap = lax.broadcasted_iota(jnp.int32, (9, cells), 0)
    row_position = clipped[:9] + (tap // 3 - 1 + HALO + lane // COLS).astype(f32)
    col_position = clipped[9:18] + (tap % 3 - 1 + lane % COLS).astype(f32)
    positions_ref[:, :, QUERIES:] = jnp.full((images, 2, LANES - QUERIES), -1000.0, f32)
    for image in range(images):
        lanes = slice(image * STRIP, (image + 1) * STRIP)
        for t in range(9):
            place = slice(t * STRIP, (t + 1) * STRIP)
            positions_ref[image, 0:1, place] = row_position[t : t + 1, lanes]
            positions_ref[image, 1:2, place] = col_position[t : t + 1, lanes]


def sample_positions(partial_offsets, above, below):
    cells = partial_offsets.shape[1]
    return pl.pallas_call(
        positions_kernel,
        out_shape=[
            jax.ShapeDtypeStruct((TAP, cells), f32),
            jax.ShapeDtypeStruct((cells // STRIP, 2, LANES), f32),
        ],
        name="sample_positions",
    )(partial_offsets, above, below)


def offset_slope_kernel(position_grad_ref, squashed_ref, back_ref, last_ref, first_ref, flat):
    images = position_grad_ref.shape[0]
    flat[...] = jnp.zeros_like(flat)
    for image in range(images):
        lanes = slice(image * STRIP, (image + 1) * STRIP)
        for t in range(9):
            place = slice(t * STRIP, (t + 1) * STRIP)
            flat[t : t + 1, lanes] = position_grad_ref[image, 0:1, place]
            flat[9 + t : 10 + t, lanes] = position_grad_ref[image, 1:2, place]
    squashed = squashed_ref[...]
    back = (flat[...] * (1.0 - squashed * squashed)).astype(bf16)
    back_ref[...] = back
    half = STRIP // 2
    wider = back.astype(f32)
    for image in range(images):
        lanes = slice(image * half, (image + 1) * half)
        last_ref[:, lanes] = own_lanes(wider, image, half).astype(bf16)
        first_ref[:, lanes] = own_lanes(wider, image, 0).astype(bf16)


def offset_slope(position_grad, squashed):
    cells = squashed.shape[1]
    rim = jax.ShapeDtypeStruct((TAP, cells // 2), bf16)
    return pl.pallas_call(
        offset_slope_kernel,
        out_shape=[jax.ShapeDtypeStruct((TAP, cells), bf16), rim, rim],
        scratch_shapes=[pltpu.VMEM((TAP, cells), f32)],
        name="offset_slope",
    )(position_grad, squashed)


def offset_back_kernel(rows, back_ref, above_ref, below_ref, input_ref, stacked_ref, chunks_ref):
    count, _, width = chunks_ref.shape
    wide = input_ref.shape[1]
    images = input_ref.shape[0] // STRIP
    own = back_ref[...].astype(f32)
    by_row = [
        up_two(own, below_ref[...].astype(f32), images),
        own,
        down_two(own, above_ref[...].astype(f32), images),
    ]
    for tap in range(9):
        moved = beside(by_row[tap // 3], -2 * (tap % 3 - 1))
        stacked_ref[TAP * tap : TAP * (tap + 1), :] = moved.astype(bf16)
    grad = dot(stacked_ref[...], input_ref[...])
    full = rows // width
    rest = rows - full * width
    chunks_ref[...] = jnp.zeros(chunks_ref.shape, bf16)
    for device in range(count):
        strip = jnp.concatenate(
            [
                grad[TAP * tap : TAP * (tap + 1), column : column + size]
                for tap, column, _, size in offset_spans(device, rows, wide)
            ],
            axis=1,
        ).astype(bf16)
        for i in range(full):
            chunks_ref[device, TAP * i : TAP * (i + 1), :] = strip[:, width * i : width * (i + 1)]
        if rest:
            tail = strip[:, width * full :]
            chunks_ref[device, TAP * full :, : 2 * rest] = jnp.concatenate(
                [tail[:16], tail[16:]], axis=1
            )


def offset_back(back, above, below, inputs, count, rows, width):
    pixels, wide = inputs.shape
    stack_rows = rows // width * TAP + (16 if rows % width else 0)
    return pl.pallas_call(
        partial(offset_back_kernel, rows),
        out_shape=[
            jax.ShapeDtypeStruct((9 * TAP, pixels), bf16),
            jax.ShapeDtypeStruct((count, stack_rows, width), bf16),
        ],
        compiler_params=pltpu.CompilerParams(vmem_limit_bytes=24 * MIB),
        name="offset_back",
    )(back, above, below, inputs)


def offset_unstack(shard, rows):
    width = shard.shape[1]
    full = rows // width
    rest = rows - full * width
    blocks = [shard[TAP * i : TAP * i + 18] for i in range(full)]
    if rest:
        tail = shard[TAP * full :]
        blocks.append(jnp.concatenate([tail[:, :rest], tail[:2, rest : 2 * rest]], axis=0))
    return jnp.concatenate(blocks, axis=1).T


def silu_slope(values):
    logistic = jax.nn.sigmoid(values)
    return logistic * (1.0 + values * (1.0 - logistic))


def box_weights(box_rows, box_cols, box_count, valid_mask, strip_rows, span_cols):
    row_ids_ = lax.axis_index("rows") * strip_rows + jnp.arange(strip_rows)
    col_ids = jnp.arange(span_cols)
    row_low = jnp.minimum(box_rows[..., 0], box_rows[..., 1])
    row_high = jnp.maximum(box_rows[..., 0], box_rows[..., 1])
    col_low = jnp.minimum(box_cols[..., 0], box_cols[..., 1])
    col_high = jnp.maximum(box_cols[..., 0], box_cols[..., 1])
    inside_rows = ((row_ids_ >= row_low[..., None]) & (row_ids_ <= row_high[..., None])).astype(f32)
    inside_cols = ((col_ids >= col_low[..., None]) & (col_ids <= col_high[..., None])).astype(f32)
    live_boxes = (jnp.arange(box_rows.shape[1])[None, :] < box_count[:, None]).astype(f32)
    covered = jnp.einsum("ib,ibh,ibw->ihw", live_boxes, inside_rows, inside_cols, precision=exact)
    return valid_mask.astype(f32) * (0.5 + covered / box_count.astype(f32)[:, None, None])


def per_batch(values):
    return values.reshape(MB, values.shape[0] // MB, values.shape[1])


def batch_totals(first, second):
    totals = all_sum(jnp.concatenate([jnp.sum(first, axis=1), jnp.sum(second, axis=1)], axis=0))
    return totals[:MB], totals[MB:]


class Norm:
    def __init__(self, values, gain, bias):
        values = per_batch(values)
        self.count = values.shape[1] * device_count()
        sums, squares = batch_totals(values, values * values)
        self.values = values
        self.center = (sums / self.count)[:, None, :]
        self.spread = lax.rsqrt(squares[:, None, :] / self.count - self.center * self.center + epsilon)
        self.gain = gain.astype(f32)
        self.bias = bias.astype(f32)

    def normed(self):
        return (self.values - self.center) * self.spread

    def forward(self):
        return self.normed() * self.gain + self.bias

    def backward(self, upstream):
        normed = self.normed()
        bias_sums, gain_sums = batch_totals(upstream, upstream * normed)
        self.gain_grad = jnp.sum(gain_sums, axis=0)
        self.bias_grad = jnp.sum(bias_sums, axis=0)
        result = (self.spread * self.gain) * (
            upstream
            - (bias_sums / self.count)[:, None, :]
            - normed * (gain_sums / self.count)[:, None, :]
        )
        return result.astype(bf16).reshape(-1, result.shape[-1])


def stacked_columns(weight, width):
    return jnp.concatenate(jnp.split(weight, weight.shape[1] // width, axis=1), axis=0)


def unstacked_columns(blocks, columns):
    width = blocks.shape[2]
    parts = jnp.split(blocks, columns // width, axis=1)
    return jnp.concatenate([part.reshape(-1, width) for part in parts], axis=1)


def gather(pieces):
    whole = lax.all_gather(jnp.concatenate(pieces, axis=0), BOTH, axis=0)
    results = []
    start = 0
    for piece in pieces:
        results.append(whole[:, start : start + piece.shape[0]])
        start += piece.shape[0]
    return results


def to_width(flat, width):
    rows = -(-flat.shape[-1] // width)
    pad = rows * width - flat.shape[-1]
    return jnp.pad(flat, [(0, 0)] * (flat.ndim - 1) + [(0, pad)]).reshape(
        flat.shape[:-1] + (rows, width)
    )


def widths(values, width):
    pieces = []
    for start in range(0, values.shape[-1], width):
        piece = values[..., start : start + width]
        pad = width - piece.shape[-1]
        pieces.append(jnp.pad(piece, [(0, 0)] * (values.ndim - 1) + [(0, pad)]))
    return pieces


def shifted(values, steps, columns):
    if steps == 0:
        return values
    cells = values.shape[-1]
    column = jnp.arange(cells) % columns
    pad = [(0, 0)] * (values.ndim - 1)
    if steps > 0:
        moved = jnp.pad(values[..., steps:], pad + [(0, steps)])
    else:
        moved = jnp.pad(values[..., :steps], pad + [(-steps, 0)])
    return jnp.where((column + steps >= 0) & (column + steps < columns), moved, 0)


def on_device(
    images_in,
    out_grad,
    box_rows,
    box_cols,
    box_count,
    valid_mask,
    reduce_one,
    offset_one,
    deform_one,
    expand_one,
    mid_gain_one,
    mid_bias_one,
    wide_gain_one,
    wide_bias_one,
    reduce_two,
    spatial_two,
    expand_two,
    mid_gain_two,
    mid_bias_two,
    wide_gain_two,
    wide_bias_two,
):
    images, strip_rows, span_cols, wide = images_in.shape
    mid = reduce_one.shape[1]
    assert strip_rows == STRIP_ROWS and span_cols == COLS
    count = device_count()
    pixels = images * STRIP

    mid_part = mid // count
    wide_part = wide // count
    vector_rows = [mid_gain_one, mid_bias_one, mid_gain_two, mid_bias_two] + [
        vector[None] for vector in (wide_gain_one, wide_bias_one, wide_gain_two, wide_bias_two)
    ]
    extent = max(mid_part, wide_part)
    vectors = jnp.concatenate(
        [jnp.pad(rows, ((0, 0), (0, extent - rows.shape[1]))) for rows in vector_rows]
        + [jnp.zeros((4, extent), bf16)],
        axis=0,
    )
    offset_rows = offset_one.shape[0]
    small = offset_stack(offset_one.T, vectors, mid)
    flat_inputs = images_in.reshape(pixels, wide)
    flat_out_grad = out_grad.reshape(pixels, wide)
    reduce_gather = Gather(reduce_one, ((8, 16), (4,), (2,), (1,)))
    small_gather = Gather(small, ((8, 16), (2,), (4,), (1,)))
    while reduce_gather.groups:
        reduce_gather.step()
        small_gather.step()
        if len(reduce_gather.groups) == 1:
            reduce_gather.value, small_gather.value, flat_inputs = meet(
                reduce_gather.value, small_gather.value, flat_inputs
            )
        else:
            reduce_gather.value, small_gather.value = meet(reduce_gather.value, small_gather.value)
    reduce_all, small_all = reduce_gather.result(), small_gather.result()
    deform_all, expand_all = gather([deform_one, stacked_columns(expand_one, mid)])
    weight_reduce_one = reduce_all.reshape(wide, mid)
    weight_deform_one = deform_all.reshape(9 * mid, mid)
    weight_expand_one = unstacked_columns(expand_all, wide)
    vector_start = 2 * (offset_rows % mid)
    vector_all = small_all[:, small.shape[0] - 16 :, vector_start : vector_start + extent]
    mid_vectors = vector_all[:, :8, :mid_part].transpose(1, 0, 2).reshape(8, mid)
    wide_vectors = vector_all[:, 8:12, :wide_part].transpose(1, 0, 2).reshape(4, wide)
    gain_mid_one, bias_mid_one = mid_vectors[0:2], mid_vectors[2:4]
    gain_mid_two, bias_mid_two = mid_vectors[4:6], mid_vectors[6:8]

    def maps(values):
        return values.reshape(images, STRIP, values.shape[-1])

    grad_weight = box_weights(box_rows, box_cols, box_count, valid_mask, strip_rows, span_cols)

    first_conv = dot(flat_inputs, weight_reduce_one)
    first_conv, small_all = meet(first_conv, small_all)
    norm_a1 = Norm(first_conv, gain_mid_one[0], bias_mid_one[0])
    tap_weights, partial_offsets, last_rim, first_rim = offset_conv(
        small_all, offset_rows, flat_inputs
    )
    hidden = jax.nn.silu(norm_a1.forward()).astype(bf16).reshape(images, STRIP, mid)
    hidden, rim_above, rim_below = meet(hidden, from_behind(last_rim, 1), from_behind(first_rim, -1))
    half = STRIP // 2
    squashed, positions = sample_positions(partial_offsets, rim_above, rim_below)
    pieces = [
        hidden,
        from_behind(hidden, -1),
        from_behind(hidden, 1),
        from_behind(hidden, -2),
        from_behind(hidden, 2),
        from_behind(hidden[:, :half], -3),
        from_behind(hidden[:, half:], 3),
    ]
    positions, reduce_two_, flat_out_grad, *pieces = meet(
        positions, reduce_two, flat_out_grad, *pieces
    )
    reduce_two_all, spatial_all, expand_two_all = gather(
        [reduce_two_, spatial_two, stacked_columns(expand_two, mid)]
    )
    weight_reduce_two = reduce_two_all.reshape(wide, mid)
    weight_spatial_two = spatial_all.reshape(9 * mid, mid)
    weight_expand_two = unstacked_columns(expand_two_all, wide)
    sampled = sample(positions, pieces).reshape(pixels, 9 * mid)
    norm_a2 = Norm(dot(sampled, weight_deform_one), gain_mid_one[1], bias_mid_one[1])
    hidden_two = jax.nn.silu(norm_a2.forward()).astype(bf16).reshape(pixels, mid)
    norm_a3 = Norm(dot(hidden_two, weight_expand_one), wide_vectors[0], wide_vectors[1])
    joined_one = norm_a3.forward() + per_batch(flat_inputs).astype(f32)
    middle = jax.nn.silu(joined_one).astype(bf16).reshape(pixels, wide)

    norm_b1 = Norm(dot(middle, weight_reduce_two), gain_mid_two[0], bias_mid_two[0])
    inner_one = maps(jax.nn.silu(norm_b1.forward()).astype(bf16))
    fifth_conv, inner_slabs = conv(
        from_behind(inner_one[:, STRIP - COLS :], 1),
        inner_one,
        from_behind(inner_one[:, :COLS], -1),
        weight_spatial_two,
    )
    norm_b2 = Norm(fifth_conv.reshape(pixels, mid), gain_mid_two[1], bias_mid_two[1])
    inner_two = jax.nn.silu(norm_b2.forward()).astype(bf16).reshape(pixels, mid)
    norm_b3 = Norm(dot(inner_two, weight_expand_two), wide_vectors[2], wide_vectors[3])
    joined_two = norm_b3.forward() + per_batch(middle).astype(f32)
    block_out = jax.nn.silu(joined_two).astype(bf16).reshape(images_in.shape)

    upstream = per_batch(flat_out_grad).astype(f32) * grad_weight.reshape(MB, pixels // MB, 1)
    masked_six = upstream * silu_slope(joined_two)
    back_sixth = norm_b3.backward(masked_six)
    grad_expand_two = dot_tn(inner_two, back_sixth).astype(bf16)
    back_fifth = norm_b2.backward(
        per_batch(dot_nt(back_sixth, weight_expand_two)) * silu_slope(norm_b2.forward())
    )
    grad_spatial_two = dot_tn(inner_slabs.reshape(pixels, 9 * mid), back_fifth).astype(bf16)
    def chunked(grad):
        return grad.reshape(count, -1, mid)

    def chunked_columns(grad):
        return [part.reshape(count, -1, mid) for part in jnp.split(grad, grad.shape[1] // mid, axis=1)]

    def unchunked_columns(shard):
        return jnp.concatenate(jnp.split(shard, wide // mid, axis=0), axis=1)

    def split_rows(shard, sizes):
        results = []
        start = 0
        for size in sizes:
            results.append(shard[start : start + size])
            start += size
        return results

    column_rows = expand_two.shape[0] * wide // mid
    spatial_chunks = chunked(grad_spatial_two)
    cut = spatial_two.shape[0] * 7 // 9
    two_left = Scatter([spatial_chunks[:, :cut]], (1, 2, 4, 8, 16))
    two_right = Scatter(
        [spatial_chunks[:, cut:]] + chunked_columns(grad_expand_two), (1, 4, 2, 8, 16)
    )

    def beside_steps(value, *scatters):
        for scatter in scatters:
            scatter.step()
        value, *sums = meet(value, *[scatter.value for scatter in scatters])
        for scatter, total in zip(scatters, sums):
            scatter.value = total
        return value

    back_fifth = beside_steps(back_fifth, two_left, two_right)
    back_maps = maps(back_fifth)
    back_inner = conv_back(
        from_behind(back_maps[:, STRIP - COLS :], 1),
        back_maps,
        from_behind(back_maps[:, :COLS], -1),
        weight_spatial_two,
    ).reshape(pixels, mid)
    back_fourth = norm_b1.backward(per_batch(back_inner) * silu_slope(norm_b1.forward()))
    back_fourth = beside_steps(back_fourth, two_left, two_right)
    grad_reduce_two = dot_tn(middle, back_fourth).astype(bf16)

    back_middle = masked_six + per_batch(dot_nt(back_fourth, weight_reduce_two))
    masked_three = back_middle * silu_slope(joined_one)
    back_third = norm_a3.backward(masked_three)
    back_third = beside_steps(back_third, two_left, two_right)
    grad_expand_one = dot_tn(hidden_two, back_third).astype(bf16)
    back_second = norm_a2.backward(
        per_batch(dot_nt(back_third, weight_expand_one)) * silu_slope(norm_a2.forward())
    )
    back_second = beside_steps(back_second, two_left, two_right)
    grad_deform_one = dot_tn(sampled, back_second).astype(bf16)
    one_left = Scatter([chunked(grad_deform_one)], (1, 2, 4, 8, 16))
    one_right = Scatter(
        chunked_columns(grad_expand_one) + [chunked(grad_reduce_two)], (1, 4, 2, 8, 16)
    )
    back_second, one_left.value, one_right.value = meet(
        back_second, one_left.value, one_right.value
    )
    back_sampled = dot_nt(back_second, weight_deform_one).astype(bf16).reshape(images, STRIP, -1)
    back_sampled = beside_steps(back_sampled, one_left, one_right, two_left, two_right)

    def returned(upstream, first):
        own, *others, position_grad = sample_back(
            positions, pieces, upstream, first, images // MB
        )
        half_sum = jnp.concatenate([from_behind(others[4], 3), from_behind(others[5], -3)], axis=1)
        own = (
            own
            + from_behind(others[0], 1).astype(f32)
            + from_behind(others[1], -1).astype(f32)
            + from_behind(others[2], 2).astype(f32)
            + from_behind(others[3], -2).astype(f32)
            + half_sum.astype(f32)
        )
        return own, position_grad

    backs = [returned(back_sampled, 0)]
    back_sampled = beside_steps(back_sampled, one_left, one_right)
    backs.append(returned(back_sampled, images // MB))
    own = jnp.concatenate([pair[0] for pair in backs], axis=0)
    own = beside_steps(own, one_left, one_right)
    position_grad = jnp.concatenate([pair[1] for pair in backs], axis=0)
    back_offsets, last_rim, first_rim = offset_slope(position_grad, squashed)
    stacked, offset_chunks = offset_back(
        back_offsets,
        from_behind(last_rim, 1),
        from_behind(first_rim, -1),
        flat_inputs,
        count,
        offset_rows,
        mid,
    )
    offset_to_images = dot_tn(stacked, tap_weights)

    back_first = norm_a1.backward(
        per_batch(own.reshape(pixels, mid)) * silu_slope(norm_a1.forward())
    )
    offset_sum = Scatter([offset_chunks], (1, 4, 2, 8, 16))
    back_first = beside_steps(back_first, one_left, one_right, offset_sum)
    grad_reduce_one = dot_tn(flat_inputs, back_first).astype(bf16)
    half_rows = reduce_one.shape[0] // 2
    last_chunks = chunked(grad_reduce_one)
    last_left = Scatter([last_chunks[:, :half_rows]], (1, 2, 4, 8, 16))
    last_right = Scatter([last_chunks[:, half_rows:]], (1, 4, 2, 8, 16))
    back_first = beside_steps(back_first, last_left, last_right)
    grad_images = (
        masked_three.reshape(pixels, wide)
        + dot_nt(back_first, weight_reduce_one)
        + offset_to_images
    )
    grad_images = beside_steps(grad_images, last_left, last_right).reshape(images_in.shape)
    reduce_shard = jnp.concatenate([last_left.finish(), last_right.finish()], axis=0)
    offset_shard = offset_unstack(offset_sum.finish(), offset_rows)
    deform_shard = one_left.finish()
    expand_shard, reduce_two_shard = split_rows(
        one_right.finish(), [column_rows, reduce_two.shape[0]]
    )
    two_rest, expand_two_shard = split_rows(
        two_right.finish(), [spatial_two.shape[0] - cut, column_rows]
    )
    spatial_shard = jnp.concatenate([two_left.finish(), two_rest], axis=0)

    me = lax.axis_index(BOTH)
    mid_grads = jnp.stack(
        [
            norm_a1.gain_grad,
            norm_a2.gain_grad,
            norm_a1.bias_grad,
            norm_a2.bias_grad,
            norm_b1.gain_grad,
            norm_b2.gain_grad,
            norm_b1.bias_grad,
            norm_b2.bias_grad,
        ]
    )
    mid_grads = lax.dynamic_slice_in_dim(mid_grads, me * mid_part, mid_part, 1)
    wide_grads = jnp.stack(
        [norm_a3.gain_grad, norm_a3.bias_grad, norm_b3.gain_grad, norm_b3.bias_grad]
    )
    wide_grads = lax.dynamic_slice_in_dim(wide_grads, me * wide_part, wide_part, 1)
    return (
        block_out,
        grad_images,
        reduce_shard,
        offset_shard,
        deform_shard,
        unchunked_columns(expand_shard),
        mid_grads[0:2],
        mid_grads[2:4],
        wide_grads[0],
        wide_grads[1],
        reduce_two_shard,
        spatial_shard,
        unchunked_columns(expand_two_shard),
        mid_grads[4:6],
        mid_grads[6:8],
        wide_grads[2],
        wide_grads[3],
    )


def solution(mesh):
    whole = P(BOTH, None)
    part = P(None, BOTH)
    line = P(BOTH)
    maps = P("img", "rows", None, None)
    return jax.shard_map(
        on_device,
        mesh=mesh,
        in_specs=(
            maps,
            maps,
            P("img", None, None),
            P("img", None, None),
            P("img"),
            P("img", "rows", None),
            whole,
            whole,
            whole,
            whole,
            part,
            part,
            line,
            line,
            whole,
            whole,
            whole,
            part,
            part,
            line,
            line,
        ),
        out_specs=(
            maps,
            maps,
            whole,
            whole,
            whole,
            whole,
            part,
            part,
            line,
            line,
            whole,
            whole,
            whole,
            part,
            part,
            line,
            line,
        ),
        check_vma=False,
    )
```

```python
from functools import partial

import jax
import jax.numpy as jnp
from jax import lax
from jax.experimental import pallas as pl
from jax.experimental.pallas import tpu as pltpu
from jax.sharding import PartitionSpec as P

CLIP = 8
HALO = 10
MB = 2
BOTH = ("rows", "img")
MIB = 2**20

epsilon = 1e-05
exact = lax.Precision.HIGHEST
f32 = jnp.float32
bf16 = jnp.bfloat16

STRIP_ROWS = 4
COLS = 44
STRIP = STRIP_ROWS * COLS
QUERIES = 9 * STRIP
LANES = 1664
CELLS = (STRIP_ROWS + 2 * HALO) * COLS
ROW_ORDER = (10, 11, 12, 13, 14, 15, 16, 17, 6, 7, 8, 9, 18, 19, 20, 21, 2, 3, 4, 5, 22, 23, 0, 1)


SMALL = pl.CostEstimate(flops=1, bytes_accessed=1, transcendentals=0)


def dot(left, right):
    return jnp.dot(left, right, preferred_element_type=f32)


def dot_nt(left, right):
    return lax.dot_general(left, right, (((1,), (1,)), ((), ())), preferred_element_type=f32)


def dot_tn(left, right):
    return lax.dot_general(left, right, (((0,), (0,)), ((), ())), preferred_element_type=f32)


def device_count():
    return lax.axis_size(BOTH)


def exchange(value, mask):
    return lax.ppermute(value, BOTH, [(i, i ^ mask) for i in range(device_count())])


def all_sum(value):
    count = device_count()
    bit = 1
    while bit < count:
        masks = [bit, 2 * bit, 3 * bit] if 2 * bit < count else [bit]
        parts = [exchange(value, mask) for mask in masks]
        for part in parts:
            value = value + part
        bit *= 4
    return value


def bits_of(order):
    bits = [1 << k for k in range(device_count().bit_length() - 1)]
    return [b for b in order if b in bits] + [b for b in bits if b not in order]


def tie(value, *others):
    return lax.optimization_barrier((value,) + others)[0]


def meet(*values):
    return lax.optimization_barrier(values)


class Scatter:
    def __init__(self, pieces, order):
        self.order = bits_of(order)
        bits = sorted(self.order, reverse=True)
        count = len(bits)
        axes = [bits.index(b) for b in self.order] + [count, count + 1]
        self.value = jnp.concatenate(
            [piece.reshape((2,) * count + piece.shape[1:]).transpose(axes) for piece in pieces],
            axis=-2,
        )

    def step(self):
        bit = self.order.pop(0)
        mine = (lax.axis_index(BOTH) // bit) % 2
        keep = lax.dynamic_index_in_dim(self.value, mine, 0, keepdims=False)
        send = lax.dynamic_index_in_dim(self.value, 1 - mine, 0, keepdims=False)
        total = keep.astype(f32) + exchange(send, bit).astype(f32)
        self.value = total.astype(bf16) if self.order else total
        return self.value

    def finish(self):
        while self.order:
            self.step()
        return self.value


def scatter_chips(scatter):
    count = device_count()
    groups = [[i for i in range(count) if i % 2 == side] for side in range(2)]
    value = scatter.value
    return lax.psum_scatter(
        value.reshape(-1, value.shape[-1]),
        BOTH,
        scatter_dimension=0,
        axis_index_groups=groups,
        tiled=True,
    ).astype(f32)


class Gather:
    def __init__(self, piece, groups):
        bits = bits_of(())
        self.groups = [tuple(b for b in group if b in bits) for group in groups]
        self.groups += [(b,) for b in bits if not any(b in group for group in self.groups)]
        self.done = []
        self.piece = piece
        self.value = piece

    def step(self):
        group = self.groups.pop(0)
        by_mask = {0: self.value}
        for bit in group:
            for mask in sub_masks(group, bit):
                by_mask[bit + mask] = exchange(self.value, bit + mask)
        for bit in group:
            mine = (lax.axis_index(BOTH) // bit) % 2 == 1
            self.done = sorted(self.done + [bit], reverse=True)
            axis = self.done.index(bit)
            merged = {}
            for mask, part in by_mask.items():
                if not mask & bit:
                    other = by_mask[mask + bit]
                    merged[mask] = jnp.stack(
                        [jnp.where(mine, other, part), jnp.where(mine, part, other)], axis=axis
                    )
            by_mask = merged
        (self.value,) = by_mask.values()

    def result(self):
        return self.value.reshape((-1,) + self.piece.shape)


def sub_masks(group, bit):
    masks = [0]
    for other in group[: group.index(bit)]:
        masks = masks + [mask + other for mask in masks]
    return masks


def from_behind(value, steps):
    count = lax.axis_size("rows")
    first, last = (max(0, -steps), min(count, count - steps))
    return lax.ppermute(value, "rows", [(source, source + steps) for source in range(first, last)])


def spline(values):
    magnitude = jnp.abs(values)
    outer = 1.5 - magnitude
    return jnp.where(
        magnitude < 0.5,
        0.75 - values * values,
        jnp.where(magnitude < 1.5, 0.5 * outer * outer, 0.0),
    )


def spline_slope(values):
    magnitude = jnp.abs(values)
    outer = 1.5 - magnitude
    return jnp.where(
        magnitude < 0.5,
        -2.0 * values,
        jnp.where(magnitude < 1.5, jnp.where(values > 0, -outer, outer), 0.0),
    )


def fill_factors(pos_ref, row_ref, col_weight, row_weight, col_slope=None, row_slope=None):
    cell_cols = lax.broadcasted_iota(jnp.int32, (2 * COLS, LANES), 0)
    cell_cols = jnp.where(cell_cols >= COLS, cell_cols - COLS, cell_cols).astype(f32)
    col_gap = pos_ref[0, 1:2, :] - cell_cols
    row_gap = pos_ref[0, 0:1, :] - row_ref[...]
    col_weight[...] = spline(col_gap)
    row_weight[...] = spline(row_gap)
    if col_slope is not None:
        col_slope[...] = spline_slope(col_gap)
        row_slope[...] = spline_slope(row_gap)


def fill_sampler(col_weight, row_weight, sampler):
    low = lax.broadcasted_iota(jnp.int32, (8, 128), 0) < 4

    def body(tile, carry):
        lanes = pl.ds(pl.multiple_of(tile * 128, 128), 128)
        for block in range(6):
            for chunk in range(11):
                halves = []
                for group in (2 * chunk, 2 * chunk + 1):
                    first, last = (8 * group) // COLS, (8 * group + 7) // COLS
                    weight = row_weight[4 * block + first : 4 * block + first + 1, lanes]
                    if first != last:
                        weight = jnp.where(
                            low, weight, row_weight[4 * block + last : 4 * block + last + 1, lanes]
                        )
                    local = group % 11
                    halves.append(col_weight[8 * local : 8 * local + 8, lanes] * weight)
                start = block * STRIP + 16 * chunk
                sampler[start : start + 16, lanes] = jnp.concatenate(halves, axis=0).astype(bf16)
        return carry

    lax.fori_loop(0, LANES // 128, body, 0)


def fill_window(pieces, window):
    for index, piece in enumerate(pieces[:5]):
        window[index * STRIP : (index + 1) * STRIP, :] = piece[0]
    window[5 * STRIP : 6 * STRIP, :] = jnp.concatenate([pieces[5][0], pieces[6][0]], axis=0)


def sample_kernel(pos_ref, row_ref, *refs):
    pieces, out_ref = refs[:7], refs[7]
    col_weight, row_weight, sampler, window = refs[8:]
    fill_factors(pos_ref, row_ref, col_weight, row_weight)
    fill_sampler(col_weight, row_weight, sampler)
    fill_window(pieces, window)
    result = dot_tn(window[...], sampler[...]).T.astype(bf16)
    width = window.shape[1]
    for tap in range(9):
        out_ref[0, :, tap * width : (tap + 1) * width] = result[tap * STRIP : (tap + 1) * STRIP]


def sample_back_kernel(pos_ref, row_ref, *refs):
    pieces, upstream_ref = refs[:7], refs[7]
    grads, pos_grad = refs[8:15], refs[15]
    (
        col_weight,
        row_weight,
        col_slope,
        row_slope,
        sampler,
        window,
        upstream,
        sampler_grad,
    ) = refs[16:]
    fill_factors(pos_ref, row_ref, col_weight, row_weight, col_slope, row_slope)
    fill_sampler(col_weight, row_weight, sampler)
    fill_window(pieces, window)
    width = window.shape[1]
    for tap in range(9):
        upstream[tap * STRIP : (tap + 1) * STRIP, :] = upstream_ref[
            0, :, tap * width : (tap + 1) * width
        ]
    upstream[QUERIES:LANES, :] = jnp.zeros((LANES - QUERIES, width), bf16)
    sampler_grad[...] = dot_nt(window[...], upstream[...])
    for index, grad in enumerate(grads[:5]):
        grad[0] = dot(sampler[index * STRIP : (index + 1) * STRIP, :], upstream[...]).astype(
            grad.dtype
        )
    last = dot(sampler[5 * STRIP :, :], upstream[...])
    grads[5][0] = last[: STRIP // 2].astype(bf16)
    grads[6][0] = last[STRIP // 2 :].astype(bf16)
    low = lax.broadcasted_iota(jnp.int32, (8, 128), 0) < 4

    def body(tile, carry):
        lanes = pl.ds(pl.multiple_of(tile * 128, 128), 128)
        zero = jnp.zeros((8, 128), f32)
        weights = [col_weight[8 * group : 8 * group + 8, lanes] for group in range(11)]
        middle_low = jnp.where(low, weights[5], 0.0)
        middle_high = jnp.where(low, 0.0, weights[5])
        row_total = zero
        col_totals = [zero] * 11
        for pair in range(12):
            first = row_weight[2 * pair : 2 * pair + 1, lanes]
            second = row_weight[2 * pair + 1 : 2 * pair + 2, lanes]
            mixed = jnp.where(low, first, second)
            first_sum = zero
            second_sum = zero
            for group in range(11):
                start = 88 * pair + 8 * group
                value = sampler_grad[start : start + 8, lanes]
                if group < 5:
                    first_sum = first_sum + value * weights[group]
                    col_totals[group] = col_totals[group] + value * first
                elif group > 5:
                    second_sum = second_sum + value * weights[group]
                    col_totals[group] = col_totals[group] + value * second
                else:
                    first_sum = first_sum + value * middle_low
                    second_sum = second_sum + value * middle_high
                    col_totals[group] = col_totals[group] + value * mixed
            row_total = (
                row_total
                + first_sum * row_slope[2 * pair : 2 * pair + 1, lanes]
                + second_sum * row_slope[2 * pair + 1 : 2 * pair + 2, lanes]
            )
        col_total = zero
        for group in range(11):
            col_total = col_total + col_totals[group] * col_slope[8 * group : 8 * group + 8, lanes]
        pos_grad[0, 0:1, lanes] = jnp.sum(row_total, axis=0, keepdims=True)
        pos_grad[0, 1:2, lanes] = jnp.sum(col_total, axis=0, keepdims=True)
        return carry

    lax.fori_loop(0, LANES // 128, body, 0)


def piece_specs(width, first=0):
    full = pl.BlockSpec((1, STRIP, width), lambda i: (i + first, 0, 0))
    half = pl.BlockSpec((1, STRIP // 2, width), lambda i: (i + first, 0, 0))
    return [full] * 5 + [half] * 2


def sampler_specs(width, first=0):
    return [
        pl.BlockSpec((1, 2, LANES), lambda i: (i + first, 0, 0)),
        pl.BlockSpec((len(ROW_ORDER), 1), lambda i: (0, 0)),
    ] + piece_specs(width, first)


def row_ids():
    return jnp.array(ROW_ORDER, f32)[:, None]


def sample(positions, pieces):
    images, _, width = pieces[0].shape
    return pl.pallas_call(
        sample_kernel,
        grid=(images,),
        in_specs=sampler_specs(width),
        out_specs=pl.BlockSpec((1, STRIP, 9 * width), lambda i: (i, 0, 0)),
        out_shape=jax.ShapeDtypeStruct((images, STRIP, 9 * width), bf16),
        scratch_shapes=[
            pltpu.VMEM((2 * COLS, LANES), f32),
            pltpu.VMEM((len(ROW_ORDER), LANES), f32),
            pltpu.VMEM((CELLS, LANES), bf16),
            pltpu.VMEM((CELLS, width), bf16),
        ],
        compiler_params=pltpu.CompilerParams(vmem_limit_bytes=60 * MIB),
        cost_estimate=SMALL,
        name="sample",
    )(positions, row_ids(), *pieces)


def sample_back(positions, pieces, upstream, first, images):
    width = pieces[0].shape[2]
    full = (images, STRIP, width)
    half = (images, STRIP // 2, width)
    return pl.pallas_call(
        sample_back_kernel,
        grid=(images,),
        in_specs=sampler_specs(width, first)
        + [pl.BlockSpec((1, STRIP, 9 * width), lambda i: (i + first, 0, 0))],
        out_specs=piece_specs(width) + [pl.BlockSpec((1, 2, LANES), lambda i: (i, 0, 0))],
        out_shape=[jax.ShapeDtypeStruct(full, f32)]
        + [jax.ShapeDtypeStruct(full, bf16)] * 4
        + [jax.ShapeDtypeStruct(half, bf16)] * 2
        + [jax.ShapeDtypeStruct((images, 2, LANES), f32)],
        scratch_shapes=[
            pltpu.VMEM((2 * COLS, LANES), f32),
            pltpu.VMEM((len(ROW_ORDER), LANES), f32),
            pltpu.VMEM((2 * COLS, LANES), f32),
            pltpu.VMEM((len(ROW_ORDER), LANES), f32),
            pltpu.VMEM((CELLS, LANES), bf16),
            pltpu.VMEM((CELLS, width), bf16),
            pltpu.VMEM((LANES, width), bf16),
            pltpu.VMEM((CELLS, LANES), f32),
        ],
        compiler_params=pltpu.CompilerParams(vmem_limit_bytes=34 * MIB),
        cost_estimate=SMALL,
        name="sample_back",
    )(positions, row_ids(), *pieces, upstream)


def tap_slabs(above, own, below, padded, image):
    padded[8 : 8 + COLS, :] = above[image].astype(f32)
    padded[8 + COLS : 8 + COLS + STRIP, :] = own[image].astype(f32)
    padded[8 + COLS + STRIP : 8 + 2 * COLS + STRIP, :] = below[image].astype(f32)
    cols = lax.broadcasted_iota(jnp.int32, (STRIP, 1), 0) % COLS
    for tap in range(9):
        start = 8 + COLS * (tap // 3) + tap % 3 - 1
        slab = padded[start : start + STRIP, :]
        if tap % 3 == 0:
            slab = jnp.where(cols > 0, slab, 0.0)
        elif tap % 3 == 2:
            slab = jnp.where(cols < COLS - 1, slab, 0.0)
        yield tap, slab.astype(bf16)


def conv_kernel(above, own, below, weight, out_ref, slabs_ref, padded):
    width = own.shape[2]
    images = own.shape[0]
    for image in range(images):
        for tap, slab in tap_slabs(above, own, below, padded, image):
            slabs_ref[image, :, tap * width : (tap + 1) * width] = slab
    total = None
    for tap in range(9):
        lanes = slice(tap * width, (tap + 1) * width)
        part = dot(slabs_ref[:, :, lanes].reshape(images * STRIP, width), weight[lanes, :])
        total = part if total is None else total + part
    out_ref[...] = total.reshape(out_ref.shape)


def conv_back_kernel(above, own, below, weight, out_ref, padded, slabs):
    width = own.shape[2]
    images = own.shape[0]
    for image in range(images):
        for tap, slab in tap_slabs(above, own, below, padded, image):
            slabs[8 - tap, image * STRIP : (image + 1) * STRIP, :] = slab
    total = None
    for tap in range(9):
        part = dot_nt(slabs[tap], weight[tap * width : (tap + 1) * width, :])
        total = part if total is None else total + part
    out_ref[...] = total.reshape(out_ref.shape)


def conv_specs(images, width):
    rim = pl.BlockSpec((images, COLS, width), lambda i: (i, 0, 0))
    own = pl.BlockSpec((images, STRIP, width), lambda i: (i, 0, 0))
    return [rim, own, rim, pl.BlockSpec((9 * width, width), lambda i: (0, 0))]


def conv(above, own, below, weight):
    images, _, width = own.shape
    step = images // MB
    return pl.pallas_call(
        conv_kernel,
        grid=(MB,),
        in_specs=conv_specs(step, width),
        out_specs=[
            pl.BlockSpec((step, STRIP, width), lambda i: (i, 0, 0)),
            pl.BlockSpec((step, STRIP, 9 * width), lambda i: (i, 0, 0)),
        ],
        out_shape=[
            jax.ShapeDtypeStruct((images, STRIP, width), f32),
            jax.ShapeDtypeStruct((images, STRIP, 9 * width), bf16),
        ],
        scratch_shapes=[pltpu.VMEM((16 + 2 * COLS + STRIP, width), f32)],
        compiler_params=pltpu.CompilerParams(vmem_limit_bytes=24 * MIB),
        cost_estimate=SMALL,
        name="conv",
    )(above, own, below, weight)


def conv_back(above, own, below, weight):
    images, _, width = own.shape
    step = images // MB
    return pl.pallas_call(
        conv_back_kernel,
        grid=(MB,),
        in_specs=conv_specs(step, width),
        out_specs=pl.BlockSpec((step, STRIP, width), lambda i: (i, 0, 0)),
        out_shape=jax.ShapeDtypeStruct((images, STRIP, width), f32),
        scratch_shapes=[
            pltpu.VMEM((16 + 2 * COLS + STRIP, width), f32),
            pltpu.VMEM((9, step * STRIP, width), bf16),
        ],
        compiler_params=pltpu.CompilerParams(vmem_limit_bytes=24 * MIB),
        cost_estimate=SMALL,
        name="conv_back",
    )(above, own, below, weight)


TAP = 32


def offset_spans(device, rows, wide):
    spans = []
    start = device * rows
    while start < (device + 1) * rows:
        tap, column = divmod(start, wide)
        size = min((device + 1) * rows - start, wide - column)
        spans.append((tap, column, start - device * rows, size))
        start += size
    return spans


def offset_stack(strip, extra, width):
    rows = strip.shape[-1]
    lead = [(0, 0)] * (strip.ndim - 2)
    strip = jnp.pad(strip, lead + [(0, TAP - 18), (0, 0)])
    full = rows // width * width
    blocks = [strip[..., start : start + width] for start in range(0, full, width)]
    rest = strip[..., full:]
    rest = jnp.concatenate([rest[..., :16, :], rest[..., 16:, :]], axis=-1)
    pad = width - rest.shape[-1] - extra.shape[-1]
    assert pad >= 0
    blocks.append(jnp.pad(jnp.concatenate([rest, extra], axis=-1), lead + [(0, 0), (0, pad)]))
    return jnp.concatenate(blocks, axis=-2)


def spread_rows(values, images, take):
    parts = []
    for image in range(images):
        parts += take(image)
    return jnp.concatenate(parts, axis=1)


def own_lanes(values, image, start):
    first = image * STRIP + start
    return values[:, first : first + STRIP // 2]


def rim_lanes(values, image):
    return values[:, image * STRIP // 2 : (image + 1) * STRIP // 2]


def down_two(own, above, images):
    return spread_rows(own, images, lambda i: [rim_lanes(above, i), own_lanes(own, i, 0)])


def up_two(own, below, images):
    return spread_rows(own, images, lambda i: [own_lanes(own, i, STRIP // 2), rim_lanes(below, i)])


def beside(values, steps):
    if steps == 0:
        return values
    rows, cells = values.shape
    column = lax.broadcasted_iota(jnp.int32, (1, cells), 1) % COLS
    empty = jnp.zeros((rows, abs(steps)), values.dtype)
    if steps > 0:
        moved = jnp.concatenate([values[:, steps:], empty], axis=1)
    else:
        moved = jnp.concatenate([empty, values[:, :steps]], axis=1)
    return jnp.where((column + steps >= 0) & (column + steps < COLS), moved, 0.0)


def offset_conv_kernel(rows, small_ref, input_ref, taps_ref, partial_ref, last_ref, first_ref):
    count, _, width = small_ref.shape
    wide = input_ref.shape[1]
    images = input_ref.shape[0] // STRIP
    full = rows // width
    rest = rows - full * width
    for device in range(count):
        blocks = [small_ref[device, TAP * i : TAP * (i + 1), :] for i in range(full)]
        if rest:
            block = small_ref[device, TAP * full : TAP * full + 16, :]
            blocks.append(
                jnp.concatenate([block[:, :rest], block[:, rest : 2 * rest]], axis=0)
            )
        strip = jnp.concatenate(blocks, axis=1)
        for tap, column, local, size in offset_spans(device, rows, wide):
            taps_ref[TAP * tap : TAP * (tap + 1), column : column + size] = strip[
                :, local : local + size
            ]
    partial = dot_nt(taps_ref[...], input_ref[...])
    partial_ref[...] = partial
    half = STRIP // 2
    for image in range(images):
        lanes = slice(image * half, (image + 1) * half)
        last_ref[:, lanes] = own_lanes(partial[: 3 * TAP], image, half)
        first_ref[:, lanes] = own_lanes(partial[6 * TAP :], image, 0)


def offset_conv(small_all, rows, inputs):
    pixels, wide = inputs.shape
    rim = (3 * TAP, pixels // 2)
    return pl.pallas_call(
        partial(offset_conv_kernel, rows),
        out_shape=[
            jax.ShapeDtypeStruct((9 * TAP, wide), bf16),
            jax.ShapeDtypeStruct((9 * TAP, pixels), f32),
            jax.ShapeDtypeStruct(rim, f32),
            jax.ShapeDtypeStruct(rim, f32),
        ],
        compiler_params=pltpu.CompilerParams(vmem_limit_bytes=24 * MIB),
        name="offset_conv",
    )(small_all, inputs)


def positions_kernel(partial_ref, above_ref, below_ref, squashed_ref, positions_ref):
    images = positions_ref.shape[0]
    rows = [
        down_two(partial_ref[: 3 * TAP, :], above_ref[...], images),
        partial_ref[3 * TAP : 6 * TAP, :],
        up_two(partial_ref[6 * TAP :, :], below_ref[...], images),
    ]
    offsets = None
    for row in rows:
        for col_tap in range(3):
            part = beside(row[TAP * col_tap : TAP * (col_tap + 1)], 2 * (col_tap - 1))
            offsets = part if offsets is None else offsets + part
    squashed = jnp.tanh(offsets / CLIP)
    squashed_ref[...] = squashed
    clipped = CLIP * squashed
    cells = images * STRIP
    lane = lax.broadcasted_iota(jnp.int32, (9, cells), 1) % STRIP
    tap = lax.broadcasted_iota(jnp.int32, (9, cells), 0)
    row_position = clipped[:9] + (tap // 3 - 1 + HALO + lane // COLS).astype(f32)
    col_position = clipped[9:18] + (tap % 3 - 1 + lane % COLS).astype(f32)
    positions_ref[:, :, QUERIES:] = jnp.full((images, 2, LANES - QUERIES), -1000.0, f32)
    for image in range(images):
        lanes = slice(image * STRIP, (image + 1) * STRIP)
        for t in range(9):
            place = slice(t * STRIP, (t + 1) * STRIP)
            positions_ref[image, 0:1, place] = row_position[t : t + 1, lanes]
            positions_ref[image, 1:2, place] = col_position[t : t + 1, lanes]


def sample_positions(partial_offsets, above, below):
    cells = partial_offsets.shape[1]
    return pl.pallas_call(
        positions_kernel,
        out_shape=[
            jax.ShapeDtypeStruct((TAP, cells), f32),
            jax.ShapeDtypeStruct((cells // STRIP, 2, LANES), f32),
        ],
        name="sample_positions",
    )(partial_offsets, above, below)


def offset_slope_kernel(position_grad_ref, squashed_ref, back_ref, last_ref, first_ref, flat):
    images = position_grad_ref.shape[0]
    flat[...] = jnp.zeros_like(flat)
    for image in range(images):
        lanes = slice(image * STRIP, (image + 1) * STRIP)
        for t in range(9):
            place = slice(t * STRIP, (t + 1) * STRIP)
            flat[t : t + 1, lanes] = position_grad_ref[image, 0:1, place]
            flat[9 + t : 10 + t, lanes] = position_grad_ref[image, 1:2, place]
    squashed = squashed_ref[...]
    back = (flat[...] * (1.0 - squashed * squashed)).astype(bf16)
    back_ref[...] = back
    half = STRIP // 2
    wider = back.astype(f32)
    for image in range(images):
        lanes = slice(image * half, (image + 1) * half)
        last_ref[:, lanes] = own_lanes(wider, image, half).astype(bf16)
        first_ref[:, lanes] = own_lanes(wider, image, 0).astype(bf16)


def offset_slope(position_grad, squashed):
    cells = squashed.shape[1]
    rim = jax.ShapeDtypeStruct((TAP, cells // 2), bf16)
    return pl.pallas_call(
        offset_slope_kernel,
        out_shape=[jax.ShapeDtypeStruct((TAP, cells), bf16), rim, rim],
        scratch_shapes=[pltpu.VMEM((TAP, cells), f32)],
        name="offset_slope",
    )(position_grad, squashed)


def offset_back_kernel(rows, back_ref, above_ref, below_ref, input_ref, stacked_ref, chunks_ref):
    count, _, width = chunks_ref.shape
    wide = input_ref.shape[1]
    images = input_ref.shape[0] // STRIP
    own = back_ref[...].astype(f32)
    by_row = [
        up_two(own, below_ref[...].astype(f32), images),
        own,
        down_two(own, above_ref[...].astype(f32), images),
    ]
    for tap in range(9):
        moved = beside(by_row[tap // 3], -2 * (tap % 3 - 1))
        stacked_ref[TAP * tap : TAP * (tap + 1), :] = moved.astype(bf16)
    grad = dot(stacked_ref[...], input_ref[...])
    full = rows // width
    rest = rows - full * width
    chunks_ref[...] = jnp.zeros(chunks_ref.shape, bf16)
    for device in range(count):
        strip = jnp.concatenate(
            [
                grad[TAP * tap : TAP * (tap + 1), column : column + size]
                for tap, column, _, size in offset_spans(device, rows, wide)
            ],
            axis=1,
        ).astype(bf16)
        for i in range(full):
            chunks_ref[device, TAP * i : TAP * (i + 1), :] = strip[:, width * i : width * (i + 1)]
        if rest:
            tail = strip[:, width * full :]
            chunks_ref[device, TAP * full :, : 2 * rest] = jnp.concatenate(
                [tail[:16], tail[16:]], axis=1
            )


def offset_back(back, above, below, inputs, count, rows, width):
    pixels, wide = inputs.shape
    stack_rows = rows // width * TAP + (16 if rows % width else 0)
    return pl.pallas_call(
        partial(offset_back_kernel, rows),
        out_shape=[
            jax.ShapeDtypeStruct((9 * TAP, pixels), bf16),
            jax.ShapeDtypeStruct((count, stack_rows, width), bf16),
        ],
        compiler_params=pltpu.CompilerParams(vmem_limit_bytes=24 * MIB),
        name="offset_back",
    )(back, above, below, inputs)


def offset_unstack(shard, rows):
    width = shard.shape[1]
    full = rows // width
    rest = rows - full * width
    blocks = [shard[TAP * i : TAP * i + 18] for i in range(full)]
    if rest:
        tail = shard[TAP * full :]
        blocks.append(jnp.concatenate([tail[:, :rest], tail[:2, rest : 2 * rest]], axis=0))
    return jnp.concatenate(blocks, axis=1).T


def silu_slope(values):
    logistic = jax.nn.sigmoid(values)
    return logistic * (1.0 + values * (1.0 - logistic))


def box_weights(box_rows, box_cols, box_count, valid_mask, strip_rows, span_cols):
    row_ids_ = lax.axis_index("rows") * strip_rows + jnp.arange(strip_rows)
    col_ids = jnp.arange(span_cols)
    row_low = jnp.minimum(box_rows[..., 0], box_rows[..., 1])
    row_high = jnp.maximum(box_rows[..., 0], box_rows[..., 1])
    col_low = jnp.minimum(box_cols[..., 0], box_cols[..., 1])
    col_high = jnp.maximum(box_cols[..., 0], box_cols[..., 1])
    inside_rows = ((row_ids_ >= row_low[..., None]) & (row_ids_ <= row_high[..., None])).astype(f32)
    inside_cols = ((col_ids >= col_low[..., None]) & (col_ids <= col_high[..., None])).astype(f32)
    live_boxes = (jnp.arange(box_rows.shape[1])[None, :] < box_count[:, None]).astype(f32)
    covered = jnp.einsum("ib,ibh,ibw->ihw", live_boxes, inside_rows, inside_cols, precision=exact)
    return valid_mask.astype(f32) * (0.5 + covered / box_count.astype(f32)[:, None, None])


def per_batch(values):
    return values.reshape(MB, values.shape[0] // MB, values.shape[1])


def batch_totals(first, second):
    totals = all_sum(jnp.concatenate([jnp.sum(first, axis=1), jnp.sum(second, axis=1)], axis=0))
    return totals[:MB], totals[MB:]


class Norm:
    def __init__(self, values, gain, bias):
        values = per_batch(values)
        self.count = values.shape[1] * device_count()
        sums, squares = batch_totals(values, values * values)
        self.values = values
        self.center = (sums / self.count)[:, None, :]
        self.spread = lax.rsqrt(squares[:, None, :] / self.count - self.center * self.center + epsilon)
        self.gain = gain.astype(f32)
        self.bias = bias.astype(f32)

    def normed(self):
        return (self.values - self.center) * self.spread

    def forward(self):
        return self.normed() * self.gain + self.bias

    def backward(self, upstream):
        normed = self.normed()
        bias_sums, gain_sums = batch_totals(upstream, upstream * normed)
        self.gain_grad = jnp.sum(gain_sums, axis=0)
        self.bias_grad = jnp.sum(bias_sums, axis=0)
        result = (self.spread * self.gain) * (
            upstream
            - (bias_sums / self.count)[:, None, :]
            - normed * (gain_sums / self.count)[:, None, :]
        )
        return result.astype(bf16).reshape(-1, result.shape[-1])


def stacked_columns(weight, width):
    return jnp.concatenate(jnp.split(weight, weight.shape[1] // width, axis=1), axis=0)


def unstacked_columns(blocks, columns):
    width = blocks.shape[2]
    parts = jnp.split(blocks, columns // width, axis=1)
    return jnp.concatenate([part.reshape(-1, width) for part in parts], axis=1)


def gather(pieces):
    whole = lax.all_gather(jnp.concatenate(pieces, axis=0), BOTH, axis=0)
    results = []
    start = 0
    for piece in pieces:
        results.append(whole[:, start : start + piece.shape[0]])
        start += piece.shape[0]
    return results


def to_width(flat, width):
    rows = -(-flat.shape[-1] // width)
    pad = rows * width - flat.shape[-1]
    return jnp.pad(flat, [(0, 0)] * (flat.ndim - 1) + [(0, pad)]).reshape(
        flat.shape[:-1] + (rows, width)
    )


def widths(values, width):
    pieces = []
    for start in range(0, values.shape[-1], width):
        piece = values[..., start : start + width]
        pad = width - piece.shape[-1]
        pieces.append(jnp.pad(piece, [(0, 0)] * (values.ndim - 1) + [(0, pad)]))
    return pieces


def shifted(values, steps, columns):
    if steps == 0:
        return values
    cells = values.shape[-1]
    column = jnp.arange(cells) % columns
    pad = [(0, 0)] * (values.ndim - 1)
    if steps > 0:
        moved = jnp.pad(values[..., steps:], pad + [(0, steps)])
    else:
        moved = jnp.pad(values[..., :steps], pad + [(-steps, 0)])
    return jnp.where((column + steps >= 0) & (column + steps < columns), moved, 0)


def on_device(
    images_in,
    out_grad,
    box_rows,
    box_cols,
    box_count,
    valid_mask,
    reduce_one,
    offset_one,
    deform_one,
    expand_one,
    mid_gain_one,
    mid_bias_one,
    wide_gain_one,
    wide_bias_one,
    reduce_two,
    spatial_two,
    expand_two,
    mid_gain_two,
    mid_bias_two,
    wide_gain_two,
    wide_bias_two,
):
    images, strip_rows, span_cols, wide = images_in.shape
    mid = reduce_one.shape[1]
    assert strip_rows == STRIP_ROWS and span_cols == COLS
    count = device_count()
    pixels = images * STRIP

    mid_part = mid // count
    wide_part = wide // count
    extent = max(mid_part, wide_part)
    mid_rows = jnp.concatenate([mid_gain_one, mid_bias_one, mid_gain_two, mid_bias_two], axis=0)
    wide_rows = jnp.concatenate(
        [v[None] for v in (wide_gain_one, wide_bias_one, wide_gain_two, wide_bias_two)], axis=0
    )
    vectors = jnp.pad(mid_rows, ((0, 8), (0, extent - mid_part))) + jnp.pad(
        wide_rows, ((8, 4), (0, extent - wide_part))
    )
    offset_rows = offset_one.shape[0]
    small = offset_stack(offset_one.T, vectors, mid)
    flat_inputs = images_in.reshape(pixels, wide)
    flat_out_grad = out_grad.reshape(pixels, wide)
    reduce_gather = Gather(reduce_one, ((8, 16), (4,), (2,), (1,)))
    small_gather = Gather(small, ((8, 16), (2,), (4,), (1,)))
    while reduce_gather.groups:
        reduce_gather.step()
        small_gather.step()
        if len(reduce_gather.groups) == 1:
            reduce_gather.value, small_gather.value, flat_inputs = meet(
                reduce_gather.value, small_gather.value, flat_inputs
            )
        else:
            reduce_gather.value, small_gather.value = meet(reduce_gather.value, small_gather.value)
    reduce_all, small_all = reduce_gather.result(), small_gather.result()
    deform_all, expand_all = gather([deform_one, stacked_columns(expand_one, mid)])
    weight_reduce_one = reduce_all.reshape(wide, mid)
    weight_deform_one = deform_all.reshape(9 * mid, mid)
    weight_expand_one = unstacked_columns(expand_all, wide)
    vector_start = 2 * (offset_rows % mid)
    vector_all = small_all[:, small.shape[0] - 16 :, vector_start : vector_start + extent]
    mid_vectors = vector_all[:, :8, :mid_part].transpose(1, 0, 2).reshape(8, mid)
    wide_vectors = vector_all[:, 8:12, :wide_part].transpose(1, 0, 2).reshape(4, wide)
    gain_mid_one, bias_mid_one = mid_vectors[0:2], mid_vectors[2:4]
    gain_mid_two, bias_mid_two = mid_vectors[4:6], mid_vectors[6:8]

    def maps(values):
        return values.reshape(images, STRIP, values.shape[-1])

    grad_weight = box_weights(box_rows, box_cols, box_count, valid_mask, strip_rows, span_cols)

    first_conv = dot(flat_inputs, weight_reduce_one)
    first_conv, small_all = meet(first_conv, small_all)
    norm_a1 = Norm(first_conv, gain_mid_one[0], bias_mid_one[0])
    tap_weights, partial_offsets, last_rim, first_rim = offset_conv(
        small_all, offset_rows, flat_inputs
    )
    hidden = jax.nn.silu(norm_a1.forward()).astype(bf16).reshape(images, STRIP, mid)
    hidden, rim_above, rim_below = meet(hidden, from_behind(last_rim, 1), from_behind(first_rim, -1))
    half = STRIP // 2
    squashed, positions = sample_positions(partial_offsets, rim_above, rim_below)
    pieces = [
        hidden,
        from_behind(hidden, -1),
        from_behind(hidden, 1),
        from_behind(hidden, -2),
        from_behind(hidden, 2),
        from_behind(hidden[:, :half], -3),
        from_behind(hidden[:, half:], 3),
    ]
    positions, flat_out_grad, reduce_two, spatial_two, expand_two, *pieces = meet(
        positions, flat_out_grad, reduce_two, spatial_two, expand_two, *pieces
    )
    reduce_two_all, spatial_all, expand_two_all = gather(
        [reduce_two, spatial_two, stacked_columns(expand_two, mid)]
    )
    weight_reduce_two = reduce_two_all.reshape(wide, mid)
    weight_spatial_two = spatial_all.reshape(9 * mid, mid)
    weight_expand_two = unstacked_columns(expand_two_all, wide)
    sampled = sample(positions, pieces).reshape(pixels, 9 * mid)
    norm_a2 = Norm(dot(sampled, weight_deform_one), gain_mid_one[1], bias_mid_one[1])
    hidden_two = jax.nn.silu(norm_a2.forward()).astype(bf16).reshape(pixels, mid)
    norm_a3 = Norm(dot(hidden_two, weight_expand_one), wide_vectors[0], wide_vectors[1])
    joined_one = norm_a3.forward() + per_batch(flat_inputs).astype(f32)
    middle = jax.nn.silu(joined_one).astype(bf16).reshape(pixels, wide)

    norm_b1 = Norm(dot(middle, weight_reduce_two), gain_mid_two[0], bias_mid_two[0])
    inner_one = maps(jax.nn.silu(norm_b1.forward()).astype(bf16))
    fifth_conv, inner_slabs = conv(
        from_behind(inner_one[:, STRIP - COLS :], 1),
        inner_one,
        from_behind(inner_one[:, :COLS], -1),
        weight_spatial_two,
    )
    norm_b2 = Norm(fifth_conv.reshape(pixels, mid), gain_mid_two[1], bias_mid_two[1])
    inner_two = jax.nn.silu(norm_b2.forward()).astype(bf16).reshape(pixels, mid)
    norm_b3 = Norm(dot(inner_two, weight_expand_two), wide_vectors[2], wide_vectors[3])
    joined_two = norm_b3.forward() + per_batch(middle).astype(f32)
    block_out = jax.nn.silu(joined_two).astype(bf16).reshape(images_in.shape)

    upstream = per_batch(flat_out_grad).astype(f32) * grad_weight.reshape(MB, pixels // MB, 1)
    masked_six = upstream * silu_slope(joined_two)
    back_sixth = norm_b3.backward(masked_six)
    grad_expand_two = dot_tn(inner_two, back_sixth).astype(bf16)
    back_fifth = norm_b2.backward(
        per_batch(dot_nt(back_sixth, weight_expand_two)) * silu_slope(norm_b2.forward())
    )
    grad_spatial_two = dot_tn(inner_slabs.reshape(pixels, 9 * mid), back_fifth).astype(bf16)
    def chunked(grad):
        return grad.reshape(count, -1, mid)

    def chunked_columns(grad):
        return [part.reshape(count, -1, mid) for part in jnp.split(grad, grad.shape[1] // mid, axis=1)]

    def unchunked_columns(shard):
        return jnp.concatenate(jnp.split(shard, wide // mid, axis=0), axis=1)

    def split_rows(shard, sizes):
        results = []
        start = 0
        for size in sizes:
            results.append(shard[start : start + size])
            start += size
        return results

    column_rows = expand_two.shape[0] * wide // mid
    two_sum = Scatter([chunked(grad_spatial_two)] + chunked_columns(grad_expand_two), (1, 16, 8, 4, 2))

    def beside_steps(value, *scatters):
        for scatter in scatters:
            scatter.step()
        value, *sums = meet(value, *[scatter.value for scatter in scatters])
        for scatter, total in zip(scatters, sums):
            scatter.value = total
        return value

    back_fifth = beside_steps(back_fifth, two_sum)
    two_shard = scatter_chips(two_sum)
    back_maps = maps(back_fifth)
    back_inner = conv_back(
        from_behind(back_maps[:, STRIP - COLS :], 1),
        back_maps,
        from_behind(back_maps[:, :COLS], -1),
        weight_spatial_two,
    ).reshape(pixels, mid)
    back_fourth = norm_b1.backward(per_batch(back_inner) * silu_slope(norm_b1.forward()))
    grad_reduce_two = dot_tn(middle, back_fourth).astype(bf16)

    back_middle = masked_six + per_batch(dot_nt(back_fourth, weight_reduce_two))
    masked_three = back_middle * silu_slope(joined_one)
    back_third = norm_a3.backward(masked_three)
    grad_expand_one = dot_tn(hidden_two, back_third).astype(bf16)
    back_second = norm_a2.backward(
        per_batch(dot_nt(back_third, weight_expand_one)) * silu_slope(norm_a2.forward())
    )
    grad_deform_one = dot_tn(sampled, back_second).astype(bf16)
    one_left = Scatter([chunked(grad_deform_one)], (1, 2, 4, 8, 16))
    one_right = Scatter(
        chunked_columns(grad_expand_one) + [chunked(grad_reduce_two)], (1, 4, 2, 8, 16)
    )
    back_second, one_left.value, one_right.value = meet(
        back_second, one_left.value, one_right.value
    )
    back_sampled = dot_nt(back_second, weight_deform_one).astype(bf16).reshape(images, STRIP, -1)
    back_sampled = beside_steps(back_sampled, one_left, one_right)

    def returned(upstream, first):
        own, *others, position_grad = sample_back(
            positions, pieces, upstream, first, images // MB
        )
        half_sum = jnp.concatenate([from_behind(others[4], 3), from_behind(others[5], -3)], axis=1)
        own = (
            own
            + from_behind(others[0], 1).astype(f32)
            + from_behind(others[1], -1).astype(f32)
            + from_behind(others[2], 2).astype(f32)
            + from_behind(others[3], -2).astype(f32)
            + half_sum.astype(f32)
        )
        return own, position_grad

    backs = [returned(back_sampled, 0)]
    back_sampled = beside_steps(back_sampled, one_left, one_right)
    back_sampled, two_shard = meet(back_sampled, two_shard)
    backs.append(returned(back_sampled, images // MB))
    own = jnp.concatenate([pair[0] for pair in backs], axis=0)
    position_grad = jnp.concatenate([pair[1] for pair in backs], axis=0)
    back_offsets, last_rim, first_rim = offset_slope(position_grad, squashed)
    stacked, offset_chunks = offset_back(
        back_offsets,
        from_behind(last_rim, 1),
        from_behind(first_rim, -1),
        flat_inputs,
        count,
        offset_rows,
        mid,
    )
    offset_to_images = dot_tn(stacked, tap_weights)

    back_first = norm_a1.backward(
        per_batch(own.reshape(pixels, mid)) * silu_slope(norm_a1.forward())
    )
    offset_sum = Scatter([offset_chunks], (1, 4, 2, 8, 16))
    back_first = beside_steps(back_first, one_left, one_right, offset_sum)
    grad_reduce_one = dot_tn(flat_inputs, back_first).astype(bf16)
    half_rows = reduce_one.shape[0] // 2
    last_chunks = chunked(grad_reduce_one)
    last_left = Scatter([last_chunks[:, :half_rows]], (1, 2, 4, 8, 16))
    last_right = Scatter([last_chunks[:, half_rows:]], (1, 4, 2, 8, 16))
    back_first = beside_steps(back_first, last_left, last_right)
    grad_images = (
        masked_three.reshape(pixels, wide)
        + dot_nt(back_first, weight_reduce_one)
        + offset_to_images
    )
    grad_images = beside_steps(grad_images, last_left, last_right).reshape(images_in.shape)
    reduce_shard = jnp.concatenate([last_left.finish(), last_right.finish()], axis=0)
    offset_shard = offset_unstack(offset_sum.finish(), offset_rows)
    deform_shard = one_left.finish()
    expand_shard, reduce_two_shard = split_rows(
        one_right.finish(), [column_rows, reduce_two.shape[0]]
    )
    spatial_shard, expand_two_shard = split_rows(two_shard, [spatial_two.shape[0], column_rows])

    me = lax.axis_index(BOTH)
    mid_grads = jnp.stack(
        [
            norm_a1.gain_grad,
            norm_a2.gain_grad,
            norm_a1.bias_grad,
            norm_a2.bias_grad,
            norm_b1.gain_grad,
            norm_b2.gain_grad,
            norm_b1.bias_grad,
            norm_b2.bias_grad,
        ]
    )
    mid_grads = lax.dynamic_slice_in_dim(mid_grads, me * mid_part, mid_part, 1)
    wide_grads = jnp.stack(
        [norm_a3.gain_grad, norm_a3.bias_grad, norm_b3.gain_grad, norm_b3.bias_grad]
    )
    wide_grads = lax.dynamic_slice_in_dim(wide_grads, me * wide_part, wide_part, 1)
    return (
        block_out,
        grad_images,
        reduce_shard,
        offset_shard,
        deform_shard,
        unchunked_columns(expand_shard),
        mid_grads[0:2],
        mid_grads[2:4],
        wide_grads[0],
        wide_grads[1],
        reduce_two_shard,
        spatial_shard,
        unchunked_columns(expand_two_shard),
        mid_grads[4:6],
        mid_grads[6:8],
        wide_grads[2],
        wide_grads[3],
    )


def solution(mesh):
    whole = P(BOTH, None)
    part = P(None, BOTH)
    line = P(BOTH)
    maps = P("img", "rows", None, None)
    return jax.shard_map(
        on_device,
        mesh=mesh,
        in_specs=(
            maps,
            maps,
            P("img", None, None),
            P("img", None, None),
            P("img"),
            P("img", "rows", None),
            whole,
            whole,
            whole,
            whole,
            part,
            part,
            line,
            line,
            whole,
            whole,
            whole,
            part,
            part,
            line,
            line,
        ),
        out_specs=(
            maps,
            maps,
            whole,
            whole,
            whole,
            whole,
            part,
            part,
            line,
            line,
            whole,
            whole,
            whole,
            part,
            part,
            line,
            line,
        ),
        check_vma=False,
    )
```

```python
from functools import partial

import jax
import jax.numpy as jnp
from jax import lax
from jax.experimental import pallas as pl
from jax.experimental.pallas import tpu as pltpu
from jax.sharding import PartitionSpec as P

CLIP = 8
HALO = 10
MB = 2
BOTH = ("rows", "img")
MIB = 2**20

epsilon = 1e-05
exact = lax.Precision.HIGHEST
f32 = jnp.float32
bf16 = jnp.bfloat16

STRIP_ROWS = 4
COLS = 44
STRIP = STRIP_ROWS * COLS
QUERIES = 9 * STRIP
LANES = 1664
CELLS = (STRIP_ROWS + 2 * HALO) * COLS
ROW_ORDER = (10, 11, 12, 13, 14, 15, 16, 17, 6, 7, 8, 9, 18, 19, 20, 21, 2, 3, 4, 5, 22, 23, 0, 1)


SMALL = pl.CostEstimate(flops=1, bytes_accessed=1, transcendentals=0)


def dot(left, right):
    return jnp.dot(left, right, preferred_element_type=f32)


def dot_nt(left, right):
    return lax.dot_general(left, right, (((1,), (1,)), ((), ())), preferred_element_type=f32)


def dot_tn(left, right):
    return lax.dot_general(left, right, (((0,), (0,)), ((), ())), preferred_element_type=f32)


def device_count():
    return lax.axis_size(BOTH)


def exchange(value, mask):
    return lax.ppermute(value, BOTH, [(i, i ^ mask) for i in range(device_count())])


def all_sum(value):
    count = device_count()
    bit = 1
    while bit < count:
        masks = [bit, 2 * bit, 3 * bit] if 2 * bit < count else [bit]
        parts = [exchange(value, mask) for mask in masks]
        for part in parts:
            value = value + part
        bit *= 4
    return value


def bits_of(order):
    bits = [1 << k for k in range(device_count().bit_length() - 1)]
    return [b for b in order if b in bits] + [b for b in bits if b not in order]


def tie(value, *others):
    return lax.optimization_barrier((value,) + others)[0]


def meet(*values):
    return lax.optimization_barrier(values)


class Scatter:
    def __init__(self, pieces, order):
        self.order = bits_of(order)
        bits = sorted(self.order, reverse=True)
        count = len(bits)
        axes = [bits.index(b) for b in self.order] + [count, count + 1]
        self.value = jnp.concatenate(
            [piece.reshape((2,) * count + piece.shape[1:]).transpose(axes) for piece in pieces],
            axis=-2,
        )

    def step(self):
        bit = self.order.pop(0)
        mine = (lax.axis_index(BOTH) // bit) % 2
        keep = lax.dynamic_index_in_dim(self.value, mine, 0, keepdims=False)
        send = lax.dynamic_index_in_dim(self.value, 1 - mine, 0, keepdims=False)
        total = keep.astype(f32) + exchange(send, bit).astype(f32)
        self.value = total.astype(bf16) if self.order else total
        return self.value

    def finish(self):
        while self.order:
            self.step()
        return self.value


def scatter_chips(scatter):
    count = device_count()
    groups = [[i for i in range(count) if i % 2 == side] for side in range(2)]
    value = scatter.value
    return lax.psum_scatter(
        value.reshape(-1, value.shape[-1]),
        BOTH,
        scatter_dimension=0,
        axis_index_groups=groups,
        tiled=True,
    ).astype(f32)


class Gather:
    def __init__(self, piece, groups):
        bits = bits_of(())
        self.groups = [tuple(b for b in group if b in bits) for group in groups]
        self.groups += [(b,) for b in bits if not any(b in group for group in self.groups)]
        self.done = []
        self.piece = piece
        self.value = piece

    def step(self):
        group = self.groups.pop(0)
        by_mask = {0: self.value}
        for bit in group:
            for mask in sub_masks(group, bit):
                by_mask[bit + mask] = exchange(self.value, bit + mask)
        for bit in group:
            mine = (lax.axis_index(BOTH) // bit) % 2 == 1
            self.done = sorted(self.done + [bit], reverse=True)
            axis = self.done.index(bit)
            merged = {}
            for mask, part in by_mask.items():
                if not mask & bit:
                    other = by_mask[mask + bit]
                    merged[mask] = jnp.stack(
                        [jnp.where(mine, other, part), jnp.where(mine, part, other)], axis=axis
                    )
            by_mask = merged
        (self.value,) = by_mask.values()

    def result(self):
        return self.value.reshape((-1,) + self.piece.shape)


def sub_masks(group, bit):
    masks = [0]
    for other in group[: group.index(bit)]:
        masks = masks + [mask + other for mask in masks]
    return masks


def from_behind(value, steps):
    count = lax.axis_size("rows")
    first, last = (max(0, -steps), min(count, count - steps))
    return lax.ppermute(value, "rows", [(source, source + steps) for source in range(first, last)])


def spline(values):
    magnitude = jnp.abs(values)
    outer = 1.5 - magnitude
    return jnp.where(
        magnitude < 0.5,
        0.75 - values * values,
        jnp.where(magnitude < 1.5, 0.5 * outer * outer, 0.0),
    )


def spline_slope(values):
    magnitude = jnp.abs(values)
    outer = 1.5 - magnitude
    return jnp.where(
        magnitude < 0.5,
        -2.0 * values,
        jnp.where(magnitude < 1.5, jnp.where(values > 0, -outer, outer), 0.0),
    )


def fill_factors(pos_ref, row_ref, col_weight, row_weight, col_slope=None, row_slope=None):
    cell_cols = lax.broadcasted_iota(jnp.int32, (2 * COLS, LANES), 0)
    cell_cols = jnp.where(cell_cols >= COLS, cell_cols - COLS, cell_cols).astype(f32)
    col_gap = pos_ref[0, 1:2, :] - cell_cols
    row_gap = pos_ref[0, 0:1, :] - row_ref[...]
    col_weight[...] = spline(col_gap)
    row_weight[...] = spline(row_gap)
    if col_slope is not None:
        col_slope[...] = spline_slope(col_gap)
        row_slope[...] = spline_slope(row_gap)


def fill_sampler(col_weight, row_weight, sampler):
    low = lax.broadcasted_iota(jnp.int32, (8, 128), 0) < 4

    def body(tile, carry):
        lanes = pl.ds(pl.multiple_of(tile * 128, 128), 128)
        for block in range(6):
            for chunk in range(11):
                halves = []
                for group in (2 * chunk, 2 * chunk + 1):
                    first, last = (8 * group) // COLS, (8 * group + 7) // COLS
                    weight = row_weight[4 * block + first : 4 * block + first + 1, lanes]
                    if first != last:
                        weight = jnp.where(
                            low, weight, row_weight[4 * block + last : 4 * block + last + 1, lanes]
                        )
                    local = group % 11
                    halves.append(col_weight[8 * local : 8 * local + 8, lanes] * weight)
                start = block * STRIP + 16 * chunk
                sampler[start : start + 16, lanes] = jnp.concatenate(halves, axis=0).astype(bf16)
        return carry

    lax.fori_loop(0, LANES // 128, body, 0)


def fill_window(pieces, window):
    for index, piece in enumerate(pieces[:5]):
        window[index * STRIP : (index + 1) * STRIP, :] = piece[0]
    window[5 * STRIP : 6 * STRIP, :] = jnp.concatenate([pieces[5][0], pieces[6][0]], axis=0)


def sample_kernel(pos_ref, row_ref, *refs):
    pieces, out_ref = refs[:7], refs[7]
    col_weight, row_weight, sampler, window = refs[8:]
    fill_factors(pos_ref, row_ref, col_weight, row_weight)
    fill_sampler(col_weight, row_weight, sampler)
    fill_window(pieces, window)
    result = dot_tn(window[...], sampler[...]).T.astype(bf16)
    width = window.shape[1]
    for tap in range(9):
        out_ref[0, :, tap * width : (tap + 1) * width] = result[tap * STRIP : (tap + 1) * STRIP]


def sample_back_kernel(pos_ref, row_ref, *refs):
    pieces, upstream_ref = refs[:7], refs[7]
    grads, pos_grad = refs[8:15], refs[15]
    (
        col_weight,
        row_weight,
        col_slope,
        row_slope,
        sampler,
        window,
        upstream,
        sampler_grad,
    ) = refs[16:]
    fill_factors(pos_ref, row_ref, col_weight, row_weight, col_slope, row_slope)
    fill_sampler(col_weight, row_weight, sampler)
    fill_window(pieces, window)
    width = window.shape[1]
    for tap in range(9):
        upstream[tap * STRIP : (tap + 1) * STRIP, :] = upstream_ref[
            0, :, tap * width : (tap + 1) * width
        ]
    upstream[QUERIES:LANES, :] = jnp.zeros((LANES - QUERIES, width), bf16)
    sampler_grad[...] = dot_nt(window[...], upstream[...])
    for index, grad in enumerate(grads[:5]):
        grad[0] = dot(sampler[index * STRIP : (index + 1) * STRIP, :], upstream[...]).astype(
            grad.dtype
        )
    last = dot(sampler[5 * STRIP :, :], upstream[...])
    grads[5][0] = last[: STRIP // 2].astype(bf16)
    grads[6][0] = last[STRIP // 2 :].astype(bf16)
    low = lax.broadcasted_iota(jnp.int32, (8, 128), 0) < 4

    def body(tile, carry):
        lanes = pl.ds(pl.multiple_of(tile * 128, 128), 128)
        zero = jnp.zeros((8, 128), f32)
        weights = [col_weight[8 * group : 8 * group + 8, lanes] for group in range(11)]
        middle_low = jnp.where(low, weights[5], 0.0)
        middle_high = jnp.where(low, 0.0, weights[5])
        row_total = zero
        col_totals = [zero] * 11
        for pair in range(12):
            first = row_weight[2 * pair : 2 * pair + 1, lanes]
            second = row_weight[2 * pair + 1 : 2 * pair + 2, lanes]
            mixed = jnp.where(low, first, second)
            first_sum = zero
            second_sum = zero
            for group in range(11):
                start = 88 * pair + 8 * group
                value = sampler_grad[start : start + 8, lanes]
                if group < 5:
                    first_sum = first_sum + value * weights[group]
                    col_totals[group] = col_totals[group] + value * first
                elif group > 5:
                    second_sum = second_sum + value * weights[group]
                    col_totals[group] = col_totals[group] + value * second
                else:
                    first_sum = first_sum + value * middle_low
                    second_sum = second_sum + value * middle_high
                    col_totals[group] = col_totals[group] + value * mixed
            row_total = (
                row_total
                + first_sum * row_slope[2 * pair : 2 * pair + 1, lanes]
                + second_sum * row_slope[2 * pair + 1 : 2 * pair + 2, lanes]
            )
        col_total = zero
        for group in range(11):
            col_total = col_total + col_totals[group] * col_slope[8 * group : 8 * group + 8, lanes]
        pos_grad[0, 0:1, lanes] = jnp.sum(row_total, axis=0, keepdims=True)
        pos_grad[0, 1:2, lanes] = jnp.sum(col_total, axis=0, keepdims=True)
        return carry

    lax.fori_loop(0, LANES // 128, body, 0)


def piece_specs(width):
    full = pl.BlockSpec((1, STRIP, width), lambda i: (i, 0, 0))
    half = pl.BlockSpec((1, STRIP // 2, width), lambda i: (i, 0, 0))
    return [full] * 5 + [half] * 2


def sampler_specs(width):
    return [
        pl.BlockSpec((1, 2, LANES), lambda i: (i, 0, 0)),
        pl.BlockSpec((len(ROW_ORDER), 1), lambda i: (0, 0)),
    ] + piece_specs(width)


def row_ids():
    return jnp.array(ROW_ORDER, f32)[:, None]


def sample(positions, pieces):
    images, _, width = pieces[0].shape
    return pl.pallas_call(
        sample_kernel,
        grid=(images,),
        in_specs=sampler_specs(width),
        out_specs=pl.BlockSpec((1, STRIP, 9 * width), lambda i: (i, 0, 0)),
        out_shape=jax.ShapeDtypeStruct((images, STRIP, 9 * width), bf16),
        scratch_shapes=[
            pltpu.VMEM((2 * COLS, LANES), f32),
            pltpu.VMEM((len(ROW_ORDER), LANES), f32),
            pltpu.VMEM((CELLS, LANES), bf16),
            pltpu.VMEM((CELLS, width), bf16),
        ],
        compiler_params=pltpu.CompilerParams(vmem_limit_bytes=60 * MIB),
        cost_estimate=SMALL,
        name="sample",
    )(positions, row_ids(), *pieces)


def sample_back(positions, pieces, upstream):
    images, _, width = pieces[0].shape
    full = (images, STRIP, width)
    half = (images, STRIP // 2, width)
    return pl.pallas_call(
        sample_back_kernel,
        grid=(images,),
        in_specs=sampler_specs(width)
        + [pl.BlockSpec((1, STRIP, 9 * width), lambda i: (i, 0, 0))],
        out_specs=piece_specs(width) + [pl.BlockSpec((1, 2, LANES), lambda i: (i, 0, 0))],
        out_shape=[jax.ShapeDtypeStruct(full, f32)]
        + [jax.ShapeDtypeStruct(full, bf16)] * 4
        + [jax.ShapeDtypeStruct(half, bf16)] * 2
        + [jax.ShapeDtypeStruct((images, 2, LANES), f32)],
        scratch_shapes=[
            pltpu.VMEM((2 * COLS, LANES), f32),
            pltpu.VMEM((len(ROW_ORDER), LANES), f32),
            pltpu.VMEM((2 * COLS, LANES), f32),
            pltpu.VMEM((len(ROW_ORDER), LANES), f32),
            pltpu.VMEM((CELLS, LANES), bf16),
            pltpu.VMEM((CELLS, width), bf16),
            pltpu.VMEM((LANES, width), bf16),
            pltpu.VMEM((CELLS, LANES), f32),
        ],
        compiler_params=pltpu.CompilerParams(vmem_limit_bytes=34 * MIB),
        cost_estimate=SMALL,
        name="sample_back",
    )(positions, row_ids(), *pieces, upstream)


def tap_slabs(above, own, below, padded, image):
    padded[8 : 8 + COLS, :] = above[image].astype(f32)
    padded[8 + COLS : 8 + COLS + STRIP, :] = own[image].astype(f32)
    padded[8 + COLS + STRIP : 8 + 2 * COLS + STRIP, :] = below[image].astype(f32)
    cols = lax.broadcasted_iota(jnp.int32, (STRIP, 1), 0) % COLS
    for tap in range(9):
        start = 8 + COLS * (tap // 3) + tap % 3 - 1
        slab = padded[start : start + STRIP, :]
        if tap % 3 == 0:
            slab = jnp.where(cols > 0, slab, 0.0)
        elif tap % 3 == 2:
            slab = jnp.where(cols < COLS - 1, slab, 0.0)
        yield tap, slab.astype(bf16)


def conv_kernel(above, own, below, weight, out_ref, slabs_ref, padded):
    width = own.shape[2]
    images = own.shape[0]
    for image in range(images):
        for tap, slab in tap_slabs(above, own, below, padded, image):
            slabs_ref[image, :, tap * width : (tap + 1) * width] = slab
    total = None
    for tap in range(9):
        lanes = slice(tap * width, (tap + 1) * width)
        part = dot(slabs_ref[:, :, lanes].reshape(images * STRIP, width), weight[lanes, :])
        total = part if total is None else total + part
    out_ref[...] = total.reshape(out_ref.shape)


def conv_back_kernel(above, own, below, weight, out_ref, padded, slabs):
    width = own.shape[2]
    images = own.shape[0]
    for image in range(images):
        for tap, slab in tap_slabs(above, own, below, padded, image):
            slabs[8 - tap, image * STRIP : (image + 1) * STRIP, :] = slab
    total = None
    for tap in range(9):
        part = dot_nt(slabs[tap], weight[tap * width : (tap + 1) * width, :])
        total = part if total is None else total + part
    out_ref[...] = total.reshape(out_ref.shape)


def conv_specs(images, width):
    rim = pl.BlockSpec((images, COLS, width), lambda i: (i, 0, 0))
    own = pl.BlockSpec((images, STRIP, width), lambda i: (i, 0, 0))
    return [rim, own, rim, pl.BlockSpec((9 * width, width), lambda i: (0, 0))]


def conv(above, own, below, weight):
    images, _, width = own.shape
    step = images // MB
    return pl.pallas_call(
        conv_kernel,
        grid=(MB,),
        in_specs=conv_specs(step, width),
        out_specs=[
            pl.BlockSpec((step, STRIP, width), lambda i: (i, 0, 0)),
            pl.BlockSpec((step, STRIP, 9 * width), lambda i: (i, 0, 0)),
        ],
        out_shape=[
            jax.ShapeDtypeStruct((images, STRIP, width), f32),
            jax.ShapeDtypeStruct((images, STRIP, 9 * width), bf16),
        ],
        scratch_shapes=[pltpu.VMEM((16 + 2 * COLS + STRIP, width), f32)],
        compiler_params=pltpu.CompilerParams(vmem_limit_bytes=24 * MIB),
        cost_estimate=SMALL,
        name="conv",
    )(above, own, below, weight)


def conv_back(above, own, below, weight):
    images, _, width = own.shape
    step = images // MB
    return pl.pallas_call(
        conv_back_kernel,
        grid=(MB,),
        in_specs=conv_specs(step, width),
        out_specs=pl.BlockSpec((step, STRIP, width), lambda i: (i, 0, 0)),
        out_shape=jax.ShapeDtypeStruct((images, STRIP, width), f32),
        scratch_shapes=[
            pltpu.VMEM((16 + 2 * COLS + STRIP, width), f32),
            pltpu.VMEM((9, step * STRIP, width), bf16),
        ],
        compiler_params=pltpu.CompilerParams(vmem_limit_bytes=24 * MIB),
        cost_estimate=SMALL,
        name="conv_back",
    )(above, own, below, weight)


TAP = 32


def offset_spans(device, rows, wide):
    spans = []
    start = device * rows
    while start < (device + 1) * rows:
        tap, column = divmod(start, wide)
        size = min((device + 1) * rows - start, wide - column)
        spans.append((tap, column, start - device * rows, size))
        start += size
    return spans


def offset_stack(strip, extra, width):
    rows = strip.shape[-1]
    lead = [(0, 0)] * (strip.ndim - 2)
    strip = jnp.pad(strip, lead + [(0, TAP - 18), (0, 0)])
    full = rows // width * width
    blocks = [strip[..., start : start + width] for start in range(0, full, width)]
    rest = strip[..., full:]
    rest = jnp.concatenate([rest[..., :16, :], rest[..., 16:, :]], axis=-1)
    pad = width - rest.shape[-1] - extra.shape[-1]
    assert pad >= 0
    blocks.append(jnp.pad(jnp.concatenate([rest, extra], axis=-1), lead + [(0, 0), (0, pad)]))
    return jnp.concatenate(blocks, axis=-2)


def spread_rows(values, images, take):
    parts = []
    for image in range(images):
        parts += take(image)
    return jnp.concatenate(parts, axis=1)


def own_lanes(values, image, start):
    first = image * STRIP + start
    return values[:, first : first + STRIP // 2]


def rim_lanes(values, image):
    return values[:, image * STRIP // 2 : (image + 1) * STRIP // 2]


def down_two(own, above, images):
    return spread_rows(own, images, lambda i: [rim_lanes(above, i), own_lanes(own, i, 0)])


def up_two(own, below, images):
    return spread_rows(own, images, lambda i: [own_lanes(own, i, STRIP // 2), rim_lanes(below, i)])


def beside(values, steps):
    if steps == 0:
        return values
    rows, cells = values.shape
    column = lax.broadcasted_iota(jnp.int32, (1, cells), 1) % COLS
    empty = jnp.zeros((rows, abs(steps)), values.dtype)
    if steps > 0:
        moved = jnp.concatenate([values[:, steps:], empty], axis=1)
    else:
        moved = jnp.concatenate([empty, values[:, :steps]], axis=1)
    return jnp.where((column + steps >= 0) & (column + steps < COLS), moved, 0.0)


def offset_conv_kernel(rows, small_ref, input_ref, taps_ref, partial_ref, last_ref, first_ref):
    count, _, width = small_ref.shape
    wide = input_ref.shape[1]
    images = input_ref.shape[0] // STRIP
    full = rows // width
    rest = rows - full * width
    for device in range(count):
        blocks = [small_ref[device, TAP * i : TAP * (i + 1), :] for i in range(full)]
        if rest:
            block = small_ref[device, TAP * full : TAP * full + 16, :]
            blocks.append(
                jnp.concatenate([block[:, :rest], block[:, rest : 2 * rest]], axis=0)
            )
        strip = jnp.concatenate(blocks, axis=1)
        for tap, column, local, size in offset_spans(device, rows, wide):
            taps_ref[TAP * tap : TAP * (tap + 1), column : column + size] = strip[
                :, local : local + size
            ]
    partial = dot_nt(taps_ref[...], input_ref[...])
    partial_ref[...] = partial
    half = STRIP // 2
    for image in range(images):
        lanes = slice(image * half, (image + 1) * half)
        last_ref[:, lanes] = own_lanes(partial[: 3 * TAP], image, half)
        first_ref[:, lanes] = own_lanes(partial[6 * TAP :], image, 0)


def offset_conv(small_all, rows, inputs):
    pixels, wide = inputs.shape
    rim = (3 * TAP, pixels // 2)
    return pl.pallas_call(
        partial(offset_conv_kernel, rows),
        out_shape=[
            jax.ShapeDtypeStruct((9 * TAP, wide), bf16),
            jax.ShapeDtypeStruct((9 * TAP, pixels), f32),
            jax.ShapeDtypeStruct(rim, f32),
            jax.ShapeDtypeStruct(rim, f32),
        ],
        compiler_params=pltpu.CompilerParams(vmem_limit_bytes=24 * MIB),
        name="offset_conv",
    )(small_all, inputs)


def positions_kernel(partial_ref, above_ref, below_ref, squashed_ref, positions_ref):
    images = positions_ref.shape[0]
    rows = [
        down_two(partial_ref[: 3 * TAP, :], above_ref[...], images),
        partial_ref[3 * TAP : 6 * TAP, :],
        up_two(partial_ref[6 * TAP :, :], below_ref[...], images),
    ]
    offsets = None
    for row in rows:
        for col_tap in range(3):
            part = beside(row[TAP * col_tap : TAP * (col_tap + 1)], 2 * (col_tap - 1))
            offsets = part if offsets is None else offsets + part
    squashed = jnp.tanh(offsets / CLIP)
    squashed_ref[...] = squashed
    clipped = CLIP * squashed
    cells = images * STRIP
    lane = lax.broadcasted_iota(jnp.int32, (9, cells), 1) % STRIP
    tap = lax.broadcasted_iota(jnp.int32, (9, cells), 0)
    row_position = clipped[:9] + (tap // 3 - 1 + HALO + lane // COLS).astype(f32)
    col_position = clipped[9:18] + (tap % 3 - 1 + lane % COLS).astype(f32)
    positions_ref[:, :, QUERIES:] = jnp.full((images, 2, LANES - QUERIES), -1000.0, f32)
    for image in range(images):
        lanes = slice(image * STRIP, (image + 1) * STRIP)
        for t in range(9):
            place = slice(t * STRIP, (t + 1) * STRIP)
            positions_ref[image, 0:1, place] = row_position[t : t + 1, lanes]
            positions_ref[image, 1:2, place] = col_position[t : t + 1, lanes]


def sample_positions(partial_offsets, above, below):
    cells = partial_offsets.shape[1]
    return pl.pallas_call(
        positions_kernel,
        out_shape=[
            jax.ShapeDtypeStruct((TAP, cells), f32),
            jax.ShapeDtypeStruct((cells // STRIP, 2, LANES), f32),
        ],
        name="sample_positions",
    )(partial_offsets, above, below)


def offset_slope_kernel(position_grad_ref, squashed_ref, back_ref, last_ref, first_ref, flat):
    images = position_grad_ref.shape[0]
    flat[...] = jnp.zeros_like(flat)
    for image in range(images):
        lanes = slice(image * STRIP, (image + 1) * STRIP)
        for t in range(9):
            place = slice(t * STRIP, (t + 1) * STRIP)
            flat[t : t + 1, lanes] = position_grad_ref[image, 0:1, place]
            flat[9 + t : 10 + t, lanes] = position_grad_ref[image, 1:2, place]
    squashed = squashed_ref[...]
    back = (flat[...] * (1.0 - squashed * squashed)).astype(bf16)
    back_ref[...] = back
    half = STRIP // 2
    wider = back.astype(f32)
    for image in range(images):
        lanes = slice(image * half, (image + 1) * half)
        last_ref[:, lanes] = own_lanes(wider, image, half).astype(bf16)
        first_ref[:, lanes] = own_lanes(wider, image, 0).astype(bf16)


def offset_slope(position_grad, squashed):
    cells = squashed.shape[1]
    rim = jax.ShapeDtypeStruct((TAP, cells // 2), bf16)
    return pl.pallas_call(
        offset_slope_kernel,
        out_shape=[jax.ShapeDtypeStruct((TAP, cells), bf16), rim, rim],
        scratch_shapes=[pltpu.VMEM((TAP, cells), f32)],
        name="offset_slope",
    )(position_grad, squashed)


def offset_back_kernel(rows, back_ref, above_ref, below_ref, input_ref, stacked_ref, chunks_ref):
    count, _, width = chunks_ref.shape
    wide = input_ref.shape[1]
    images = input_ref.shape[0] // STRIP
    own = back_ref[...].astype(f32)
    by_row = [
        up_two(own, below_ref[...].astype(f32), images),
        own,
        down_two(own, above_ref[...].astype(f32), images),
    ]
    for tap in range(9):
        moved = beside(by_row[tap // 3], -2 * (tap % 3 - 1))
        stacked_ref[TAP * tap : TAP * (tap + 1), :] = moved.astype(bf16)
    grad = dot(stacked_ref[...], input_ref[...])
    full = rows // width
    rest = rows - full * width
    chunks_ref[...] = jnp.zeros(chunks_ref.shape, bf16)
    for device in range(count):
        strip = jnp.concatenate(
            [
                grad[TAP * tap : TAP * (tap + 1), column : column + size]
                for tap, column, _, size in offset_spans(device, rows, wide)
            ],
            axis=1,
        ).astype(bf16)
        for i in range(full):
            chunks_ref[device, TAP * i : TAP * (i + 1), :] = strip[:, width * i : width * (i + 1)]
        if rest:
            tail = strip[:, width * full :]
            chunks_ref[device, TAP * full :, : 2 * rest] = jnp.concatenate(
                [tail[:16], tail[16:]], axis=1
            )


def offset_back(back, above, below, inputs, count, rows, width):
    pixels, wide = inputs.shape
    stack_rows = rows // width * TAP + (16 if rows % width else 0)
    return pl.pallas_call(
        partial(offset_back_kernel, rows),
        out_shape=[
            jax.ShapeDtypeStruct((9 * TAP, pixels), bf16),
            jax.ShapeDtypeStruct((count, stack_rows, width), bf16),
        ],
        compiler_params=pltpu.CompilerParams(vmem_limit_bytes=24 * MIB),
        name="offset_back",
    )(back, above, below, inputs)


def offset_unstack(shard, rows):
    width = shard.shape[1]
    full = rows // width
    rest = rows - full * width
    blocks = [shard[TAP * i : TAP * i + 18] for i in range(full)]
    if rest:
        tail = shard[TAP * full :]
        blocks.append(jnp.concatenate([tail[:, :rest], tail[:2, rest : 2 * rest]], axis=0))
    return jnp.concatenate(blocks, axis=1).T


def silu_slope(values):
    logistic = jax.nn.sigmoid(values)
    return logistic * (1.0 + values * (1.0 - logistic))


def box_weights(box_rows, box_cols, box_count, valid_mask, strip_rows, span_cols):
    row_ids_ = lax.axis_index("rows") * strip_rows + jnp.arange(strip_rows)
    col_ids = jnp.arange(span_cols)
    row_low = jnp.minimum(box_rows[..., 0], box_rows[..., 1])
    row_high = jnp.maximum(box_rows[..., 0], box_rows[..., 1])
    col_low = jnp.minimum(box_cols[..., 0], box_cols[..., 1])
    col_high = jnp.maximum(box_cols[..., 0], box_cols[..., 1])
    inside_rows = ((row_ids_ >= row_low[..., None]) & (row_ids_ <= row_high[..., None])).astype(f32)
    inside_cols = ((col_ids >= col_low[..., None]) & (col_ids <= col_high[..., None])).astype(f32)
    live_boxes = (jnp.arange(box_rows.shape[1])[None, :] < box_count[:, None]).astype(f32)
    covered = jnp.einsum("ib,ibh,ibw->ihw", live_boxes, inside_rows, inside_cols, precision=exact)
    return valid_mask.astype(f32) * (0.5 + covered / box_count.astype(f32)[:, None, None])


def per_batch(values):
    return values.reshape(MB, values.shape[0] // MB, values.shape[1])


def batch_totals(first, second):
    totals = all_sum(jnp.concatenate([jnp.sum(first, axis=1), jnp.sum(second, axis=1)], axis=0))
    return totals[:MB], totals[MB:]


class Norm:
    def __init__(self, values, gain, bias):
        values = per_batch(values)
        self.count = values.shape[1] * device_count()
        sums, squares = batch_totals(values, values * values)
        self.values = values
        self.center = (sums / self.count)[:, None, :]
        self.spread = lax.rsqrt(squares[:, None, :] / self.count - self.center * self.center + epsilon)
        self.gain = gain.astype(f32)
        self.bias = bias.astype(f32)

    def normed(self):
        return (self.values - self.center) * self.spread

    def forward(self):
        return self.normed() * self.gain + self.bias

    def backward(self, upstream):
        normed = self.normed()
        bias_sums, gain_sums = batch_totals(upstream, upstream * normed)
        self.gain_grad = jnp.sum(gain_sums, axis=0)
        self.bias_grad = jnp.sum(bias_sums, axis=0)
        result = (self.spread * self.gain) * (
            upstream
            - (bias_sums / self.count)[:, None, :]
            - normed * (gain_sums / self.count)[:, None, :]
        )
        return result.astype(bf16).reshape(-1, result.shape[-1])


def stacked_columns(weight, width):
    return jnp.concatenate(jnp.split(weight, weight.shape[1] // width, axis=1), axis=0)


def unstacked_columns(blocks, columns):
    width = blocks.shape[2]
    parts = jnp.split(blocks, columns // width, axis=1)
    return jnp.concatenate([part.reshape(-1, width) for part in parts], axis=1)


def gather(pieces):
    whole = lax.all_gather(jnp.concatenate(pieces, axis=0), BOTH, axis=0)
    results = []
    start = 0
    for piece in pieces:
        results.append(whole[:, start : start + piece.shape[0]])
        start += piece.shape[0]
    return results


def to_width(flat, width):
    rows = -(-flat.shape[-1] // width)
    pad = rows * width - flat.shape[-1]
    return jnp.pad(flat, [(0, 0)] * (flat.ndim - 1) + [(0, pad)]).reshape(
        flat.shape[:-1] + (rows, width)
    )


def widths(values, width):
    pieces = []
    for start in range(0, values.shape[-1], width):
        piece = values[..., start : start + width]
        pad = width - piece.shape[-1]
        pieces.append(jnp.pad(piece, [(0, 0)] * (values.ndim - 1) + [(0, pad)]))
    return pieces


def shifted(values, steps, columns):
    if steps == 0:
        return values
    cells = values.shape[-1]
    column = jnp.arange(cells) % columns
    pad = [(0, 0)] * (values.ndim - 1)
    if steps > 0:
        moved = jnp.pad(values[..., steps:], pad + [(0, steps)])
    else:
        moved = jnp.pad(values[..., :steps], pad + [(-steps, 0)])
    return jnp.where((column + steps >= 0) & (column + steps < columns), moved, 0)


def on_device(
    images_in,
    out_grad,
    box_rows,
    box_cols,
    box_count,
    valid_mask,
    reduce_one,
    offset_one,
    deform_one,
    expand_one,
    mid_gain_one,
    mid_bias_one,
    wide_gain_one,
    wide_bias_one,
    reduce_two,
    spatial_two,
    expand_two,
    mid_gain_two,
    mid_bias_two,
    wide_gain_two,
    wide_bias_two,
):
    images, strip_rows, span_cols, wide = images_in.shape
    mid = reduce_one.shape[1]
    assert strip_rows == STRIP_ROWS and span_cols == COLS
    count = device_count()
    pixels = images * STRIP

    mid_part = mid // count
    wide_part = wide // count
    extent = max(mid_part, wide_part)
    mid_rows = jnp.concatenate([mid_gain_one, mid_bias_one, mid_gain_two, mid_bias_two], axis=0)
    wide_rows = jnp.concatenate(
        [v[None] for v in (wide_gain_one, wide_bias_one, wide_gain_two, wide_bias_two)], axis=0
    )
    vectors = jnp.pad(mid_rows, ((0, 8), (0, extent - mid_part))) + jnp.pad(
        wide_rows, ((8, 4), (0, extent - wide_part))
    )
    offset_rows = offset_one.shape[0]
    small = offset_stack(offset_one.T, vectors, mid)
    flat_inputs = images_in.reshape(pixels, wide)
    flat_out_grad = out_grad.reshape(pixels, wide)
    reduce_gather = Gather(reduce_one, ((8, 16), (4,), (2,), (1,)))
    small_gather = Gather(small, ((8, 16), (2,), (4,), (1,)))
    while reduce_gather.groups:
        reduce_gather.step()
        small_gather.step()
        if len(reduce_gather.groups) == 1:
            reduce_gather.value, small_gather.value, flat_inputs = meet(
                reduce_gather.value, small_gather.value, flat_inputs
            )
        else:
            reduce_gather.value, small_gather.value = meet(reduce_gather.value, small_gather.value)
    reduce_all, small_all = reduce_gather.result(), small_gather.result()
    deform_all, expand_all = gather([deform_one, stacked_columns(expand_one, mid)])
    weight_reduce_one = reduce_all.reshape(wide, mid)
    weight_deform_one = deform_all.reshape(9 * mid, mid)
    weight_expand_one = unstacked_columns(expand_all, wide)
    vector_start = 2 * (offset_rows % mid)
    vector_all = small_all[:, small.shape[0] - 16 :, vector_start : vector_start + extent]
    mid_vectors = vector_all[:, :8, :mid_part].transpose(1, 0, 2).reshape(8, mid)
    wide_vectors = vector_all[:, 8:12, :wide_part].transpose(1, 0, 2).reshape(4, wide)
    gain_mid_one, bias_mid_one = mid_vectors[0:2], mid_vectors[2:4]
    gain_mid_two, bias_mid_two = mid_vectors[4:6], mid_vectors[6:8]

    def maps(values):
        return values.reshape(images, STRIP, values.shape[-1])

    grad_weight = box_weights(box_rows, box_cols, box_count, valid_mask, strip_rows, span_cols)

    first_conv = dot(flat_inputs, weight_reduce_one)
    first_conv, small_all = meet(first_conv, small_all)
    norm_a1 = Norm(first_conv, gain_mid_one[0], bias_mid_one[0])
    tap_weights, partial_offsets, last_rim, first_rim = offset_conv(
        small_all, offset_rows, flat_inputs
    )
    hidden = jax.nn.silu(norm_a1.forward()).astype(bf16).reshape(images, STRIP, mid)
    hidden, rim_above, rim_below = meet(hidden, from_behind(last_rim, 1), from_behind(first_rim, -1))
    half = STRIP // 2
    squashed, positions = sample_positions(partial_offsets, rim_above, rim_below)
    pieces = [
        hidden,
        from_behind(hidden, -1),
        from_behind(hidden, 1),
        from_behind(hidden, -2),
        from_behind(hidden, 2),
        from_behind(hidden[:, :half], -3),
        from_behind(hidden[:, half:], 3),
    ]
    positions, flat_out_grad, reduce_two, spatial_two, expand_two, *pieces = meet(
        positions, flat_out_grad, reduce_two, spatial_two, expand_two, *pieces
    )
    reduce_two_all, spatial_all, expand_two_all = gather(
        [reduce_two, spatial_two, stacked_columns(expand_two, mid)]
    )
    weight_reduce_two = reduce_two_all.reshape(wide, mid)
    weight_spatial_two = spatial_all.reshape(9 * mid, mid)
    weight_expand_two = unstacked_columns(expand_two_all, wide)
    sampled = sample(positions, pieces).reshape(pixels, 9 * mid)
    norm_a2 = Norm(dot(sampled, weight_deform_one), gain_mid_one[1], bias_mid_one[1])
    hidden_two = jax.nn.silu(norm_a2.forward()).astype(bf16).reshape(pixels, mid)
    norm_a3 = Norm(dot(hidden_two, weight_expand_one), wide_vectors[0], wide_vectors[1])
    joined_one = norm_a3.forward() + per_batch(flat_inputs).astype(f32)
    middle = jax.nn.silu(joined_one).astype(bf16).reshape(pixels, wide)

    norm_b1 = Norm(dot(middle, weight_reduce_two), gain_mid_two[0], bias_mid_two[0])
    inner_one = maps(jax.nn.silu(norm_b1.forward()).astype(bf16))
    fifth_conv, inner_slabs = conv(
        from_behind(inner_one[:, STRIP - COLS :], 1),
        inner_one,
        from_behind(inner_one[:, :COLS], -1),
        weight_spatial_two,
    )
    norm_b2 = Norm(fifth_conv.reshape(pixels, mid), gain_mid_two[1], bias_mid_two[1])
    inner_two = jax.nn.silu(norm_b2.forward()).astype(bf16).reshape(pixels, mid)
    norm_b3 = Norm(dot(inner_two, weight_expand_two), wide_vectors[2], wide_vectors[3])
    joined_two = norm_b3.forward() + per_batch(middle).astype(f32)
    block_out = jax.nn.silu(joined_two).astype(bf16).reshape(images_in.shape)

    upstream = per_batch(flat_out_grad).astype(f32) * grad_weight.reshape(MB, pixels // MB, 1)
    masked_six = upstream * silu_slope(joined_two)
    back_sixth = norm_b3.backward(masked_six)
    grad_expand_two = dot_tn(inner_two, back_sixth).astype(bf16)
    back_fifth = norm_b2.backward(
        per_batch(dot_nt(back_sixth, weight_expand_two)) * silu_slope(norm_b2.forward())
    )
    grad_spatial_two = dot_tn(inner_slabs.reshape(pixels, 9 * mid), back_fifth).astype(bf16)
    def chunked(grad):
        return grad.reshape(count, -1, mid)

    def chunked_columns(grad):
        return [part.reshape(count, -1, mid) for part in jnp.split(grad, grad.shape[1] // mid, axis=1)]

    def unchunked_columns(shard):
        return jnp.concatenate(jnp.split(shard, wide // mid, axis=0), axis=1)

    def split_rows(shard, sizes):
        results = []
        start = 0
        for size in sizes:
            results.append(shard[start : start + size])
            start += size
        return results

    column_rows = expand_two.shape[0] * wide // mid
    two_sum = Scatter([chunked(grad_spatial_two)] + chunked_columns(grad_expand_two), (1, 16, 8, 4, 2))

    def beside_steps(value, *scatters):
        for scatter in scatters:
            scatter.step()
        value, *sums = meet(value, *[scatter.value for scatter in scatters])
        for scatter, total in zip(scatters, sums):
            scatter.value = total
        return value

    back_fifth = beside_steps(back_fifth, two_sum)
    two_shard = scatter_chips(two_sum)
    back_maps = maps(back_fifth)
    back_inner = conv_back(
        from_behind(back_maps[:, STRIP - COLS :], 1),
        back_maps,
        from_behind(back_maps[:, :COLS], -1),
        weight_spatial_two,
    ).reshape(pixels, mid)
    back_fourth = norm_b1.backward(per_batch(back_inner) * silu_slope(norm_b1.forward()))
    grad_reduce_two = dot_tn(middle, back_fourth).astype(bf16)

    back_middle = masked_six + per_batch(dot_nt(back_fourth, weight_reduce_two))
    masked_three = back_middle * silu_slope(joined_one)
    back_third = norm_a3.backward(masked_three)
    grad_expand_one = dot_tn(hidden_two, back_third).astype(bf16)
    back_second = norm_a2.backward(
        per_batch(dot_nt(back_third, weight_expand_one)) * silu_slope(norm_a2.forward())
    )
    grad_deform_one = dot_tn(sampled, back_second).astype(bf16)
    one_left = Scatter([chunked(grad_deform_one)], (1, 2, 4, 8, 16))
    one_right = Scatter(
        chunked_columns(grad_expand_one) + [chunked(grad_reduce_two)], (1, 4, 2, 8, 16)
    )
    back_second, one_left.value, one_right.value = meet(
        back_second, one_left.value, one_right.value
    )
    back_sampled = dot_nt(back_second, weight_deform_one).astype(bf16).reshape(images, STRIP, -1)
    back_sampled = beside_steps(back_sampled, one_left, one_right)

    own, *others, position_grad = sample_back(positions, pieces, back_sampled)
    half_sum = jnp.concatenate([from_behind(others[4], 3), from_behind(others[5], -3)], axis=1)
    own = (
        own
        + from_behind(others[0], 1).astype(f32)
        + from_behind(others[1], -1).astype(f32)
        + from_behind(others[2], 2).astype(f32)
        + from_behind(others[3], -2).astype(f32)
        + half_sum.astype(f32)
    )
    own, two_shard = meet(own, two_shard)
    back_offsets, last_rim, first_rim = offset_slope(position_grad, squashed)
    stacked, offset_chunks = offset_back(
        back_offsets,
        from_behind(last_rim, 1),
        from_behind(first_rim, -1),
        flat_inputs,
        count,
        offset_rows,
        mid,
    )
    offset_to_images = dot_tn(stacked, tap_weights)

    back_first = norm_a1.backward(
        per_batch(own.reshape(pixels, mid)) * silu_slope(norm_a1.forward())
    )
    offset_sum = Scatter([offset_chunks], (1, 4, 2, 8, 16))
    back_first = beside_steps(back_first, one_left, one_right, offset_sum)
    grad_reduce_one = dot_tn(flat_inputs, back_first).astype(bf16)
    half_rows = reduce_one.shape[0] // 2
    last_chunks = chunked(grad_reduce_one)
    last_left = Scatter([last_chunks[:, :half_rows]], (1, 2, 4, 8, 16))
    last_right = Scatter([last_chunks[:, half_rows:]], (1, 4, 2, 8, 16))
    back_first = beside_steps(back_first, last_left, last_right)
    grad_images = (
        masked_three.reshape(pixels, wide)
        + dot_nt(back_first, weight_reduce_one)
        + offset_to_images
    )
    grad_images = beside_steps(grad_images, last_left, last_right).reshape(images_in.shape)
    reduce_shard = jnp.concatenate([last_left.finish(), last_right.finish()], axis=0)
    offset_shard = offset_unstack(offset_sum.finish(), offset_rows)
    deform_shard = one_left.finish()
    expand_shard, reduce_two_shard = split_rows(
        one_right.finish(), [column_rows, reduce_two.shape[0]]
    )
    spatial_shard, expand_two_shard = split_rows(two_shard, [spatial_two.shape[0], column_rows])

    me = lax.axis_index(BOTH)
    mid_grads = jnp.stack(
        [
            norm_a1.gain_grad,
            norm_a2.gain_grad,
            norm_a1.bias_grad,
            norm_a2.bias_grad,
            norm_b1.gain_grad,
            norm_b2.gain_grad,
            norm_b1.bias_grad,
            norm_b2.bias_grad,
        ]
    )
    mid_grads = lax.dynamic_slice_in_dim(mid_grads, me * mid_part, mid_part, 1)
    wide_grads = jnp.stack(
        [norm_a3.gain_grad, norm_a3.bias_grad, norm_b3.gain_grad, norm_b3.bias_grad]
    )
    wide_grads = lax.dynamic_slice_in_dim(wide_grads, me * wide_part, wide_part, 1)
    return (
        block_out,
        grad_images,
        reduce_shard,
        offset_shard,
        deform_shard,
        unchunked_columns(expand_shard),
        mid_grads[0:2],
        mid_grads[2:4],
        wide_grads[0],
        wide_grads[1],
        reduce_two_shard,
        spatial_shard,
        unchunked_columns(expand_two_shard),
        mid_grads[4:6],
        mid_grads[6:8],
        wide_grads[2],
        wide_grads[3],
    )


def solution(mesh):
    whole = P(BOTH, None)
    part = P(None, BOTH)
    line = P(BOTH)
    maps = P("img", "rows", None, None)
    return jax.shard_map(
        on_device,
        mesh=mesh,
        in_specs=(
            maps,
            maps,
            P("img", None, None),
            P("img", None, None),
            P("img"),
            P("img", "rows", None),
            whole,
            whole,
            whole,
            whole,
            part,
            part,
            line,
            line,
            whole,
            whole,
            whole,
            part,
            part,
            line,
            line,
        ),
        out_specs=(
            maps,
            maps,
            whole,
            whole,
            whole,
            whole,
            part,
            part,
            line,
            line,
            whole,
            whole,
            whole,
            part,
            part,
            line,
            line,
        ),
        check_vma=False,
    )
```

```python
from functools import partial

import jax
import jax.numpy as jnp
from jax import lax
from jax.experimental import pallas as pl
from jax.experimental.pallas import tpu as pltpu
from jax.sharding import PartitionSpec as P

CLIP = 8
HALO = 10
MB = 2
BOTH = ("rows", "img")
MIB = 2**20

epsilon = 1e-05
exact = lax.Precision.HIGHEST
f32 = jnp.float32
bf16 = jnp.bfloat16

STRIP_ROWS = 4
COLS = 44
STRIP = STRIP_ROWS * COLS
QUERIES = 9 * STRIP
LANES = 1664
CELLS = (STRIP_ROWS + 2 * HALO) * COLS
ROW_ORDER = (10, 11, 12, 13, 14, 15, 16, 17, 6, 7, 8, 9, 18, 19, 20, 21, 2, 3, 4, 5, 22, 23, 0, 1)


SMALL = pl.CostEstimate(flops=1, bytes_accessed=1, transcendentals=0)


def dot(left, right):
    return jnp.dot(left, right, preferred_element_type=f32)


def dot_nt(left, right):
    return lax.dot_general(left, right, (((1,), (1,)), ((), ())), preferred_element_type=f32)


def dot_tn(left, right):
    return lax.dot_general(left, right, (((0,), (0,)), ((), ())), preferred_element_type=f32)


def device_count():
    return lax.axis_size(BOTH)


def exchange(value, mask):
    return lax.ppermute(value, BOTH, [(i, i ^ mask) for i in range(device_count())])


def all_sum(value):
    count = device_count()
    bit = 1
    if count.bit_length() % 2 == 0:
        value = value + exchange(value, 1)
        bit = 2
    while bit < count:
        parts = [exchange(value, mask) for mask in (bit, 2 * bit, 3 * bit)]
        for part in parts:
            value = value + part
        bit *= 4
    return value


def bits_of(order):
    bits = [1 << k for k in range(device_count().bit_length() - 1)]
    return [b for b in order if b in bits] + [b for b in bits if b not in order]


def tie(value, *others):
    return lax.optimization_barrier((value,) + others)[0]


def meet(*values):
    return lax.optimization_barrier(values)


class Scatter:
    def __init__(self, pieces, order):
        self.order = bits_of(order)
        bits = sorted(self.order, reverse=True)
        count = len(bits)
        axes = [bits.index(b) for b in self.order] + [count, count + 1]
        self.value = jnp.concatenate(
            [piece.reshape((2,) * count + piece.shape[1:]).transpose(axes) for piece in pieces],
            axis=-2,
        )

    def step(self):
        bit = self.order.pop(0)
        mine = (lax.axis_index(BOTH) // bit) % 2
        keep = lax.dynamic_index_in_dim(self.value, mine, 0, keepdims=False)
        send = lax.dynamic_index_in_dim(self.value, 1 - mine, 0, keepdims=False)
        total = keep.astype(f32) + exchange(send, bit).astype(f32)
        self.value = total.astype(bf16) if self.order else total
        return self.value

    def finish(self):
        while self.order:
            self.step()
        return self.value


def scatter_chips(scatter):
    count = device_count()
    groups = [[i for i in range(count) if i % 2 == side] for side in range(2)]
    value = scatter.value
    return lax.psum_scatter(
        value.reshape(-1, value.shape[-1]),
        BOTH,
        scatter_dimension=0,
        axis_index_groups=groups,
        tiled=True,
    ).astype(f32)


class Gather:
    def __init__(self, piece, groups):
        bits = bits_of(())
        self.groups = [tuple(b for b in group if b in bits) for group in groups]
        self.groups += [(b,) for b in bits if not any(b in group for group in self.groups)]
        self.done = []
        self.piece = piece
        self.value = piece

    def step(self):
        group = self.groups.pop(0)
        by_mask = {0: self.value}
        for bit in group:
            for mask in sub_masks(group, bit):
                by_mask[bit + mask] = exchange(self.value, bit + mask)
        for bit in group:
            mine = (lax.axis_index(BOTH) // bit) % 2 == 1
            self.done = sorted(self.done + [bit], reverse=True)
            axis = self.done.index(bit)
            merged = {}
            for mask, part in by_mask.items():
                if not mask & bit:
                    other = by_mask[mask + bit]
                    merged[mask] = jnp.stack(
                        [jnp.where(mine, other, part), jnp.where(mine, part, other)], axis=axis
                    )
            by_mask = merged
        (self.value,) = by_mask.values()

    def result(self):
        return self.value.reshape((-1,) + self.piece.shape)


def sub_masks(group, bit):
    masks = [0]
    for other in group[: group.index(bit)]:
        masks = masks + [mask + other for mask in masks]
    return masks


def from_behind(value, steps):
    count = lax.axis_size("rows")
    first, last = (max(0, -steps), min(count, count - steps))
    return lax.ppermute(value, "rows", [(source, source + steps) for source in range(first, last)])


def spline(values):
    magnitude = jnp.abs(values)
    outer = 1.5 - magnitude
    return jnp.where(
        magnitude < 0.5,
        0.75 - values * values,
        jnp.where(magnitude < 1.5, 0.5 * outer * outer, 0.0),
    )


def spline_slope(values):
    magnitude = jnp.abs(values)
    outer = 1.5 - magnitude
    return jnp.where(
        magnitude < 0.5,
        -2.0 * values,
        jnp.where(magnitude < 1.5, jnp.where(values > 0, -outer, outer), 0.0),
    )


def fill_factors(pos_ref, row_ref, col_weight, row_weight, col_slope=None, row_slope=None):
    cell_cols = lax.broadcasted_iota(jnp.int32, (2 * COLS, LANES), 0)
    cell_cols = jnp.where(cell_cols >= COLS, cell_cols - COLS, cell_cols).astype(f32)
    col_gap = pos_ref[0, 1:2, :] - cell_cols
    row_gap = pos_ref[0, 0:1, :] - row_ref[...]
    col_weight[...] = spline(col_gap)
    row_weight[...] = spline(row_gap)
    if col_slope is not None:
        col_slope[...] = spline_slope(col_gap)
        row_slope[...] = spline_slope(row_gap)


def fill_sampler(col_weight, row_weight, sampler):
    low = lax.broadcasted_iota(jnp.int32, (8, 128), 0) < 4

    def body(tile, carry):
        lanes = pl.ds(pl.multiple_of(tile * 128, 128), 128)
        for block in range(6):
            for chunk in range(11):
                halves = []
                for group in (2 * chunk, 2 * chunk + 1):
                    first, last = (8 * group) // COLS, (8 * group + 7) // COLS
                    weight = row_weight[4 * block + first : 4 * block + first + 1, lanes]
                    if first != last:
                        weight = jnp.where(
                            low, weight, row_weight[4 * block + last : 4 * block + last + 1, lanes]
                        )
                    local = group % 11
                    halves.append(col_weight[8 * local : 8 * local + 8, lanes] * weight)
                start = block * STRIP + 16 * chunk
                sampler[start : start + 16, lanes] = jnp.concatenate(halves, axis=0).astype(bf16)
        return carry

    lax.fori_loop(0, LANES // 128, body, 0)


def fill_window(pieces, window):
    for index, piece in enumerate(pieces[:5]):
        window[index * STRIP : (index + 1) * STRIP, :] = piece[0]
    window[5 * STRIP : 6 * STRIP, :] = jnp.concatenate([pieces[5][0], pieces[6][0]], axis=0)


def sample_kernel(pos_ref, row_ref, *refs):
    pieces, out_ref = refs[:7], refs[7]
    col_weight, row_weight, sampler, window = refs[8:]
    fill_factors(pos_ref, row_ref, col_weight, row_weight)
    fill_sampler(col_weight, row_weight, sampler)
    fill_window(pieces, window)
    result = dot_tn(window[...], sampler[...]).T.astype(bf16)
    width = window.shape[1]
    for tap in range(9):
        out_ref[0, :, tap * width : (tap + 1) * width] = result[tap * STRIP : (tap + 1) * STRIP]


def sample_back_kernel(pos_ref, row_ref, *refs):
    pieces, upstream_ref = refs[:7], refs[7]
    grads, pos_grad = refs[8:15], refs[15]
    (
        col_weight,
        row_weight,
        col_slope,
        row_slope,
        sampler,
        window,
        upstream,
        sampler_grad,
    ) = refs[16:]
    fill_factors(pos_ref, row_ref, col_weight, row_weight, col_slope, row_slope)
    fill_sampler(col_weight, row_weight, sampler)
    fill_window(pieces, window)
    width = window.shape[1]
    for tap in range(9):
        upstream[tap * STRIP : (tap + 1) * STRIP, :] = upstream_ref[
            0, :, tap * width : (tap + 1) * width
        ]
    upstream[QUERIES:LANES, :] = jnp.zeros((LANES - QUERIES, width), bf16)
    sampler_grad[...] = dot_nt(window[...], upstream[...])
    for index, grad in enumerate(grads[:5]):
        grad[0] = dot(sampler[index * STRIP : (index + 1) * STRIP, :], upstream[...]).astype(
            grad.dtype
        )
    last = dot(sampler[5 * STRIP :, :], upstream[...])
    grads[5][0] = last[: STRIP // 2].astype(bf16)
    grads[6][0] = last[STRIP // 2 :].astype(bf16)
    low = lax.broadcasted_iota(jnp.int32, (8, 128), 0) < 4

    def body(tile, carry):
        lanes = pl.ds(pl.multiple_of(tile * 128, 128), 128)
        zero = jnp.zeros((8, 128), f32)
        weights = [col_weight[8 * group : 8 * group + 8, lanes] for group in range(11)]
        middle_low = jnp.where(low, weights[5], 0.0)
        middle_high = jnp.where(low, 0.0, weights[5])
        row_total = zero
        col_totals = [zero] * 11
        for pair in range(12):
            first = row_weight[2 * pair : 2 * pair + 1, lanes]
            second = row_weight[2 * pair + 1 : 2 * pair + 2, lanes]
            mixed = jnp.where(low, first, second)
            first_sum = zero
            second_sum = zero
            for group in range(11):
                start = 88 * pair + 8 * group
                value = sampler_grad[start : start + 8, lanes]
                if group < 5:
                    first_sum = first_sum + value * weights[group]
                    col_totals[group] = col_totals[group] + value * first
                elif group > 5:
                    second_sum = second_sum + value * weights[group]
                    col_totals[group] = col_totals[group] + value * second
                else:
                    first_sum = first_sum + value * middle_low
                    second_sum = second_sum + value * middle_high
                    col_totals[group] = col_totals[group] + value * mixed
            row_total = (
                row_total
                + first_sum * row_slope[2 * pair : 2 * pair + 1, lanes]
                + second_sum * row_slope[2 * pair + 1 : 2 * pair + 2, lanes]
            )
        col_total = zero
        for group in range(11):
            col_total = col_total + col_totals[group] * col_slope[8 * group : 8 * group + 8, lanes]
        pos_grad[0, 0:1, lanes] = jnp.sum(row_total, axis=0, keepdims=True)
        pos_grad[0, 1:2, lanes] = jnp.sum(col_total, axis=0, keepdims=True)
        return carry

    lax.fori_loop(0, LANES // 128, body, 0)


def piece_specs(width):
    full = pl.BlockSpec((1, STRIP, width), lambda i: (i, 0, 0))
    half = pl.BlockSpec((1, STRIP // 2, width), lambda i: (i, 0, 0))
    return [full] * 5 + [half] * 2


def sampler_specs(width):
    return [
        pl.BlockSpec((1, 2, LANES), lambda i: (i, 0, 0)),
        pl.BlockSpec((len(ROW_ORDER), 1), lambda i: (0, 0)),
    ] + piece_specs(width)


def row_ids():
    return jnp.array(ROW_ORDER, f32)[:, None]


def sample(positions, pieces):
    images, _, width = pieces[0].shape
    return pl.pallas_call(
        sample_kernel,
        grid=(images,),
        in_specs=sampler_specs(width),
        out_specs=pl.BlockSpec((1, STRIP, 9 * width), lambda i: (i, 0, 0)),
        out_shape=jax.ShapeDtypeStruct((images, STRIP, 9 * width), bf16),
        scratch_shapes=[
            pltpu.VMEM((2 * COLS, LANES), f32),
            pltpu.VMEM((len(ROW_ORDER), LANES), f32),
            pltpu.VMEM((CELLS, LANES), bf16),
            pltpu.VMEM((CELLS, width), bf16),
        ],
        compiler_params=pltpu.CompilerParams(vmem_limit_bytes=60 * MIB),
        cost_estimate=SMALL,
        name="sample",
    )(positions, row_ids(), *pieces)


def sample_back(positions, pieces, upstream):
    images, _, width = pieces[0].shape
    full = (images, STRIP, width)
    half = (images, STRIP // 2, width)
    return pl.pallas_call(
        sample_back_kernel,
        grid=(images,),
        in_specs=sampler_specs(width)
        + [pl.BlockSpec((1, STRIP, 9 * width), lambda i: (i, 0, 0))],
        out_specs=piece_specs(width) + [pl.BlockSpec((1, 2, LANES), lambda i: (i, 0, 0))],
        out_shape=[jax.ShapeDtypeStruct(full, f32)]
        + [jax.ShapeDtypeStruct(full, bf16)] * 4
        + [jax.ShapeDtypeStruct(half, bf16)] * 2
        + [jax.ShapeDtypeStruct((images, 2, LANES), f32)],
        scratch_shapes=[
            pltpu.VMEM((2 * COLS, LANES), f32),
            pltpu.VMEM((len(ROW_ORDER), LANES), f32),
            pltpu.VMEM((2 * COLS, LANES), f32),
            pltpu.VMEM((len(ROW_ORDER), LANES), f32),
            pltpu.VMEM((CELLS, LANES), bf16),
            pltpu.VMEM((CELLS, width), bf16),
            pltpu.VMEM((LANES, width), bf16),
            pltpu.VMEM((CELLS, LANES), f32),
        ],
        compiler_params=pltpu.CompilerParams(vmem_limit_bytes=34 * MIB),
        cost_estimate=SMALL,
        name="sample_back",
    )(positions, row_ids(), *pieces, upstream)


def tap_slabs(above, own, below, padded, image):
    padded[8 : 8 + COLS, :] = above[image].astype(f32)
    padded[8 + COLS : 8 + COLS + STRIP, :] = own[image].astype(f32)
    padded[8 + COLS + STRIP : 8 + 2 * COLS + STRIP, :] = below[image].astype(f32)
    cols = lax.broadcasted_iota(jnp.int32, (STRIP, 1), 0) % COLS
    for tap in range(9):
        start = 8 + COLS * (tap // 3) + tap % 3 - 1
        slab = padded[start : start + STRIP, :]
        if tap % 3 == 0:
            slab = jnp.where(cols > 0, slab, 0.0)
        elif tap % 3 == 2:
            slab = jnp.where(cols < COLS - 1, slab, 0.0)
        yield tap, slab.astype(bf16)


def conv_kernel(above, own, below, weight, out_ref, slabs_ref, padded):
    width = own.shape[2]
    images = own.shape[0]
    for image in range(images):
        for tap, slab in tap_slabs(above, own, below, padded, image):
            slabs_ref[image, :, tap * width : (tap + 1) * width] = slab
    total = None
    for tap in range(9):
        lanes = slice(tap * width, (tap + 1) * width)
        part = dot(slabs_ref[:, :, lanes].reshape(images * STRIP, width), weight[lanes, :])
        total = part if total is None else total + part
    out_ref[...] = total.reshape(out_ref.shape)


def conv_back_kernel(above, own, below, weight, out_ref, padded, slabs):
    width = own.shape[2]
    images = own.shape[0]
    for image in range(images):
        for tap, slab in tap_slabs(above, own, below, padded, image):
            slabs[8 - tap, image * STRIP : (image + 1) * STRIP, :] = slab
    total = None
    for tap in range(9):
        part = dot_nt(slabs[tap], weight[tap * width : (tap + 1) * width, :])
        total = part if total is None else total + part
    out_ref[...] = total.reshape(out_ref.shape)


def conv_specs(images, width):
    rim = pl.BlockSpec((images, COLS, width), lambda i: (i, 0, 0))
    own = pl.BlockSpec((images, STRIP, width), lambda i: (i, 0, 0))
    return [rim, own, rim, pl.BlockSpec((9 * width, width), lambda i: (0, 0))]


def conv(above, own, below, weight):
    images, _, width = own.shape
    step = images // MB
    return pl.pallas_call(
        conv_kernel,
        grid=(MB,),
        in_specs=conv_specs(step, width),
        out_specs=[
            pl.BlockSpec((step, STRIP, width), lambda i: (i, 0, 0)),
            pl.BlockSpec((step, STRIP, 9 * width), lambda i: (i, 0, 0)),
        ],
        out_shape=[
            jax.ShapeDtypeStruct((images, STRIP, width), f32),
            jax.ShapeDtypeStruct((images, STRIP, 9 * width), bf16),
        ],
        scratch_shapes=[pltpu.VMEM((16 + 2 * COLS + STRIP, width), f32)],
        compiler_params=pltpu.CompilerParams(vmem_limit_bytes=24 * MIB),
        cost_estimate=SMALL,
        name="conv",
    )(above, own, below, weight)


def conv_back(above, own, below, weight):
    images, _, width = own.shape
    step = images // MB
    return pl.pallas_call(
        conv_back_kernel,
        grid=(MB,),
        in_specs=conv_specs(step, width),
        out_specs=pl.BlockSpec((step, STRIP, width), lambda i: (i, 0, 0)),
        out_shape=jax.ShapeDtypeStruct((images, STRIP, width), f32),
        scratch_shapes=[
            pltpu.VMEM((16 + 2 * COLS + STRIP, width), f32),
            pltpu.VMEM((9, step * STRIP, width), bf16),
        ],
        compiler_params=pltpu.CompilerParams(vmem_limit_bytes=24 * MIB),
        cost_estimate=SMALL,
        name="conv_back",
    )(above, own, below, weight)


TAP = 32


def offset_spans(device, rows, wide):
    spans = []
    start = device * rows
    while start < (device + 1) * rows:
        tap, column = divmod(start, wide)
        size = min((device + 1) * rows - start, wide - column)
        spans.append((tap, column, start - device * rows, size))
        start += size
    return spans


def offset_stack(strip, extra, width):
    rows = strip.shape[-1]
    lead = [(0, 0)] * (strip.ndim - 2)
    strip = jnp.pad(strip, lead + [(0, TAP - 18), (0, 0)])
    full = rows // width * width
    blocks = [strip[..., start : start + width] for start in range(0, full, width)]
    rest = strip[..., full:]
    rest = jnp.concatenate([rest[..., :16, :], rest[..., 16:, :]], axis=-1)
    pad = width - rest.shape[-1] - extra.shape[-1]
    assert pad >= 0
    blocks.append(jnp.pad(jnp.concatenate([rest, extra], axis=-1), lead + [(0, 0), (0, pad)]))
    return jnp.concatenate(blocks, axis=-2)


def spread_rows(values, images, take):
    parts = []
    for image in range(images):
        parts += take(image)
    return jnp.concatenate(parts, axis=1)


def own_lanes(values, image, start):
    first = image * STRIP + start
    return values[:, first : first + STRIP // 2]


def rim_lanes(values, image):
    return values[:, image * STRIP // 2 : (image + 1) * STRIP // 2]


def down_two(own, above, images):
    return spread_rows(own, images, lambda i: [rim_lanes(above, i), own_lanes(own, i, 0)])


def up_two(own, below, images):
    return spread_rows(own, images, lambda i: [own_lanes(own, i, STRIP // 2), rim_lanes(below, i)])


def beside(values, steps):
    if steps == 0:
        return values
    rows, cells = values.shape
    column = lax.broadcasted_iota(jnp.int32, (1, cells), 1) % COLS
    empty = jnp.zeros((rows, abs(steps)), values.dtype)
    if steps > 0:
        moved = jnp.concatenate([values[:, steps:], empty], axis=1)
    else:
        moved = jnp.concatenate([empty, values[:, :steps]], axis=1)
    return jnp.where((column + steps >= 0) & (column + steps < COLS), moved, 0.0)


def offset_conv_kernel(rows, small_ref, input_ref, taps_ref, partial_ref, last_ref, first_ref):
    count, _, width = small_ref.shape
    wide = input_ref.shape[1]
    images = input_ref.shape[0] // STRIP
    full = rows // width
    rest = rows - full * width
    for device in range(count):
        blocks = [small_ref[device, TAP * i : TAP * (i + 1), :] for i in range(full)]
        if rest:
            block = small_ref[device, TAP * full : TAP * full + 16, :]
            blocks.append(
                jnp.concatenate([block[:, :rest], block[:, rest : 2 * rest]], axis=0)
            )
        strip = jnp.concatenate(blocks, axis=1)
        for tap, column, local, size in offset_spans(device, rows, wide):
            taps_ref[TAP * tap : TAP * (tap + 1), column : column + size] = strip[
                :, local : local + size
            ]
    partial = dot_nt(taps_ref[...], input_ref[...])
    partial_ref[...] = partial
    half = STRIP // 2
    for image in range(images):
        lanes = slice(image * half, (image + 1) * half)
        last_ref[:, lanes] = own_lanes(partial[: 3 * TAP], image, half)
        first_ref[:, lanes] = own_lanes(partial[6 * TAP :], image, 0)


def offset_conv(small_all, rows, inputs):
    pixels, wide = inputs.shape
    rim = (3 * TAP, pixels // 2)
    return pl.pallas_call(
        partial(offset_conv_kernel, rows),
        out_shape=[
            jax.ShapeDtypeStruct((9 * TAP, wide), bf16),
            jax.ShapeDtypeStruct((9 * TAP, pixels), f32),
            jax.ShapeDtypeStruct(rim, f32),
            jax.ShapeDtypeStruct(rim, f32),
        ],
        compiler_params=pltpu.CompilerParams(vmem_limit_bytes=24 * MIB),
        name="offset_conv",
    )(small_all, inputs)


def positions_kernel(partial_ref, above_ref, below_ref, squashed_ref, positions_ref):
    images = positions_ref.shape[0]
    rows = [
        down_two(partial_ref[: 3 * TAP, :], above_ref[...], images),
        partial_ref[3 * TAP : 6 * TAP, :],
        up_two(partial_ref[6 * TAP :, :], below_ref[...], images),
    ]
    offsets = None
    for row in rows:
        for col_tap in range(3):
            part = beside(row[TAP * col_tap : TAP * (col_tap + 1)], 2 * (col_tap - 1))
            offsets = part if offsets is None else offsets + part
    squashed = jnp.tanh(offsets / CLIP)
    squashed_ref[...] = squashed
    clipped = CLIP * squashed
    cells = images * STRIP
    lane = lax.broadcasted_iota(jnp.int32, (9, cells), 1) % STRIP
    tap = lax.broadcasted_iota(jnp.int32, (9, cells), 0)
    row_position = clipped[:9] + (tap // 3 - 1 + HALO + lane // COLS).astype(f32)
    col_position = clipped[9:18] + (tap % 3 - 1 + lane % COLS).astype(f32)
    positions_ref[:, :, QUERIES:] = jnp.full((images, 2, LANES - QUERIES), -1000.0, f32)
    for image in range(images):
        lanes = slice(image * STRIP, (image + 1) * STRIP)
        for t in range(9):
            place = slice(t * STRIP, (t + 1) * STRIP)
            positions_ref[image, 0:1, place] = row_position[t : t + 1, lanes]
            positions_ref[image, 1:2, place] = col_position[t : t + 1, lanes]


def sample_positions(partial_offsets, above, below):
    cells = partial_offsets.shape[1]
    return pl.pallas_call(
        positions_kernel,
        out_shape=[
            jax.ShapeDtypeStruct((TAP, cells), f32),
            jax.ShapeDtypeStruct((cells // STRIP, 2, LANES), f32),
        ],
        name="sample_positions",
    )(partial_offsets, above, below)


def offset_slope_kernel(position_grad_ref, squashed_ref, back_ref, last_ref, first_ref, flat):
    images = position_grad_ref.shape[0]
    flat[...] = jnp.zeros_like(flat)
    for image in range(images):
        lanes = slice(image * STRIP, (image + 1) * STRIP)
        for t in range(9):
            place = slice(t * STRIP, (t + 1) * STRIP)
            flat[t : t + 1, lanes] = position_grad_ref[image, 0:1, place]
            flat[9 + t : 10 + t, lanes] = position_grad_ref[image, 1:2, place]
    squashed = squashed_ref[...]
    back = (flat[...] * (1.0 - squashed * squashed)).astype(bf16)
    back_ref[...] = back
    half = STRIP // 2
    wider = back.astype(f32)
    for image in range(images):
        lanes = slice(image * half, (image + 1) * half)
        last_ref[:, lanes] = own_lanes(wider, image, half).astype(bf16)
        first_ref[:, lanes] = own_lanes(wider, image, 0).astype(bf16)


def offset_slope(position_grad, squashed):
    cells = squashed.shape[1]
    rim = jax.ShapeDtypeStruct((TAP, cells // 2), bf16)
    return pl.pallas_call(
        offset_slope_kernel,
        out_shape=[jax.ShapeDtypeStruct((TAP, cells), bf16), rim, rim],
        scratch_shapes=[pltpu.VMEM((TAP, cells), f32)],
        name="offset_slope",
    )(position_grad, squashed)


def offset_back_kernel(rows, back_ref, above_ref, below_ref, input_ref, stacked_ref, chunks_ref):
    count, _, width = chunks_ref.shape
    wide = input_ref.shape[1]
    images = input_ref.shape[0] // STRIP
    own = back_ref[...].astype(f32)
    by_row = [
        up_two(own, below_ref[...].astype(f32), images),
        own,
        down_two(own, above_ref[...].astype(f32), images),
    ]
    for tap in range(9):
        moved = beside(by_row[tap // 3], -2 * (tap % 3 - 1))
        stacked_ref[TAP * tap : TAP * (tap + 1), :] = moved.astype(bf16)
    grad = dot(stacked_ref[...], input_ref[...])
    full = rows // width
    rest = rows - full * width
    chunks_ref[...] = jnp.zeros(chunks_ref.shape, bf16)
    for device in range(count):
        strip = jnp.concatenate(
            [
                grad[TAP * tap : TAP * (tap + 1), column : column + size]
                for tap, column, _, size in offset_spans(device, rows, wide)
            ],
            axis=1,
        ).astype(bf16)
        for i in range(full):
            chunks_ref[device, TAP * i : TAP * (i + 1), :] = strip[:, width * i : width * (i + 1)]
        if rest:
            tail = strip[:, width * full :]
            chunks_ref[device, TAP * full :, : 2 * rest] = jnp.concatenate(
                [tail[:16], tail[16:]], axis=1
            )


def offset_back(back, above, below, inputs, count, rows, width):
    pixels, wide = inputs.shape
    stack_rows = rows // width * TAP + (16 if rows % width else 0)
    return pl.pallas_call(
        partial(offset_back_kernel, rows),
        out_shape=[
            jax.ShapeDtypeStruct((9 * TAP, pixels), bf16),
            jax.ShapeDtypeStruct((count, stack_rows, width), bf16),
        ],
        compiler_params=pltpu.CompilerParams(vmem_limit_bytes=24 * MIB),
        name="offset_back",
    )(back, above, below, inputs)


def offset_unstack(shard, rows):
    width = shard.shape[1]
    full = rows // width
    rest = rows - full * width
    blocks = [shard[TAP * i : TAP * i + 18] for i in range(full)]
    if rest:
        tail = shard[TAP * full :]
        blocks.append(jnp.concatenate([tail[:, :rest], tail[:2, rest : 2 * rest]], axis=0))
    return jnp.concatenate(blocks, axis=1).T


def silu_slope(values):
    logistic = jax.nn.sigmoid(values)
    return logistic * (1.0 + values * (1.0 - logistic))


def box_weights(box_rows, box_cols, box_count, valid_mask, strip_rows, span_cols):
    row_ids_ = lax.axis_index("rows") * strip_rows + jnp.arange(strip_rows)
    col_ids = jnp.arange(span_cols)
    row_low = jnp.minimum(box_rows[..., 0], box_rows[..., 1])
    row_high = jnp.maximum(box_rows[..., 0], box_rows[..., 1])
    col_low = jnp.minimum(box_cols[..., 0], box_cols[..., 1])
    col_high = jnp.maximum(box_cols[..., 0], box_cols[..., 1])
    inside_rows = ((row_ids_ >= row_low[..., None]) & (row_ids_ <= row_high[..., None])).astype(f32)
    inside_cols = ((col_ids >= col_low[..., None]) & (col_ids <= col_high[..., None])).astype(f32)
    live_boxes = (jnp.arange(box_rows.shape[1])[None, :] < box_count[:, None]).astype(f32)
    covered = jnp.einsum("ib,ibh,ibw->ihw", live_boxes, inside_rows, inside_cols, precision=exact)
    return valid_mask.astype(f32) * (0.5 + covered / box_count.astype(f32)[:, None, None])


def per_batch(values):
    return values.reshape(MB, values.shape[0] // MB, values.shape[1])


def batch_totals(first, second):
    totals = all_sum(jnp.concatenate([jnp.sum(first, axis=1), jnp.sum(second, axis=1)], axis=0))
    return totals[:MB], totals[MB:]


class Norm:
    def __init__(self, values, gain, bias):
        values = per_batch(values)
        self.count = values.shape[1] * device_count()
        sums, squares = batch_totals(values, values * values)
        self.values = values
        self.center = (sums / self.count)[:, None, :]
        self.spread = lax.rsqrt(squares[:, None, :] / self.count - self.center * self.center + epsilon)
        self.gain = gain.astype(f32)
        self.bias = bias.astype(f32)

    def normed(self):
        return (self.values - self.center) * self.spread

    def forward(self):
        return self.normed() * self.gain + self.bias

    def backward(self, upstream):
        normed = self.normed()
        bias_sums, gain_sums = batch_totals(upstream, upstream * normed)
        self.gain_grad = jnp.sum(gain_sums, axis=0)
        self.bias_grad = jnp.sum(bias_sums, axis=0)
        result = (self.spread * self.gain) * (
            upstream
            - (bias_sums / self.count)[:, None, :]
            - normed * (gain_sums / self.count)[:, None, :]
        )
        return result.astype(bf16).reshape(-1, result.shape[-1])


def stacked_columns(weight, width):
    return jnp.concatenate(jnp.split(weight, weight.shape[1] // width, axis=1), axis=0)


def unstacked_columns(blocks, columns):
    width = blocks.shape[2]
    parts = jnp.split(blocks, columns // width, axis=1)
    return jnp.concatenate([part.reshape(-1, width) for part in parts], axis=1)


def gather(pieces):
    whole = lax.all_gather(jnp.concatenate(pieces, axis=0), BOTH, axis=0)
    results = []
    start = 0
    for piece in pieces:
        results.append(whole[:, start : start + piece.shape[0]])
        start += piece.shape[0]
    return results


def to_width(flat, width):
    rows = -(-flat.shape[-1] // width)
    pad = rows * width - flat.shape[-1]
    return jnp.pad(flat, [(0, 0)] * (flat.ndim - 1) + [(0, pad)]).reshape(
        flat.shape[:-1] + (rows, width)
    )


def widths(values, width):
    pieces = []
    for start in range(0, values.shape[-1], width):
        piece = values[..., start : start + width]
        pad = width - piece.shape[-1]
        pieces.append(jnp.pad(piece, [(0, 0)] * (values.ndim - 1) + [(0, pad)]))
    return pieces


def shifted(values, steps, columns):
    if steps == 0:
        return values
    cells = values.shape[-1]
    column = jnp.arange(cells) % columns
    pad = [(0, 0)] * (values.ndim - 1)
    if steps > 0:
        moved = jnp.pad(values[..., steps:], pad + [(0, steps)])
    else:
        moved = jnp.pad(values[..., :steps], pad + [(-steps, 0)])
    return jnp.where((column + steps >= 0) & (column + steps < columns), moved, 0)


def on_device(
    images_in,
    out_grad,
    box_rows,
    box_cols,
    box_count,
    valid_mask,
    reduce_one,
    offset_one,
    deform_one,
    expand_one,
    mid_gain_one,
    mid_bias_one,
    wide_gain_one,
    wide_bias_one,
    reduce_two,
    spatial_two,
    expand_two,
    mid_gain_two,
    mid_bias_two,
    wide_gain_two,
    wide_bias_two,
):
    images, strip_rows, span_cols, wide = images_in.shape
    mid = reduce_one.shape[1]
    assert strip_rows == STRIP_ROWS and span_cols == COLS
    count = device_count()
    pixels = images * STRIP

    mid_part = mid // count
    wide_part = wide // count
    extent = max(mid_part, wide_part)
    mid_rows = jnp.concatenate([mid_gain_one, mid_bias_one, mid_gain_two, mid_bias_two], axis=0)
    wide_rows = jnp.concatenate(
        [v[None] for v in (wide_gain_one, wide_bias_one, wide_gain_two, wide_bias_two)], axis=0
    )
    vectors = jnp.pad(mid_rows, ((0, 8), (0, extent - mid_part))) + jnp.pad(
        wide_rows, ((8, 4), (0, extent - wide_part))
    )
    offset_rows = offset_one.shape[0]
    small = offset_stack(offset_one.T, vectors, mid)
    flat_inputs = images_in.reshape(pixels, wide)
    flat_out_grad = out_grad.reshape(pixels, wide)
    reduce_gather = Gather(reduce_one, ((8, 16), (4,), (2,), (1,)))
    small_gather = Gather(small, ((8, 16), (2,), (4,), (1,)))
    while reduce_gather.groups:
        reduce_gather.step()
        small_gather.step()
        if len(reduce_gather.groups) == 1:
            reduce_gather.value, small_gather.value, flat_inputs = meet(
                reduce_gather.value, small_gather.value, flat_inputs
            )
        else:
            reduce_gather.value, small_gather.value = meet(reduce_gather.value, small_gather.value)
    reduce_all, small_all = reduce_gather.result(), small_gather.result()
    deform_all, expand_all = gather([deform_one, stacked_columns(expand_one, mid)])
    weight_reduce_one = reduce_all.reshape(wide, mid)
    weight_deform_one = deform_all.reshape(9 * mid, mid)
    weight_expand_one = unstacked_columns(expand_all, wide)
    vector_start = 2 * (offset_rows % mid)
    vector_all = small_all[:, small.shape[0] - 16 :, vector_start : vector_start + extent]
    mid_vectors = vector_all[:, :8, :mid_part].transpose(1, 0, 2).reshape(8, mid)
    wide_vectors = vector_all[:, 8:12, :wide_part].transpose(1, 0, 2).reshape(4, wide)
    gain_mid_one, bias_mid_one = mid_vectors[0:2], mid_vectors[2:4]
    gain_mid_two, bias_mid_two = mid_vectors[4:6], mid_vectors[6:8]

    def maps(values):
        return values.reshape(images, STRIP, values.shape[-1])

    grad_weight = box_weights(box_rows, box_cols, box_count, valid_mask, strip_rows, span_cols)

    first_conv = dot(flat_inputs, weight_reduce_one)
    first_conv, small_all = meet(first_conv, small_all)
    norm_a1 = Norm(first_conv, gain_mid_one[0], bias_mid_one[0])
    tap_weights, partial_offsets, last_rim, first_rim = offset_conv(
        small_all, offset_rows, flat_inputs
    )
    hidden = jax.nn.silu(norm_a1.forward()).astype(bf16).reshape(images, STRIP, mid)
    hidden, rim_above, rim_below = meet(hidden, from_behind(last_rim, 1), from_behind(first_rim, -1))
    half = STRIP // 2
    squashed, positions = sample_positions(partial_offsets, rim_above, rim_below)
    pieces = [
        hidden,
        from_behind(hidden, -1),
        from_behind(hidden, 1),
        from_behind(hidden, -2),
        from_behind(hidden, 2),
        from_behind(hidden[:, :half], -3),
        from_behind(hidden[:, half:], 3),
    ]
    positions, flat_out_grad, reduce_two, spatial_two, expand_two, *pieces = meet(
        positions, flat_out_grad, reduce_two, spatial_two, expand_two, *pieces
    )
    reduce_two_all, spatial_all, expand_two_all = gather(
        [reduce_two, spatial_two, stacked_columns(expand_two, mid)]
    )
    weight_reduce_two = reduce_two_all.reshape(wide, mid)
    weight_spatial_two = spatial_all.reshape(9 * mid, mid)
    weight_expand_two = unstacked_columns(expand_two_all, wide)
    sampled = sample(positions, pieces).reshape(pixels, 9 * mid)
    norm_a2 = Norm(dot(sampled, weight_deform_one), gain_mid_one[1], bias_mid_one[1])
    hidden_two = jax.nn.silu(norm_a2.forward()).astype(bf16).reshape(pixels, mid)
    norm_a3 = Norm(dot(hidden_two, weight_expand_one), wide_vectors[0], wide_vectors[1])
    joined_one = norm_a3.forward() + per_batch(flat_inputs).astype(f32)
    middle = jax.nn.silu(joined_one).astype(bf16).reshape(pixels, wide)

    norm_b1 = Norm(dot(middle, weight_reduce_two), gain_mid_two[0], bias_mid_two[0])
    inner_one = maps(jax.nn.silu(norm_b1.forward()).astype(bf16))
    fifth_conv, inner_slabs = conv(
        from_behind(inner_one[:, STRIP - COLS :], 1),
        inner_one,
        from_behind(inner_one[:, :COLS], -1),
        weight_spatial_two,
    )
    norm_b2 = Norm(fifth_conv.reshape(pixels, mid), gain_mid_two[1], bias_mid_two[1])
    inner_two = jax.nn.silu(norm_b2.forward()).astype(bf16).reshape(pixels, mid)
    norm_b3 = Norm(dot(inner_two, weight_expand_two), wide_vectors[2], wide_vectors[3])
    joined_two = norm_b3.forward() + per_batch(middle).astype(f32)
    block_out = jax.nn.silu(joined_two).astype(bf16).reshape(images_in.shape)

    upstream = per_batch(flat_out_grad).astype(f32) * grad_weight.reshape(MB, pixels // MB, 1)
    masked_six = upstream * silu_slope(joined_two)
    back_sixth = norm_b3.backward(masked_six)
    grad_expand_two = dot_tn(inner_two, back_sixth).astype(bf16)
    back_fifth = norm_b2.backward(
        per_batch(dot_nt(back_sixth, weight_expand_two)) * silu_slope(norm_b2.forward())
    )
    grad_spatial_two = dot_tn(inner_slabs.reshape(pixels, 9 * mid), back_fifth).astype(bf16)
    def chunked(grad):
        return grad.reshape(count, -1, mid)

    def chunked_columns(grad):
        return [part.reshape(count, -1, mid) for part in jnp.split(grad, grad.shape[1] // mid, axis=1)]

    def unchunked_columns(shard):
        return jnp.concatenate(jnp.split(shard, wide // mid, axis=0), axis=1)

    def split_rows(shard, sizes):
        results = []
        start = 0
        for size in sizes:
            results.append(shard[start : start + size])
            start += size
        return results

    column_rows = expand_two.shape[0] * wide // mid
    two_sum = Scatter([chunked(grad_spatial_two)] + chunked_columns(grad_expand_two), (1, 16, 8, 4, 2))

    def beside_steps(value, *scatters):
        for scatter in scatters:
            scatter.step()
        value, *sums = meet(value, *[scatter.value for scatter in scatters])
        for scatter, total in zip(scatters, sums):
            scatter.value = total
        return value

    back_fifth = beside_steps(back_fifth, two_sum)
    two_shard = scatter_chips(two_sum)
    back_maps = maps(back_fifth)
    back_inner = conv_back(
        from_behind(back_maps[:, STRIP - COLS :], 1),
        back_maps,
        from_behind(back_maps[:, :COLS], -1),
        weight_spatial_two,
    ).reshape(pixels, mid)
    back_fourth = norm_b1.backward(per_batch(back_inner) * silu_slope(norm_b1.forward()))
    grad_reduce_two = dot_tn(middle, back_fourth).astype(bf16)

    back_middle = masked_six + per_batch(dot_nt(back_fourth, weight_reduce_two))
    masked_three = back_middle * silu_slope(joined_one)
    back_third = norm_a3.backward(masked_three)
    grad_expand_one = dot_tn(hidden_two, back_third).astype(bf16)
    back_second = norm_a2.backward(
        per_batch(dot_nt(back_third, weight_expand_one)) * silu_slope(norm_a2.forward())
    )
    grad_deform_one = dot_tn(sampled, back_second).astype(bf16)
    one_left = Scatter([chunked(grad_deform_one)], (1, 2, 4, 8, 16))
    one_right = Scatter(
        chunked_columns(grad_expand_one) + [chunked(grad_reduce_two)], (1, 4, 2, 8, 16)
    )
    back_second, one_left.value, one_right.value = meet(
        back_second, one_left.value, one_right.value
    )
    back_sampled = dot_nt(back_second, weight_deform_one).astype(bf16).reshape(images, STRIP, -1)
    back_sampled = beside_steps(back_sampled, one_left, one_right)

    own, *others, position_grad = sample_back(positions, pieces, back_sampled)
    half_sum = jnp.concatenate([from_behind(others[4], 3), from_behind(others[5], -3)], axis=1)
    own = (
        own
        + from_behind(others[0], 1).astype(f32)
        + from_behind(others[1], -1).astype(f32)
        + from_behind(others[2], 2).astype(f32)
        + from_behind(others[3], -2).astype(f32)
        + half_sum.astype(f32)
    )
    own, two_shard = meet(own, two_shard)
    back_offsets, last_rim, first_rim = offset_slope(position_grad, squashed)
    stacked, offset_chunks = offset_back(
        back_offsets,
        from_behind(last_rim, 1),
        from_behind(first_rim, -1),
        flat_inputs,
        count,
        offset_rows,
        mid,
    )
    offset_to_images = dot_tn(stacked, tap_weights)

    back_first = norm_a1.backward(
        per_batch(own.reshape(pixels, mid)) * silu_slope(norm_a1.forward())
    )
    offset_sum = Scatter([offset_chunks], (1, 4, 2, 8, 16))
    back_first = beside_steps(back_first, one_left, one_right, offset_sum)
    grad_reduce_one = dot_tn(flat_inputs, back_first).astype(bf16)
    half_rows = reduce_one.shape[0] // 2
    last_chunks = chunked(grad_reduce_one)
    last_left = Scatter([last_chunks[:, :half_rows]], (1, 2, 4, 8, 16))
    last_right = Scatter([last_chunks[:, half_rows:]], (1, 4, 2, 8, 16))
    back_first = beside_steps(back_first, last_left, last_right)
    grad_images = (
        masked_three.reshape(pixels, wide)
        + dot_nt(back_first, weight_reduce_one)
        + offset_to_images
    )
    grad_images = beside_steps(grad_images, last_left, last_right).reshape(images_in.shape)
    reduce_shard = jnp.concatenate([last_left.finish(), last_right.finish()], axis=0)
    offset_shard = offset_unstack(offset_sum.finish(), offset_rows)
    deform_shard = one_left.finish()
    expand_shard, reduce_two_shard = split_rows(
        one_right.finish(), [column_rows, reduce_two.shape[0]]
    )
    spatial_shard, expand_two_shard = split_rows(two_shard, [spatial_two.shape[0], column_rows])

    me = lax.axis_index(BOTH)
    mid_grads = jnp.stack(
        [
            norm_a1.gain_grad,
            norm_a2.gain_grad,
            norm_a1.bias_grad,
            norm_a2.bias_grad,
            norm_b1.gain_grad,
            norm_b2.gain_grad,
            norm_b1.bias_grad,
            norm_b2.bias_grad,
        ]
    )
    mid_grads = lax.dynamic_slice_in_dim(mid_grads, me * mid_part, mid_part, 1)
    wide_grads = jnp.stack(
        [norm_a3.gain_grad, norm_a3.bias_grad, norm_b3.gain_grad, norm_b3.bias_grad]
    )
    wide_grads = lax.dynamic_slice_in_dim(wide_grads, me * wide_part, wide_part, 1)
    return (
        block_out,
        grad_images,
        reduce_shard,
        offset_shard,
        deform_shard,
        unchunked_columns(expand_shard),
        mid_grads[0:2],
        mid_grads[2:4],
        wide_grads[0],
        wide_grads[1],
        reduce_two_shard,
        spatial_shard,
        unchunked_columns(expand_two_shard),
        mid_grads[4:6],
        mid_grads[6:8],
        wide_grads[2],
        wide_grads[3],
    )


def solution(mesh):
    whole = P(BOTH, None)
    part = P(None, BOTH)
    line = P(BOTH)
    maps = P("img", "rows", None, None)
    return jax.shard_map(
        on_device,
        mesh=mesh,
        in_specs=(
            maps,
            maps,
            P("img", None, None),
            P("img", None, None),
            P("img"),
            P("img", "rows", None),
            whole,
            whole,
            whole,
            whole,
            part,
            part,
            line,
            line,
            whole,
            whole,
            whole,
            part,
            part,
            line,
            line,
        ),
        out_specs=(
            maps,
            maps,
            whole,
            whole,
            whole,
            whole,
            part,
            part,
            line,
            line,
            whole,
            whole,
            whole,
            part,
            part,
            line,
            line,
        ),
        check_vma=False,
    )
```
